32 devices in a mesh: row: 4 (over x, core), col: 8 (over z, y).
Axes of the slice: x: 2, y: 2, z: 4, core: 2. Of those that a mesh axis runs over, the one named last changes fastest.
Arguments:
- latents: bfloat16 [64, 64, 16], P('row', 'col'), may hold values from -6 to 6
- captions: bfloat16 [256, 4096], replicated, may hold values from -6 to 6
- item_heights: int32 [21], replicated, may hold values from 1 to 8, 64 in all
- item_bands: int32 [21], replicated, may hold values from 0 to 7
- embedding: bfloat16 [144, 1536], P(None, 'col'), may hold values from -0.5 to 0.5
- embed_bias: bfloat16 [1536], P('col'), may hold values from -2 to 2
- band_table: bfloat16 [8, 1536], P(None, 'col'), may hold values from -6 to 6
- adaptive: bfloat16 [1536, 6144], P('col'), may hold values from -0.15625 to 0.15625
- adaptive_bias: bfloat16 [6144], P('col'), may hold values from -2 to 2
- attention_gain: bfloat16 [1536], P('col'), may hold values from 0.5 to 1.5
- projection: bfloat16 [1536, 4608], P('col'), may hold values from -0.15625 to 0.15625
- query_gain: bfloat16 [1536], P('col'), may hold values from 0.5 to 1.5
- key_gain: bfloat16 [1536], P('col'), may hold values from 0.5 to 1.5
- cross_query: bfloat16 [1536, 1536], P('col'), may hold values from -0.15625 to 0.15625
- caption_weight: bfloat16 [4096, 3072], P('col'), may hold values from -0.09375 to 0.09375
- cross_gate: bfloat16 [1536], P('col'), may hold values from -1.5 to 1.5
- output_weight: bfloat16 [1536, 1536], P('col'), may hold values from -1.25 to 1.25
- feedforward_gain: bfloat16 [1536], P('col'), may hold values from 0.5 to 1.5
- gate_weight: bfloat16 [1536, 4096], P('col'), may hold values from -0.15625 to 0.15625
- up_weight: bfloat16 [1536, 4096], P('col'), may hold values from -0.15625 to 0.15625
- down_weight: bfloat16 [4096, 1536], P('col'), may hold values from -0.09375 to 0.09375
- unpatch_weight: bfloat16 [1536, 144], P('col'), may hold values from -0.15625 to 0.15625
- cotangent: bfloat16 [64, 64, 16], P('row', 'col'), may hold values from -6 to 6
Outputs:
- prediction: bfloat16 [64, 64, 16], P('row', 'col')
- latent_grad: bfloat16 [64, 64, 16], P('row', 'col')
- grad_embedding: float32 [144, 1536], P(None, ('row', 'col'))
- grad_embed_bias: float32 [1536], P(('row', 'col'))
- grad_band_table: float32 [8, 1536], P(None, ('row', 'col'))
- grad_adaptive: float32 [1536, 6144], P(('row', 'col'))
- grad_adaptive_bias: float32 [6144], P(('row', 'col'))
- grad_attention_gain: float32 [1536], P(('row', 'col'))
- grad_projection: float32 [1536, 4608], P(('row', 'col'))
- grad_query_gain: float32 [1536], P(('row', 'col'))
- grad_key_gain: float32 [1536], P(('row', 'col'))
- grad_cross_query: float32 [1536, 1536], P(('row', 'col'))
- grad_caption_weight: float32 [4096, 3072], P(('row', 'col'))
- grad_cross_gate: float32 [1536], P(('row', 'col'))
- grad_output_weight: float32 [1536, 1536], P(('row', 'col'))
- grad_feedforward_gain: float32 [1536], P(('row', 'col'))
- grad_gate_weight: float32 [1536, 4096], P(('row', 'col'))
- grad_up_weight: float32 [1536, 4096], P(('row', 'col'))
- grad_down_weight: float32 [4096, 1536], P(('row', 'col'))
- grad_unpatch_weight: float32 [1536, 144], P(('row', 'col'))
The draws below stay inside these ranges and needn't reach their ends.
Inputs may be any that keep to these rules, and one draw needn't show every extreme that they name: `item_heights`: item heights in grid rows, summing to 64; the tallest item has exactly 8 rows.
All inputs are finite; a program needn't handle non-finite values.
Results may differ from the reference program's by a relative error of at most 0.025.
Values may be sent and summed in bfloat16 or wider, within the bound.
No kernel may reach another device: no remote copies, remote signals or barrier semaphores. Data moves between devices by JAX's collectives and lax.ppermute only.
A program may use at most 704 MiB of HBM per device.

```python
import math
import jax
import jax.numpy as jnp
import numpy as np
from jax import lax

D = 1536
HEADS = 24
HD = 64
FF = 4096
CAP = 4096
TXT = 256
NBAND = 8
TH = 16
MOSTH = 8
RB = 4
GH = 64
GW = 64
NITEM = 21
N_ROW = 4


def touch_ends(drawn, rng, smallest, high):
    longest = drawn.shape.index(max(drawn.shape))
    spots = []
    for shift in (0, 1):
        where = [jax.random.randint(jax.random.fold_in(rng, axis), (), 0, length) for axis, length in enumerate(drawn.shape)]
        where[longest] = (where[longest] + shift) % drawn.shape[longest]
        spots.append(tuple(where))
    return drawn.at[spots[0]].set(smallest).at[spots[1]].set(high)


def block_scale(key, extent, split, low, top_value):
    gain = 1.0
    for position, shards_of in split:
        steps = jax.random.uniform(jax.random.fold_in(jax.random.fold_in(key, 6), position), (shards_of,), jnp.float32, low / len(split), top_value / len(split))
        gain = gain * jnp.repeat(jnp.exp(steps), extent[position] // shards_of).reshape((-1,) + (1,) * (len(extent) - 1 - position))
    return gain


def split_up(number_of, total, most, skew):
    loads = [(1 << 20) // math.isqrt(rank ** skew) + 1 for rank in range(2, number_of + 1)]
    spare, counts = total - most - (number_of - 1), [1] * (number_of - 1)
    while spare > 0:
        candidates = [i for i in range(number_of - 1) if counts[i] < most]
        whole, remaining = sum([loads[i] for i in candidates]), spare
        for i in candidates:
            extra = min(most - counts[i], max(1, remaining * loads[i] // whole), spare)
            counts[i] = counts[i] + extra
            spare = spare - extra
    return np.array([most] + counts)


def uneven(stream_key, count, total, limit, skew):
    if count == 2:
        one = jax.random.randint(stream_key, (), max(1, total - limit), min(limit, total - 1) + 1)
        return jnp.stack([one, total - one])
    sizes = jnp.asarray(split_up(count, total, limit, skew), jnp.int32)
    couples = (count - 1) // 2
    donor, sink = sizes[1:1 + 2 * couples:2], sizes[2:2 + 2 * couples:2]
    slack = jnp.minimum(donor - 1, limit - sink)
    passed = jax.random.randint(jax.random.fold_in(stream_key, 1), (couples,), 0, 1 << 20) % (slack + 1)
    sizes = sizes.at[1:1 + 2 * couples:2].set(donor - passed).at[2:2 + 2 * couples:2].set(sink + passed)
    return sizes[jax.random.permutation(jax.random.fold_in(stream_key, 2), count)]


def bell_draw(own_key, dims, width, reach, cuts=(), held_as=jnp.bfloat16):
    gain = block_scale(own_key, dims, cuts, -0.22, 0.18) if cuts else 1.0
    entries = jax.random.normal(own_key, dims, jnp.float32) * width * gain
    return jnp.minimum(jnp.maximum(entries, -reach), reach).astype(held_as)


def setup_inputs(seed: int = 0) -> dict:
    seeds = jax.random.split(jax.random.key(seed), 24)
    return {
        "latents": bell_draw(seeds[0], (GH, GW, 16), 1.0, 6.0, ((0, 4), (1, 8))),
        "captions": bell_draw(seeds[1], (TXT, CAP), 1.0, 6.0),
        "item_heights": uneven(seeds[2], NITEM, TH * N_ROW, MOSTH, 1).astype(jnp.int32),
        "item_bands": touch_ends(jax.random.randint(seeds[3], (NITEM,), 0, NBAND), jax.random.fold_in(seeds[3], 1), 0, NBAND - 1).astype(jnp.int32),
        "embedding": bell_draw(seeds[4], (144, D), 144 ** -0.5, 0.5, ((1, 8),)),
        "embed_bias": bell_draw(seeds[5], (D,), 0.3, 2.0, ((0, 8),)),
        "band_table": bell_draw(seeds[6], (NBAND, D), 1.0, 6.0, ((1, 8),)),
        "adaptive": bell_draw(seeds[7], (D, 4 * D), D ** -0.5, 0.15625, ((0, 8),)),
        "adaptive_bias": bell_draw(seeds[8], (4 * D,), 0.3, 2.0, ((0, 8),)),
        "attention_gain": jnp.clip(1.0 + 0.1 * jax.random.normal(seeds[9], (D,), jnp.float32), 0.5, 1.5).astype(jnp.bfloat16),
        "projection": bell_draw(seeds[10], (D, 3 * D), D ** -0.5, 0.15625, ((0, 8),)),
        "query_gain": jnp.clip(1.0 + 0.1 * jax.random.normal(seeds[11], (D,), jnp.float32), 0.5, 1.5).astype(jnp.bfloat16),
        "key_gain": jnp.clip(1.0 + 0.1 * jax.random.normal(seeds[12], (D,), jnp.float32), 0.5, 1.5).astype(jnp.bfloat16),
        "cross_query": bell_draw(seeds[13], (D, D), D ** -0.5, 0.15625, ((0, 8),)),
        "caption_weight": bell_draw(seeds[14], (CAP, 2 * D), CAP ** -0.5, 0.09375, ((0, 8),)),
        "cross_gate": jnp.clip(jax.random.uniform(seeds[15], (D,), jnp.float32, -1.5, 1.5) * block_scale(seeds[15], (D,), ((0, 8),), -0.4, 0.0), -1.5, 1.5).astype(jnp.bfloat16),
        "output_weight": bell_draw(seeds[16], (D, D), (D // 64) ** -0.5, 1.25, ((0, 8),)),
        "feedforward_gain": jnp.clip(1.0 + 0.1 * jax.random.normal(seeds[17], (D,), jnp.float32), 0.5, 1.5).astype(jnp.bfloat16),
        "gate_weight": bell_draw(seeds[18], (D, FF), D ** -0.5, 0.15625, ((0, 8),)),
        "up_weight": bell_draw(seeds[19], (D, FF), D ** -0.5, 0.15625, ((0, 8),)),
        "down_weight": bell_draw(seeds[20], (FF, D), FF ** -0.5, 0.09375, ((0, 8),)),
        "unpatch_weight": bell_draw(seeds[21], (D, 144), D ** -0.5, 0.15625, ((0, 8),)),
        "cotangent": bell_draw(seeds[22], (GH, GW, 16), 1.0, 6.0, ((0, 4), (1, 8))),
    }


EPS = 1e-06
THETA = 10000.0
NEG = -1e+30
HIGH = lax.Precision.HIGHEST
OFFSETS = ((-1, -1), (-1, 0), (-1, 1), (0, -1), (0, 0), (0, 1), (1, -1), (1, 0), (1, 1))

@jax.custom_vjp
def low(v):
    return lax.optimization_barrier(v.astype(jnp.bfloat16)).astype(jnp.float32)

@jax.custom_vjp
def low_back(v):
    return v

def low_keep(v):
    return (low(v), None)

def low_pass(kept, grad):
    return (grad,)

def back_keep(v):
    return (v, None)

def back_low(kept, grad):
    return (low(grad),)
low.defvjp(low_keep, low_pass)
low_back.defvjp(back_keep, back_low)

def matmul(left_mat, right_mat):
    return jnp.dot(left_mat, right_mat, precision=HIGH)

def norm_rows(values):
    return values * lax.rsqrt(lax.optimization_barrier(jnp.mean(values * values, axis=-1, keepdims=True)) + EPS)

def gather_cells(padded, row_count, col_count):
    return jnp.concatenate([padded[1 + row_off:1 + row_off + row_count, 1 + col_off:1 + col_off + col_count] for row_off, col_off in OFFSETS], axis=-1)

def spread_cells(padded, row_count, col_count, channels):
    summed = jnp.zeros((row_count, col_count, channels), jnp.float32)
    for offset_index, (row_off, col_off) in enumerate(OFFSETS):
        summed = summed + padded[1 - row_off:1 - row_off + row_count, 1 - col_off:1 - col_off + col_count, offset_index * channels:(offset_index + 1) * channels].astype(jnp.float32)
    return summed

def row_items(heights, band_ids, row_count):
    item_ends = jnp.cumsum(heights).astype(jnp.int32)
    row_ids = jnp.arange(row_count, dtype=jnp.int32)
    item_of_row = lax.optimization_barrier(jnp.sum((item_ends[None, :] <= row_ids[:, None]).astype(jnp.int32), axis=1)).astype(jnp.int32)
    picked = item_of_row[:, None] == jnp.arange(heights.shape[0], dtype=jnp.int32)[None, :]
    item_top = lax.optimization_barrier(jnp.sum(jnp.where(picked, (item_ends - heights)[None, :], 0), axis=1)).astype(jnp.int32)
    row_band = lax.optimization_barrier(jnp.sum(jnp.where(picked, band_ids[None, :], 0), axis=1)).astype(jnp.int32)
    band_onehot = (row_band[:, None] == jnp.arange(NBAND, dtype=jnp.int32)[None, :]).astype(jnp.float32)
    return (item_of_row, row_ids - item_top, band_onehot)

def rope_tables(row_place, col_place, head_dim):
    quarter = head_dim // 4
    frequency = THETA ** (-jnp.arange(quarter, dtype=jnp.float32) / quarter)
    angle_rows = row_place.astype(jnp.float32)[:, None] * frequency
    angle_cols = col_place.astype(jnp.float32)[:, None] * frequency
    return (jnp.cos(angle_rows), jnp.sin(angle_rows), jnp.cos(angle_cols), jnp.sin(angle_cols))

def rotate(values, tables):
    cos_rows, sin_rows, cos_cols, sin_cols = tables
    quarter = values.shape[-1] // 4
    first, second, third, fourth = (values[..., segment * quarter:(segment + 1) * quarter] for segment in range(4))
    cos_r = cos_rows[:, None, None, :]
    sin_r = sin_rows[:, None, None, :]
    cos_c = cos_cols[None, :, None, :]
    sin_c = sin_cols[None, :, None, :]
    return jnp.concatenate([first * cos_r - second * sin_r, first * sin_r + second * cos_r, third * cos_c - fourth * sin_c, third * sin_c + fourth * cos_c], axis=-1)

def head_norm(raw_heads, gain_vec, tables):
    shaped = gain_vec.reshape(raw_heads.shape[2], raw_heads.shape[3])
    return rotate(norm_rows(raw_heads) * shaped, tables)

def reference(latents, captions, item_heights, item_bands, embedding, embed_bias, band_table, adaptive, adaptive_bias, attention_gain, projection, query_gain, key_gain, cross_query, caption_weight, cross_gate, output_weight, feedforward_gain, gate_weight, up_weight, down_weight, unpatch_weight, cotangent):
    grid_rows, grid_cols = (latents.shape[0], latents.shape[1])
    item_of_row, row_place, band_onehot = row_items(item_heights, item_bands, grid_rows)
    tables = rope_tables(row_place, jnp.arange(grid_cols, dtype=jnp.int32), HD)
    captions_wide = captions.astype(jnp.float32)
    score_scale = 1.0 / math.sqrt(HD)
    block_count = grid_rows // RB
    window = RB + 2 * (MOSTH - 1)

    def forward(cells_in, embedding, embed_bias, band_table, adaptive, adaptive_bias, attention_gain, projection, query_gain, key_gain, cross_query, caption_weight, cross_gate, output_weight, feedforward_gain, gate_weight, up_weight, down_weight, unpatch_weight):
        padded = jnp.pad(cells_in, ((1, 1), (1, 1), (0, 0)))
        neighbours = low_back(gather_cells(padded, grid_rows, grid_cols))
        embedded = low_back(matmul(neighbours, embedding) + embed_bias)
        modulations = matmul(jax.nn.silu(band_table), adaptive) + adaptive_bias
        row_modulation = matmul(band_onehot, modulations)[:, None, :]
        first_scale = row_modulation[..., 0:D]
        first_gate = row_modulation[..., D:2 * D]
        second_scale = row_modulation[..., 2 * D:3 * D]
        second_gate = row_modulation[..., 3 * D:4 * D]
        normed = low(norm_rows(embedded) * attention_gain * (1.0 + first_scale))
        queries_raw = low_back(low(matmul(normed, projection[:, 0:D]))).reshape(grid_rows, grid_cols, HEADS, HD)
        keys_raw = low_back(low(matmul(normed, projection[:, D:2 * D]))).reshape(grid_rows, grid_cols, HEADS, HD)
        values = low_back(low(matmul(normed, projection[:, 2 * D:3 * D]))).reshape(grid_rows, grid_cols, HEADS, HD)
        cross_raw = low_back(low(matmul(normed, cross_query))).reshape(grid_rows, grid_cols, HEADS, HD)
        queries = low_back(low(head_norm(queries_raw, query_gain, tables)))
        keys = low_back(low(head_norm(keys_raw, key_gain, tables)))
        caption_keys = low(matmul(captions_wide, caption_weight[:, 0:D])).reshape(TXT, HEADS, HD)
        caption_values = low(matmul(captions_wide, caption_weight[:, D:2 * D])).reshape(TXT, HEADS, HD)

        def attend_block(block_index):
            first_row = block_index * RB
            key_row = jnp.clip(first_row - (MOSTH - 1), 0, grid_rows - window).astype(jnp.int32)
            block_queries = lax.dynamic_slice_in_dim(queries, first_row, RB, 0).reshape(RB * grid_cols, HEADS, HD)
            block_keys = lax.dynamic_slice_in_dim(keys, key_row, window, 0).reshape(window * grid_cols, HEADS, HD)
            block_values = lax.dynamic_slice_in_dim(values, key_row, window, 0).reshape(window * grid_cols, HEADS, HD)
            query_items = jnp.repeat(lax.dynamic_slice_in_dim(item_of_row, first_row, RB, 0), grid_cols)
            key_items = jnp.repeat(lax.dynamic_slice_in_dim(item_of_row, key_row, window, 0), grid_cols)
            scores = low_back(jnp.einsum('qhd,khd->hqk', block_queries, block_keys, precision=HIGH) * score_scale)
            scores = jnp.where((query_items[:, None] == key_items[None, :])[None], scores, NEG)
            weights = jnp.exp(scores - lax.optimization_barrier(jnp.max(scores, axis=-1, keepdims=True)))
            probability = low(weights / lax.optimization_barrier(jnp.sum(weights, axis=-1, keepdims=True)))
            attended = jnp.einsum('hqk,khd->qhd', probability, block_values, precision=HIGH)
            block_cross = lax.dynamic_slice_in_dim(cross_raw, first_row, RB, 0).reshape(RB * grid_cols, HEADS, HD)
            cross_scores = low_back(jnp.einsum('qhd,khd->hqk', block_cross, caption_keys, precision=HIGH) * score_scale)
            cross_weights = jnp.exp(cross_scores - lax.optimization_barrier(jnp.max(cross_scores, axis=-1, keepdims=True)))
            cross_probability = low(cross_weights / lax.optimization_barrier(jnp.sum(cross_weights, axis=-1, keepdims=True)))
            crossed = low_back(jnp.einsum('hqk,khd->qhd', cross_probability, caption_values, precision=HIGH))
            return (attended, crossed)
        attended, crossed = lax.map(jax.checkpoint(attend_block), jnp.arange(block_count, dtype=jnp.int32))
        attended = attended.reshape(grid_rows, grid_cols, D)
        crossed = crossed.reshape(grid_rows, grid_cols, D)
        mixed = low_back(low(attended + jnp.tanh(cross_gate) * crossed))
        branch = low_back(matmul(mixed, output_weight))
        residual = embedded + jnp.tanh(first_gate) * branch
        inner = low(norm_rows(residual) * feedforward_gain * (1.0 + second_scale))
        gate = low_back(matmul(inner, gate_weight))
        upward = low_back(matmul(inner, up_weight))
        hidden = low(jax.nn.silu(gate) * upward)
        feed = low_back(matmul(hidden, down_weight))
        result = residual + jnp.tanh(second_gate) * feed
        patches = low(matmul(low(result), unpatch_weight))
        return spread_cells(jnp.pad(patches, ((1, 1), (1, 1), (0, 0))), grid_rows, grid_cols, 16)
    weights_in = tuple((weight.astype(jnp.float32) for weight in (embedding, embed_bias, band_table, adaptive, adaptive_bias, attention_gain, projection, query_gain, key_gain, cross_query, caption_weight, cross_gate, output_weight, feedforward_gain, gate_weight, up_weight, down_weight, unpatch_weight)))
    prediction, pull = jax.vjp(forward, latents.astype(jnp.float32), *weights_in)
    grads = pull(cotangent.astype(jnp.float32))
    return (prediction.astype(jnp.bfloat16), grads[0].astype(jnp.bfloat16), grads[1], grads[2], grads[3], grads[4], grads[5], grads[6], grads[7], grads[8], grads[9], grads[10], grads[11], grads[12], grads[13], grads[14], grads[15], grads[16], grads[17], grads[18])
```

```python
import functools
import math

import jax
import jax.numpy as jnp
import numpy as np
from jax import lax
from jax.experimental import pallas as pl
from jax.experimental.pallas import tpu as pltpu
from jax.sharding import Mesh, PartitionSpec as P

HD = 64
NBAND = 8
MOSTH = 8
HALO = 8
LANES = 256

EPS = 1e-06
THETA = 10000.0
NEG = -1e30
HIGH = lax.Precision.HIGHEST
OFFSETS = ((-1, -1), (-1, 0), (-1, 1), (0, -1), (0, 0), (0, 1), (1, -1), (1, 0), (1, 1))
ALL = ("row", "sub", "tp")
COL = ("sub", "tp")
f32 = jnp.float32
bf16 = jnp.bfloat16


def spread_all(value, axes):
    count = lax.axis_size(axes)
    return lax.all_to_all(
        jnp.broadcast_to(value[None], (count,) + value.shape), axes, 0, 0, tiled=True
    )


def swap(value, axes):
    return lax.all_to_all(value, axes, 0, 0, tiled=True)


def dot(left, right, left_dim, right_dim, precision=None):
    return lax.dot_general(
        left,
        right,
        (((left_dim,), (right_dim,)), ((), ())),
        precision=precision,
        preferred_element_type=f32,
    )


def shift(cells, axis, up):
    count = lax.axis_size(axis)
    pairs = [(i, i + 1) if up else (i + 1, i) for i in range(count - 1)]
    return lax.ppermute(cells, axis, pairs)


def with_halo(cells, sides, width):
    for axis, dim in sides:
        head = lax.slice_in_dim(cells, 0, width, axis=dim)
        tail = lax.slice_in_dim(cells, cells.shape[dim] - width, cells.shape[dim], axis=dim)
        cells = jnp.concatenate([shift(tail, axis, True), cells, shift(head, axis, False)], axis=dim)
    return cells


def silu_slope(values):
    sigmoid = jax.nn.sigmoid(values)
    return sigmoid * (1.0 + values * (1.0 - sigmoid))


def gather_cells(padded, row_count, col_count):
    return jnp.concatenate(
        [
            padded[1 + row_off : 1 + row_off + row_count, 1 + col_off : 1 + col_off + col_count]
            for row_off, col_off in OFFSETS
        ],
        axis=-1,
    )


def spread_cells(padded, row_count, col_count, channels):
    summed = jnp.zeros((row_count, col_count, channels), f32)
    for offset_index, (row_off, col_off) in enumerate(OFFSETS):
        summed = summed + padded[
            1 - row_off : 1 - row_off + row_count,
            1 - col_off : 1 - col_off + col_count,
            offset_index * channels : (offset_index + 1) * channels,
        ].astype(f32)
    return summed


def row_items(heights, band_ids, row_count):
    count = heights.shape[0]
    below = jnp.arange(count)[:, None] >= jnp.arange(count)[None, :]
    item_ends = jnp.sum(jnp.where(below, heights[None, :], 0), axis=1)
    row_ids = jnp.arange(row_count, dtype=jnp.int32)
    item_of_row = jnp.sum((item_ends[None, :] <= row_ids[:, None]).astype(jnp.int32), axis=1)
    picked = item_of_row[:, None] == jnp.arange(count, dtype=jnp.int32)[None, :]
    item_top = jnp.sum(jnp.where(picked, (item_ends - heights)[None, :], 0), axis=1)
    row_band = jnp.sum(jnp.where(picked, band_ids[None, :], 0), axis=1)
    band_onehot = (row_band[:, None] == jnp.arange(NBAND, dtype=jnp.int32)[None, :]).astype(f32)
    return (item_of_row, row_ids - item_top, band_onehot)


def rotate(values, tables):
    cos_rows, sin_rows, cos_cols, sin_cols = tables
    first, second, third, fourth = (values[:, i] for i in range(4))
    return jnp.stack(
        [
            first * cos_rows - second * sin_rows,
            first * sin_rows + second * cos_rows,
            third * cos_cols - fourth * sin_cols,
            third * sin_cols + fourth * cos_cols,
        ],
        axis=1,
    )


def head_norm(raw, gain, tables):
    heads, _, tokens = raw.shape
    normed = raw * lax.rsqrt(jnp.mean(raw * raw, axis=1, keepdims=True) + EPS) * gain
    return rotate(normed.reshape(heads, 4, HD // 4, tokens), tables).reshape(raw.shape)


def head_norm_back(raw, gain, tables, grad):
    heads, _, tokens = raw.shape
    cos_rows, sin_rows, cos_cols, sin_cols = tables
    turned = rotate(
        grad.reshape(heads, 4, HD // 4, tokens), (cos_rows, -sin_rows, cos_cols, -sin_cols)
    ).reshape(raw.shape)
    inverse = lax.rsqrt(jnp.mean(raw * raw, axis=1, keepdims=True) + EPS)
    unit = raw * inverse
    grad_gain = jnp.sum(turned * unit, axis=2)
    weighted = turned * gain
    grad_raw = inverse * (weighted - unit * jnp.mean(weighted * unit, axis=1, keepdims=True))
    return grad_raw, grad_gain


def tn(left, right):
    return dot(left, right, 0, 0)


def nt(left, right):
    return dot(left, right, 1, 1)


def nn(left, right):
    return dot(left, right, 1, 0)


def masked_scores(key_block, query_block, bias):
    return tn(key_block, query_block) + bias


def block_bias(items_ref, item_query, chunk, key_rows, width):
    rows = []
    for key_row in range(key_rows):
        item = items_ref[chunk * key_rows + key_row]
        rows.append(
            jnp.broadcast_to(jnp.where(item_query == item, 0.0, NEG), (width, item_query.shape[1]))
        )
    return rows[0] if len(rows) == 1 else jnp.concatenate(rows, axis=0)


def attend_kernel(
    heads,
    key_rows,
    key_width,
    items_ref,
    low_ref,
    high_ref,
    item_query_ref,
    query_ref,
    key_ref,
    value_ref,
    cross_ref,
    caption_key_ref,
    caption_value_ref,
    gate_ref,
    mixed_ref,
    self_ref,
    crossed_ref,
    stats_ref,
    total_ref,
):
    block = pl.program_id(0)
    item_query = item_query_ref[0:1, :]
    self_ref[...] = jnp.zeros_like(self_ref)
    total_ref[...] = jnp.zeros_like(total_ref)

    def chunk_step(chunk, carry):
        lanes = pl.ds(pl.multiple_of(chunk * LANES, LANES), LANES)
        bias = block_bias(items_ref, item_query, chunk, key_rows, key_width)
        for head in range(heads):
            part = slice(head * HD, (head + 1) * HD)
            scores = masked_scores(key_ref[part, lanes], query_ref[part, :], bias)
            weights = jnp.exp(scores)
            total_ref[head : head + 1, :] += jnp.sum(weights, axis=0, keepdims=True)
            self_ref[part, :] += nn(value_ref[part, lanes], weights.astype(bf16))
        return carry

    lax.fori_loop(low_ref[block], high_ref[block], chunk_step, 0)
    stats_ref[...] = jnp.zeros_like(stats_ref)
    for head in range(heads):
        part = slice(head * HD, (head + 1) * HD)
        total = total_ref[head : head + 1, :]
        attended = self_ref[part, :] / total
        self_ref[part, :] = attended
        stats_ref[head : head + 1, :] = jnp.log(total)
        scores = tn(caption_key_ref[part, :], cross_ref[part, :])
        best = jnp.max(scores, axis=0, keepdims=True)
        weights = jnp.exp(scores - best)
        total = jnp.sum(weights, axis=0, keepdims=True)
        crossed = nn(caption_value_ref[part, :], (weights / total).astype(bf16))
        crossed_ref[part, :] = crossed
        stats_ref[heads + head : heads + head + 1, :] = best + jnp.log(total)
        mixed_ref[part, :] = (attended + gate_ref[part, 0:1] * crossed).astype(bf16)


def cross_back_kernel(
    heads,
    cross_ref,
    caption_key_ref,
    caption_value_ref,
    gate_ref,
    grad_ref,
    crossed_ref,
    stats_ref,
    grad_cross_ref,
    grad_key_ref,
    grad_value_ref,
    grad_gate_ref,
):
    @pl.when(pl.program_id(0) == 0)
    def _():
        grad_key_ref[...] = jnp.zeros_like(grad_key_ref)
        grad_value_ref[...] = jnp.zeros_like(grad_value_ref)
        grad_gate_ref[...] = jnp.zeros_like(grad_gate_ref)

    for head in range(heads):
        part = slice(head * HD, (head + 1) * HD)
        gate = gate_ref[part, 0:1]
        grad_wide = grad_ref[part, :].astype(f32)
        grad_crossed = (gate * grad_wide).astype(bf16)
        grad_gate_ref[part, 0:1] += jnp.sum(
            grad_wide * crossed_ref[part, :], axis=1, keepdims=True
        ) * (1.0 - gate * gate)
        scores = tn(caption_key_ref[part, :], cross_ref[part, :])
        weights = jnp.exp(scores - stats_ref[heads + head : heads + head + 1, :])
        grad_weights = tn(caption_value_ref[part, :], grad_crossed)
        delta = jnp.sum(weights * grad_weights, axis=0, keepdims=True)
        grad_scores = (weights * (grad_weights - delta)).astype(bf16)
        grad_cross_ref[part, :] = (
            nn(caption_key_ref[part, :], grad_scores) * (1.0 / math.sqrt(HD))
        ).astype(bf16)
        grad_key_ref[part, :] += nt(cross_ref[part, :], grad_scores)
        grad_value_ref[part, :] += nt(grad_crossed, weights.astype(bf16))


def attend_back_kernel(
    heads,
    key_rows,
    key_width,
    items_ref,
    low_ref,
    high_ref,
    item_query_ref,
    query_ref,
    key_ref,
    value_ref,
    grad_ref,
    self_ref,
    stats_ref,
    grad_query_ref,
    grad_key_ref,
    grad_value_ref,
    delta_ref,
):
    block = pl.program_id(0)

    @pl.when(block == 0)
    def _():
        grad_key_ref[...] = jnp.zeros_like(grad_key_ref)
        grad_value_ref[...] = jnp.zeros_like(grad_value_ref)

    item_query = item_query_ref[0:1, :]
    grad_query_ref[...] = jnp.zeros_like(grad_query_ref)
    for head in range(heads):
        part = slice(head * HD, (head + 1) * HD)
        delta_ref[head : head + 1, :] = jnp.sum(
            grad_ref[part, :].astype(f32) * self_ref[part, :], axis=0, keepdims=True
        )

    def chunk_step(chunk, carry):
        lanes = pl.ds(pl.multiple_of(chunk * LANES, LANES), LANES)
        bias = block_bias(items_ref, item_query, chunk, key_rows, key_width)
        for head in range(heads):
            part = slice(head * HD, (head + 1) * HD)
            key_block = key_ref[part, lanes]
            query_block = query_ref[part, :]
            grad_block = grad_ref[part, :]
            scores = masked_scores(key_block, query_block, bias)
            weights = jnp.exp(scores - stats_ref[head : head + 1, :])
            grad_weights = tn(value_ref[part, lanes], grad_block)
            grad_scores = (weights * (grad_weights - delta_ref[head : head + 1, :])).astype(bf16)
            grad_query_ref[part, :] += nn(key_block, grad_scores)
            grad_key_ref[part, lanes] += nt(query_block, grad_scores)
            grad_value_ref[part, lanes] += nt(grad_block, weights.astype(bf16))
        return carry

    lax.fori_loop(low_ref[block], high_ref[block], chunk_step, 0)


def on_device(
    latents,
    captions,
    item_heights,
    item_bands,
    embedding,
    embed_bias,
    band_table,
    adaptive,
    adaptive_bias,
    attention_gain,
    projection,
    query_gain,
    key_gain,
    cross_query,
    caption_weight,
    cross_gate,
    output_weight,
    feedforward_gain,
    gate_weight,
    up_weight,
    down_weight,
    unpatch_weight,
    cotangent,
):
    rows_n, sub_n, tp_n = (lax.axis_size(a) for a in ALL)
    col_n = sub_n * tp_n
    all_n = rows_n * col_n
    row = lax.axis_index("row")
    sub = lax.axis_index("sub")
    tp = lax.axis_index("tp")
    tile_rows, tile_cols, channels = latents.shape
    grid_rows = tile_rows * rows_n
    grid_cols = tile_cols * col_n
    span = tile_cols * tp_n
    tokens = tile_rows * span
    own = tile_rows * tile_cols
    width = embed_bias.shape[0]
    model = width * col_n
    head_width = model // tp_n
    heads = head_width // HD
    owned = model // all_n
    quarter = width // rows_n
    ff = gate_weight.shape[1]
    ff_part = ff // col_n
    ff_mine = ff // tp_n
    text = captions.shape[0]
    patch = 9 * channels

    grid = spread_all(jnp.concatenate([latents, cotangent], axis=-1), ALL)
    grid = (
        grid.reshape(rows_n, col_n, tile_rows, tile_cols, 2 * channels)
        .transpose(0, 2, 1, 3, 4)
        .reshape(grid_rows, grid_cols, 2 * channels)
    )
    grid = jnp.pad(grid, ((1, 1), (1, 1), (0, 0)))
    bordered = lax.dynamic_slice(
        grid,
        (row * tile_rows, sub * span, 0),
        (tile_rows + 2, span + 2, 2 * channels),
    )
    packed = jnp.concatenate(
        [
            embedding,
            unpatch_weight.T,
            embed_bias[None],
            attention_gain[None],
            feedforward_gain[None],
            band_table,
            adaptive_bias.reshape(-1, width),
        ],
        axis=0,
    )
    packed = spread_all(packed, COL)
    parts = packed.shape[1]
    bias_all = packed[:, 2 * patch + 3 + NBAND :].reshape(-1).astype(f32)
    packed = packed.transpose(1, 0, 2).reshape(parts, model)
    full_embedding = packed[0:patch]
    full_unpatch = packed[patch : 2 * patch]
    full_bias, attn_gain, ff_gain = (packed[2 * patch + i].astype(f32) for i in range(3))
    full_band = packed[2 * patch + 3 : 2 * patch + 3 + NBAND].astype(f32)

    mod_width = adaptive.shape[1] // rows_n
    mod_part = jnp.dot(
        jax.nn.silu(band_table.astype(f32)),
        lax.dynamic_slice_in_dim(adaptive, row * mod_width, mod_width, 1).astype(f32),
        precision=HIGH,
    )
    mod_part = jnp.sum(spread_all(mod_part, COL), axis=0)
    modulations = (
        spread_all(mod_part, "row").transpose(1, 0, 2).reshape(NBAND, adaptive.shape[1]) + bias_all
    )
    item_of_row, row_place, band_onehot = row_items(item_heights, item_bands, grid_rows)
    tile_onehot = lax.dynamic_slice_in_dim(band_onehot, row * tile_rows, tile_rows, 0)
    tile_modulation = jnp.dot(tile_onehot, modulations, precision=HIGH)[:, None, :]
    first_scale, first_gate, second_scale, second_gate = (
        tile_modulation[..., i * model : (i + 1) * model] for i in range(4)
    )

    def fetch(weight):
        piece = lax.dynamic_slice_in_dim(weight, row * quarter, quarter, 0).transpose(1, 0, 2)
        piece = jnp.broadcast_to(piece[None], (sub_n,) + piece.shape).reshape(
            col_n, quarter, weight.shape[2]
        )
        piece = swap(piece, COL)
        whole = lax.all_gather(piece, "row", axis=0, tiled=False)
        return whole.transpose(1, 0, 2, 3).reshape(model, weight.shape[2])

    weight_qkvc = fetch(
        jnp.concatenate(
            [
                projection.reshape(width, 3, tp_n, head_width),
                cross_query.reshape(width, 1, tp_n, head_width),
            ],
            axis=1,
        )
        .transpose(0, 2, 1, 3)
        .reshape(width, tp_n, 4 * head_width)
    )

    text_part = text // rows_n
    cap_part = jnp.dot(
        lax.dynamic_slice(
            captions,
            (row * text_part, (sub * tp_n + tp) * caption_weight.shape[0]),
            (text_part, caption_weight.shape[0]),
        ),
        caption_weight,
        preferred_element_type=f32,
    ).astype(bf16)
    cap_part = cap_part.reshape(text_part, 2, tp_n, head_width).transpose(2, 0, 1, 3)
    cap_part = jnp.broadcast_to(cap_part[None], (sub_n,) + cap_part.shape).reshape(
        col_n, text_part, 2 * head_width
    )
    cap_part = jnp.sum(swap(cap_part, COL).astype(f32), axis=0).astype(bf16)
    caption_heads = spread_all(cap_part, "row").reshape(text, 2 * head_width).T
    caption_keys = caption_heads[:head_width]
    caption_values = caption_heads[head_width:]

    neighbours = gather_cells(bordered[..., 0:channels], tile_rows, span)
    patch_grads = gather_cells(bordered[..., channels : 2 * channels], tile_rows, span)
    embedded = (
        jnp.dot(neighbours, full_embedding, preferred_element_type=f32) + full_bias
    )
    inverse_one = lax.rsqrt(jnp.mean(embedded * embedded, axis=-1, keepdims=True) + EPS)
    normed = (embedded * inverse_one * (attn_gain * (1.0 + first_scale))).astype(bf16)
    normed = normed.reshape(tokens, model)
    raw = dot(weight_qkvc, normed, 0, 1).astype(bf16)
    raw_query = raw[0:head_width].reshape(heads, HD, tokens)
    raw_key = raw[head_width : 2 * head_width].reshape(heads, HD, tokens)
    values = raw[2 * head_width : 3 * head_width]
    score_scale = 1.0 / math.sqrt(HD)
    raw_cross = raw[3 * head_width :] * jnp.asarray(score_scale, bf16)

    frequency = THETA ** (-jnp.arange(HD // 4, dtype=f32) / (HD // 4))
    tile_place = lax.dynamic_slice_in_dim(row_place, row * tile_rows, tile_rows, 0)
    row_angles = frequency[:, None] * tile_place.astype(f32)[None, :]
    col_angles = frequency[:, None] * (sub * span + jnp.arange(span)).astype(f32)[None, :]

    def on_rows(table):
        return jnp.repeat(table, span, axis=1)

    def on_cols(table):
        return jnp.tile(table, (1, tile_rows))

    tables = (
        on_rows(jnp.cos(row_angles)),
        on_rows(jnp.sin(row_angles)),
        on_cols(jnp.cos(col_angles)),
        on_cols(jnp.sin(col_angles)),
    )
    gain_query = _mine(query_gain, tp, sub_n).astype(f32).reshape(heads, HD, 1)
    gain_key = _mine(key_gain, tp, sub_n).astype(f32).reshape(heads, HD, 1)
    gate_cross = jnp.tanh(_mine(cross_gate, tp, sub_n).astype(f32))
    query_wide = raw_query.astype(f32)
    key_wide = raw_key.astype(f32)
    queries = head_norm(query_wide, gain_query, tables).astype(bf16) * jnp.asarray(
        score_scale, bf16
    )
    queries = queries.reshape(head_width, tokens)
    keys = head_norm(key_wide, gain_key, tables).astype(bf16).reshape(head_width, tokens)

    both = jnp.concatenate([keys, values], axis=0)
    if sub_n > 1:
        both = (
            lax.all_gather(both, "sub", axis=0)
            .reshape(sub_n, 2 * head_width, tile_rows, span)
            .transpose(1, 2, 0, 3)
            .reshape(2 * head_width, tile_rows * grid_cols)
        )
    edge = HALO * grid_cols
    both = jnp.concatenate(
        [
            shift(both[:, both.shape[1] - edge :], "row", True),
            both,
            shift(both[:, :edge], "row", False),
        ],
        axis=1,
    )
    keys_near, values_near = both[:head_width], both[head_width:]

    near_rows = tile_rows + 2 * HALO
    key_rows = max(1, LANES // grid_cols)
    key_width = LANES // key_rows
    block_rows = LANES // span
    blocks = tile_rows // block_rows
    items_padded = jnp.concatenate(
        [
            jnp.full((HALO,), -1, jnp.int32),
            item_of_row.astype(jnp.int32),
            jnp.full((HALO,), item_heights.shape[0] + 1, jnp.int32),
        ]
    )
    items_near = lax.dynamic_slice_in_dim(items_padded, row * tile_rows, near_rows, 0)
    item_query = jnp.repeat(items_near[HALO : HALO + tile_rows], span)[None, :]
    chunk_items = jnp.repeat(items_near, grid_cols // (key_width)).reshape(-1, key_rows)
    query_items = items_near[HALO : HALO + tile_rows].reshape(blocks, block_rows)
    before = chunk_items[None, :, -1] < query_items[:, None, 0]
    after = chunk_items[None, :, 0] <= query_items[:, None, -1]
    low = jnp.sum(before.astype(jnp.int32), axis=1)
    high = jnp.sum(after.astype(jnp.int32), axis=1)
    chunk_items = chunk_items.reshape(-1)
    near = near_rows * grid_cols

    def by_block(count):
        return pl.BlockSpec((count, LANES), lambda i, *_: (0, i))

    def whole(*shape):
        return pl.BlockSpec(shape, lambda i, *_: (0, 0))

    vmem = pltpu.CompilerParams(vmem_limit_bytes=48 * 2**20)
    gate_column = gate_cross[:, None]
    mixed, self_out, crossed, stats = pl.pallas_call(
        functools.partial(attend_kernel, heads, key_rows, key_width),
        grid_spec=pltpu.PrefetchScalarGridSpec(
            num_scalar_prefetch=3,
            grid=(blocks,),
            in_specs=[
                by_block(1),
                by_block(head_width),
                whole(head_width, near),
                whole(head_width, near),
                by_block(head_width),
                whole(head_width, text),
                whole(head_width, text),
                whole(head_width, 1),
            ],
            out_specs=[by_block(head_width), by_block(head_width), by_block(head_width), by_block(8)],
            scratch_shapes=[pltpu.VMEM((8, LANES), f32)],
        ),
        out_shape=[
            jax.ShapeDtypeStruct((head_width, tokens), bf16),
            jax.ShapeDtypeStruct((head_width, tokens), f32),
            jax.ShapeDtypeStruct((head_width, tokens), f32),
            jax.ShapeDtypeStruct((8, tokens), f32),
        ],
        compiler_params=vmem,
        name="attend",
    )(
        chunk_items,
        low,
        high,
        item_query,
        queries,
        keys_near,
        values_near,
        raw_cross,
        caption_keys,
        caption_values,
        gate_column,
    )

    full_output = lax.all_gather(output_weight, COL, axis=0, tiled=True)
    mixed_all = lax.all_gather(mixed, "tp", axis=0, tiled=True)
    branch = dot(mixed_all, full_output, 0, 0).reshape(tile_rows, span, model)
    tanh_one = jnp.tanh(first_gate)
    residual = embedded + tanh_one * branch
    inverse_two = lax.rsqrt(jnp.mean(residual * residual, axis=-1, keepdims=True) + EPS)
    inner = (residual * inverse_two * (ff_gain * (1.0 + second_scale))).astype(bf16)
    inner = inner.reshape(tokens, model)

    def ff_slices(weight):
        return weight.reshape(width, sub_n, tp_n, ff_part).transpose(0, 2, 1, 3)

    weight_gu = fetch(
        jnp.stack([ff_slices(gate_weight), ff_slices(up_weight)], axis=2).reshape(
            width, tp_n, 2 * ff_mine
        )
    )
    down_mine = down_weight
    if sub_n > 1:
        down_mine = lax.all_gather(down_weight, "sub", axis=0, tiled=True)
    gate_up = dot(inner, weight_gu, 1, 0)
    gate = gate_up[:, :ff_mine]
    upward = gate_up[:, ff_mine:]
    sigmoid = jax.nn.sigmoid(gate)
    hidden = (gate * sigmoid * upward).astype(bf16)

    def to_tiles(partial):
        count = partial.shape[-1]
        return (
            partial.astype(bf16)
            .reshape(tile_rows, tp_n, tile_cols, count)
            .transpose(1, 0, 2, 3)
            .reshape(tokens, count)
        )

    def scatter(partial):
        return lax.psum_scatter(to_tiles(partial), "tp", scatter_dimension=0, tiled=True).astype(f32)

    def own_tile(values):
        return lax.dynamic_slice_in_dim(
            values.reshape(tile_rows, span, -1), tp * tile_cols, tile_cols, 1
        )

    tanh_two = jnp.tanh(second_gate)
    grad_result = jnp.dot(patch_grads, full_unpatch, preferred_element_type=f32)
    grad_feed = (tanh_two * grad_result).astype(bf16).reshape(tokens, model)
    grad_hidden = dot(grad_feed, down_mine, 1, 1)
    grad_gate = (
        grad_hidden * upward * (sigmoid * (1.0 + gate * (1.0 - sigmoid)))
    ).astype(bf16)
    grad_upward = (grad_hidden * (gate * sigmoid)).astype(bf16)
    grad_gu = jnp.concatenate([grad_gate, grad_upward], axis=1)
    grad_inner = scatter(dot(grad_gu, weight_gu, 1, 1))
    feed = scatter(dot(hidden, down_mine, 1, 0))

    own_residual = own_tile(residual)
    own_embedded = own_tile(embedded)
    own_branch = own_tile(branch)
    own_patch_grads = own_tile(patch_grads)
    tile3 = (tile_rows, tile_cols, model)
    grad_inner = grad_inner.reshape(tile3)
    feed = feed.reshape(tile3)
    own_grad_result = jnp.dot(own_patch_grads, full_unpatch, preferred_element_type=f32)
    own_inverse = lax.rsqrt(jnp.mean(own_residual * own_residual, axis=-1, keepdims=True) + EPS)
    unit_two = own_residual * own_inverse
    grad_unit = grad_inner * (ff_gain * (1.0 + second_scale))
    grad_residual = own_grad_result + own_inverse * (
        grad_unit - unit_two * jnp.mean(grad_unit * unit_two, axis=-1, keepdims=True)
    )
    grad_inner_unit = grad_inner * unit_two
    grad_branch = (tanh_one * grad_residual).astype(bf16)
    grad_mixed_own = dot(grad_branch.reshape(own, model), full_output, 1, 1).astype(bf16)
    grad_mixed = swap(
        grad_mixed_own.reshape(own, tp_n, head_width).transpose(1, 0, 2), "tp"
    )
    grad_mixed = (
        grad_mixed.reshape(tp_n, tile_rows, tile_cols, head_width)
        .transpose(1, 0, 2, 3)
        .reshape(tokens, head_width)
        .T
    )

    result_low = (own_residual + tanh_two * feed).astype(bf16)
    patches = dot(result_low.reshape(own, model), full_unpatch, 1, 1).astype(bf16)
    patches = patches.reshape(tile_rows, tile_cols, patch)
    patch_border = with_halo(patches, (("row", 0), (COL, 1)), 1)
    prediction = spread_cells(patch_border, tile_rows, tile_cols, channels).astype(bf16)
    grad_unpatch = dot(result_low.reshape(own, model), own_patch_grads.reshape(own, patch), 0, 0)

    rows_second_scale = jnp.sum(grad_inner_unit * ff_gain, axis=1)
    grad_ff_gain = jnp.sum(grad_inner_unit * (1.0 + second_scale), axis=(0, 1))
    rows_second_gate = jnp.sum(
        own_grad_result * feed * (1.0 - tanh_two * tanh_two), axis=1
    )
    rows_first_gate = jnp.sum(
        grad_residual * own_branch * (1.0 - tanh_one * tanh_one), axis=1
    )

    mixed_own = (
        lax.dynamic_slice_in_dim(
            mixed_all.reshape(model, tile_rows, span), tp * tile_cols, tile_cols, 2
        )
        .reshape(model, own)
        .T
    )
    mixed_rows = swap(
        mixed_own.reshape(own, rows_n, model // rows_n).transpose(1, 0, 2), "row"
    ).reshape(rows_n * own, model // rows_n)
    branch_rows = lax.all_gather(grad_branch.reshape(own, model), "row", axis=0, tiled=True)
    grad_output = lax.psum_scatter(
        dot(mixed_rows, branch_rows, 0, 0).astype(bf16), COL, scatter_dimension=0, tiled=True
    ).astype(f32)

    grad_cross, grad_cap_keys, grad_cap_values, grad_gate_part = pl.pallas_call(
        functools.partial(cross_back_kernel, heads),
        grid=(blocks,),
        in_specs=[
            by_block(head_width),
            whole(head_width, text),
            whole(head_width, text),
            whole(head_width, 1),
            by_block(head_width),
            by_block(head_width),
            by_block(8),
        ],
        out_specs=[
            by_block(head_width),
            whole(head_width, text),
            whole(head_width, text),
            whole(head_width, 128),
        ],
        out_shape=[
            jax.ShapeDtypeStruct((head_width, tokens), bf16),
            jax.ShapeDtypeStruct((head_width, text), f32),
            jax.ShapeDtypeStruct((head_width, text), f32),
            jax.ShapeDtypeStruct((head_width, 128), f32),
        ],
        compiler_params=vmem,
        name="cross_back",
    )(raw_cross, caption_keys, caption_values, gate_column, grad_mixed, crossed, stats)

    grad_queries, grad_keys, grad_values = pl.pallas_call(
        functools.partial(attend_back_kernel, heads, key_rows, key_width),
        grid_spec=pltpu.PrefetchScalarGridSpec(
            num_scalar_prefetch=3,
            grid=(blocks,),
            in_specs=[
                by_block(1),
                by_block(head_width),
                whole(head_width, near),
                whole(head_width, near),
                by_block(head_width),
                by_block(head_width),
                by_block(8),
            ],
            out_specs=[by_block(head_width), whole(head_width, near), whole(head_width, near)],
            scratch_shapes=[pltpu.VMEM((8, LANES), f32)],
        ),
        out_shape=[
            jax.ShapeDtypeStruct((head_width, tokens), f32),
            jax.ShapeDtypeStruct((head_width, near), f32),
            jax.ShapeDtypeStruct((head_width, near), f32),
        ],
        compiler_params=vmem,
        name="attend_back",
    )(chunk_items, low, high, item_query, queries, keys_near, values_near, grad_mixed, self_out, stats)

    grad_cap = jnp.concatenate([grad_cap_keys, grad_cap_values], axis=0).astype(bf16)
    share = 2 * head_width // rows_n
    if sub_n > 1:
        grad_cap = lax.psum_scatter(
            grad_cap.reshape(rows_n, sub_n, share // sub_n, text).reshape(-1, text),
            ("row", "sub"),
            scatter_dimension=0,
            tiled=True,
        )
    else:
        grad_cap = jnp.sum(
            swap(grad_cap.reshape(rows_n, share, text), "row").astype(f32), axis=0
        ).astype(bf16)
    grad_cap = lax.all_gather(grad_cap, ALL, axis=0, tiled=True)
    grad_cap = (
        grad_cap.reshape(rows_n * sub_n, tp_n, share // sub_n, text)
        .transpose(1, 0, 2, 3)
        .reshape(tp_n, 2, head_width, text)
        .transpose(1, 0, 2, 3)
        .reshape(2 * model, text)
    )
    index = (row * sub_n + sub) * tp_n + tp
    cap_own = captions.shape[1] // all_n
    own_captions = lax.dynamic_slice_in_dim(captions, index * cap_own, cap_own, 1)
    grad_caption = dot(own_captions, grad_cap, 0, 1)

    grad_both = jnp.concatenate([grad_keys, grad_values], axis=0)
    upper = grad_both[:, :edge].astype(bf16)
    lower = grad_both[:, near - edge :].astype(bf16)
    middle = grad_both[:, edge : near - edge]
    from_above = shift(lower, "row", True).astype(f32)
    from_below = shift(upper, "row", False).astype(f32)
    side = middle.shape[1] - edge
    middle = (
        middle
        + jnp.pad(from_above, ((0, 0), (0, side)))
        + jnp.pad(from_below, ((0, 0), (side, 0)))
    )
    if sub_n > 1:
        middle = (
            middle.astype(bf16)
            .reshape(2 * head_width, tile_rows, sub_n, span)
            .transpose(2, 0, 1, 3)
            .reshape(sub_n, 2 * head_width, tokens)
        )
        middle = jnp.sum(swap(middle, "sub").astype(f32), axis=0)
    grad_keys = middle[:head_width].astype(bf16).astype(f32).reshape(heads, HD, tokens)
    grad_values = middle[head_width:].astype(bf16)
    grad_queries = (grad_queries * score_scale).astype(bf16).astype(f32).reshape(heads, HD, tokens)
    grad_raw_query, part_query_gain = head_norm_back(query_wide, gain_query, tables, grad_queries)
    grad_raw_key, part_key_gain = head_norm_back(key_wide, gain_key, tables, grad_keys)
    grad_raw = jnp.concatenate(
        [
            grad_raw_query.astype(bf16).reshape(head_width, tokens),
            grad_raw_key.astype(bf16).reshape(head_width, tokens),
            grad_values,
            grad_cross,
        ],
        axis=0,
    )

    grad_normed = dot(grad_raw, weight_qkvc, 0, 1).reshape(tile_rows, span, model)
    unit_one = embedded * inverse_one
    normed_unit = grad_normed * unit_one
    grad_unit_one = grad_normed * (attn_gain * (1.0 + first_scale))
    part_embedded = inverse_one * (
        grad_unit_one - unit_one * jnp.mean(grad_unit_one * unit_one, axis=-1, keepdims=True)
    )
    part_attn_gain = jnp.sum(normed_unit * (1.0 + first_scale), axis=(0, 1))
    rows_first_scale = jnp.sum(normed_unit * attn_gain, axis=1)
    mine = (jnp.arange(span) // tile_cols == tp)[None, :, None]
    spread_residual = jnp.where(mine, jnp.tile(grad_residual, (1, tp_n, 1)), 0.0)
    part_embedded = (part_embedded + spread_residual).astype(bf16)
    part_flat = part_embedded.reshape(tokens, model)
    grad_embedding = dot(neighbours.reshape(tokens, patch), part_flat, 0, 0)
    grad_embed_bias = jnp.sum(part_embedded.astype(f32), axis=(0, 1))
    cells = dot(part_flat, full_embedding, 1, 1).reshape(tile_rows, span, patch)
    around = spread_cells(
        jnp.pad(cells, ((2, 2), (2, 2), (0, 0))), tile_rows + 2, span + 2, channels
    )
    inside = around[:, 1 : span + 1]
    if sub_n > 1:
        from_left = shift(around[:, span + 1 :].astype(bf16), "sub", True).astype(f32)
        from_right = shift(around[:, :1].astype(bf16), "sub", False).astype(f32)
        inside = (
            inside
            + jnp.pad(from_left, ((0, 0), (0, span - 1), (0, 0)))
            + jnp.pad(from_right, ((0, 0), (span - 1, 0), (0, 0)))
        )
    inside = (
        inside.astype(bf16)
        .reshape(tile_rows + 2, tp_n, tile_cols, channels)
        .transpose(1, 0, 2, 3)
    )
    inside = jnp.sum(swap(inside, "tp").astype(f32), axis=0)
    from_above = shift(inside[tile_rows + 1 :].astype(bf16), "row", True).astype(f32)
    from_below = shift(inside[:1].astype(bf16), "row", False).astype(f32)
    latent_grad = (
        inside[1 : tile_rows + 1]
        + jnp.pad(from_above, ((0, tile_rows - 1), (0, 0), (0, 0)))
        + jnp.pad(from_below, ((tile_rows - 1, 0), (0, 0), (0, 0)))
    ).astype(bf16)

    def to_owner(partial):
        count = partial.shape[1]
        summed = lax.psum_scatter(
            partial.astype(bf16), ("row", "sub"), scatter_dimension=0, tiled=True
        )
        moved = swap(summed.reshape(tp_n, owned, count), "tp")
        return moved.transpose(1, 0, 2).astype(f32)

    grad_qkvc = to_owner(dot(normed, grad_raw, 0, 1))
    grad_qkvc = grad_qkvc.reshape(owned, tp_n, 4, head_width).transpose(0, 2, 1, 3)
    grad_projection = grad_qkvc[:, 0:3].reshape(owned, 3 * model)
    grad_cross_query = grad_qkvc[:, 3].reshape(owned, model)
    grad_gu_weight = to_owner(dot(inner, grad_gu, 0, 0))
    grad_gu_weight = grad_gu_weight.reshape(owned, tp_n, 2, sub_n, ff_part).transpose(2, 0, 3, 1, 4)
    grad_gu_weight = grad_gu_weight.reshape(2, owned, ff)
    grad_down = dot(hidden, grad_feed, 0, 0).astype(bf16)
    ff_own = ff // all_n
    grad_down = (
        grad_down.reshape(sub_n, rows_n, ff_own, model).transpose(1, 0, 2, 3).reshape(-1, model)
    )
    grad_down = lax.psum_scatter(grad_down, ("row", "sub"), scatter_dimension=0, tiled=True)
    moves = []
    for source in range(all_n):
        source_row, rest = divmod(source, col_n)
        moves.append((source, rest * rows_n + source_row))
    grad_down = lax.ppermute(grad_down, ALL, moves).astype(f32)

    def place(vector):
        return lax.dynamic_update_slice_in_dim(
            jnp.zeros((model,), f32), vector.reshape(-1), tp * head_width, 0
        )

    onehot = tile_onehot
    mod_grads = jnp.concatenate(
        [
            dot(onehot, rows, 0, 0, HIGH)
            for rows in (rows_first_scale, rows_first_gate, rows_second_scale, rows_second_gate)
        ],
        axis=0,
    )
    small = jnp.concatenate(
        [
            grad_embedding,
            grad_unpatch.T,
            mod_grads,
            grad_embed_bias[None],
            part_attn_gain[None],
            place(part_query_gain)[None],
            place(part_key_gain)[None],
            place(grad_gate_part[:, 0])[None],
            grad_ff_gain[None],
        ],
        axis=0,
    )
    count = small.shape[0]
    small = small.astype(bf16).reshape(count, all_n, owned).transpose(1, 0, 2)
    small = jnp.sum(swap(small, ALL).astype(f32), axis=0)
    grad_embedding = small[0:patch]
    grad_unpatch = small[patch : 2 * patch].T
    mods = 4 * NBAND
    vectors = small[2 * patch + mods :]
    all_mods = spread_all(small[2 * patch : 2 * patch + mods].astype(bf16), ALL).astype(f32)
    all_mods = (
        all_mods.reshape(all_n, 4, NBAND, owned).transpose(2, 1, 0, 3).reshape(NBAND, 4 * model)
    )
    own_band = lax.dynamic_slice_in_dim(full_band, index * owned, owned, 1)
    grad_adaptive = dot(jax.nn.silu(own_band), all_mods, 0, 0, HIGH)
    bias_own = 4 * owned
    grad_adaptive_bias = lax.dynamic_slice_in_dim(
        jnp.sum(all_mods, axis=0), index * bias_own, bias_own, 0
    )
    local_rows = lax.dynamic_slice_in_dim(adaptive, row * quarter, quarter, 0)
    local_band = lax.dynamic_slice_in_dim(band_table, row * quarter, quarter, 1).astype(f32)
    grad_band = dot(all_mods, local_rows.astype(f32), 1, 1, HIGH) * silu_slope(local_band)
    grad_band = lax.ppermute(grad_band, ALL, moves)

    return (
        prediction,
        latent_grad,
        grad_embedding,
        vectors[0],
        grad_band,
        grad_adaptive,
        grad_adaptive_bias,
        vectors[1],
        grad_projection,
        vectors[2],
        vectors[3],
        grad_cross_query,
        grad_caption,
        vectors[4],
        grad_output,
        vectors[5],
        grad_gu_weight[0],
        grad_gu_weight[1],
        grad_down,
        grad_unpatch,
    )


def _mine(vector, tp, sub_n):
    if sub_n == 1:
        return vector
    size = vector.shape[0] * sub_n
    whole = lax.all_gather(vector, COL, axis=0, tiled=True)
    return lax.dynamic_slice_in_dim(whole, tp * size, size, 0)


def solution(mesh):
    rows_n, col_n = mesh.shape["row"], mesh.shape["col"]

    def run(*args):
        heads = args[5].shape[0] // HD
        tp_n = math.gcd(heads, col_n)
        split = Mesh(mesh.devices.reshape(rows_n, col_n // tp_n, tp_n), ALL)
        in_specs = (
            P("row", COL, None),
            P(),
            P(),
            P(),
            P(None, COL),
            P(COL),
            P(None, COL),
            P(COL, None),
            P(COL),
            P(COL),
            P(COL, None),
            P(COL),
            P(COL),
            P(COL, None),
            P(COL, None),
            P(COL),
            P(COL, None),
            P(COL),
            P(COL, None),
            P(COL, None),
            P(COL, None),
            P(COL, None),
            P("row", COL, None),
        )
        out_specs = (
            P("row", COL, None),
            P("row", COL, None),
            P(None, ALL),
            P(ALL),
            P(None, ALL),
            P(ALL, None),
            P(ALL),
            P(ALL),
            P(ALL, None),
            P(ALL),
            P(ALL),
            P(ALL, None),
            P(ALL, None),
            P(ALL),
            P(ALL, None),
            P(ALL),
            P(ALL, None),
            P(ALL, None),
            P(ALL, None),
            P(ALL, None),
        )
        return jax.shard_map(
            on_device, mesh=split, in_specs=in_specs, out_specs=out_specs, check_vma=False
        )(*args)

    return run
```

```python
import functools
import math

import jax
import jax.numpy as jnp
import numpy as np
from jax import lax
from jax.experimental import pallas as pl
from jax.experimental.pallas import tpu as pltpu
from jax.sharding import Mesh, PartitionSpec as P

HD = 64
NBAND = 8
MOSTH = 8
HALO = 8
LANES = 256

EPS = 1e-06
THETA = 10000.0
NEG = -1e30
HIGH = lax.Precision.HIGHEST
OFFSETS = ((-1, -1), (-1, 0), (-1, 1), (0, -1), (0, 0), (0, 1), (1, -1), (1, 0), (1, 1))
ALL = ("row", "sub", "tp")
COL = ("sub", "tp")
f32 = jnp.float32
bf16 = jnp.bfloat16


def spread_all(value, axes):
    count = lax.axis_size(axes)
    return lax.all_to_all(
        jnp.broadcast_to(value[None], (count,) + value.shape), axes, 0, 0, tiled=True
    )


def swap(value, axes):
    return lax.all_to_all(value, axes, 0, 0, tiled=True)


def nothing(*others):
    return sum(other[(0,) * other.ndim].astype(f32) * 0.0 for other in others)


def after(value, *others):
    return value + nothing(*others).astype(value.dtype)


def waits_for(kernel, at, count):
    def run(*refs):
        return kernel(*refs[:at], *refs[at + count :])

    return run


def cost(microseconds):
    return pl.CostEstimate(
        flops=int(microseconds * 1e9), bytes_accessed=int(microseconds * 3e6), transcendentals=0
    )


ANYWHERE = pl.BlockSpec(memory_space=pl.ANY)


def pairwise(value, flip):
    return lax.ppermute(value, "row", [(i, i ^ flip) for i in range(4)])


def row_gather(value):
    if lax.axis_size("row") != 4:
        return lax.all_gather(value, "row", axis=0)
    row = lax.axis_index("row")
    chip, core = row // 2, row % 2
    other = pairwise(value, 2)
    pair = jnp.stack([jnp.where(chip == 0, value, other), jnp.where(chip == 0, other, value)])
    far = pairwise(pair, 1)
    both = jnp.stack([jnp.where(core == 0, pair, far), jnp.where(core == 0, far, pair)], axis=1)
    return both.reshape((4,) + value.shape)


def row_scatter(value):
    count = lax.axis_size("row")
    if count != 4:
        return lax.psum_scatter(value, "row", scatter_dimension=0, tiled=True)
    row = lax.axis_index("row")
    chip, core = row // 2, row % 2
    parts = value.astype(bf16).reshape((2, 2, value.shape[0] // 4) + value.shape[1:])

    def pick(array, which, axis):
        return lax.dynamic_index_in_dim(array, which, axis, keepdims=False)

    near = pairwise(pick(parts, 1 - core, 1), 1)
    kept = (pick(parts, core, 1).astype(f32) + near.astype(f32)).astype(bf16)
    far = pairwise(pick(kept, 1 - chip, 0), 2)
    return pick(kept, chip, 0).astype(f32) + far.astype(f32)


def row_sums(value, rows):
    if lax.axis_size("row") != 4:
        return row_scatter(value), lax.psum(rows.astype(bf16), "row").astype(f32)
    row = lax.axis_index("row")
    chip, core = row // 2, row % 2
    size = value.shape[0] // 4
    parts = value.astype(bf16).reshape((2, 2, size) + value.shape[1:])
    rows = rows.astype(bf16)

    def pick(array, which, axis):
        return lax.dynamic_index_in_dim(array, which, axis, keepdims=False)

    sent = pick(parts, 1 - core, 1).reshape((2 * size,) + value.shape[1:])
    near = pairwise(jnp.concatenate([sent, rows], axis=0), 1).astype(f32)
    kept = pick(parts, core, 1).astype(f32) + near[: 2 * size].reshape((2, size) + value.shape[1:])
    kept = kept.astype(bf16)
    rows = (rows.astype(f32) + near[2 * size :]).astype(bf16)
    far = pairwise(jnp.concatenate([pick(kept, 1 - chip, 0), rows], axis=0), 2).astype(f32)
    return pick(kept, chip, 0).astype(f32) + far[:size], rows.astype(f32) + far[size:]


def ring_of(count):
    return list(range(0, count, 2)) + list(range(count - 1, 0, -2))


def look_up(table, index):
    ids = jnp.arange(len(table))
    return jnp.sum(jnp.where(ids == index, jnp.asarray(table, jnp.int32), 0)).astype(jnp.int32)


def ring_steps(axis):
    count = lax.axis_size(axis)
    ring = ring_of(count)
    place = look_up([ring.index(i) for i in range(count)], lax.axis_index(axis))

    def member(step):
        return look_up(ring, lax.rem(place + (step + count), count))

    def onward(value):
        return lax.ppermute(value, axis, [(ring[i], ring[(i + 1) % count]) for i in range(count)])

    def back(value):
        return lax.ppermute(value, axis, [(ring[(i + 1) % count], ring[i]) for i in range(count)])

    return member, onward, back


def ring_gather(value, axis):
    count = lax.axis_size(axis)
    member, onward, back = ring_steps(axis)
    rows = value.shape[0]
    pieces, starts = [value], [member(0) * rows]
    right = left = value
    for step in range(1, count // 2):
        right, left = onward(right), back(left)
        pieces += [right, left]
        starts += [member(-step) * rows, member(step) * rows]
    half = rows // 2
    far = member(count // 2) * rows
    pieces += [onward(right[:half]), back(left[half:])]
    starts += [far, far + half]
    return pieces, jnp.stack(starts)


def ring_scatter(block, axis, beside):
    count = lax.axis_size(axis)
    member, onward, back = ring_steps(axis)
    beside, done = list(beside), []

    def step_on(right, left):
        held = (right, left)
        right, left = onward(right.astype(bf16)), back(left.astype(bf16))
        if beside:
            done.append(beside.pop(0)(held))
            right, left = after(right.astype(f32), *done[-1]), left.astype(f32)
        return right.astype(f32), left.astype(f32)

    far = block(member(count // 2)).astype(bf16)
    half = far.shape[0] // 2
    far_right, far_left = onward(far[:half]), back(far[half:])
    right = block(member(count // 2 - 1))
    left = block(member(1 - count // 2))
    right = jnp.concatenate([right[:half] + far_right.astype(f32), right[half:]], axis=0)
    left = jnp.concatenate([left[:half], left[half:] + far_left.astype(f32)], axis=0)
    for step in range(count // 2 - 2, 0, -1):
        right, left = step_on(right, left)
        right = right + block(member(step))
        left = left + block(member(-step))
    own = block(member(0))
    right, left = step_on(right, left)
    return right + left + own, done


def pack_kernel(copies, *refs):
    for source, source_lead, source_at, target, target_lead, target_at, size in copies:
        taken = slice(source_at, source_at + size)
        given = slice(target_at, target_at + size)
        value = refs[source][:, taken] if source_lead is None else refs[source][source_lead, :, taken]
        value = value.astype(refs[target].dtype)
        if target_lead is None:
            refs[target][:, given] = value
        else:
            refs[target][target_lead, :, given] = value


def pack(copies, out_shapes, *sources):
    return pl.pallas_call(
        functools.partial(pack_kernel, copies),
        out_shape=out_shapes,
        compiler_params=pltpu.CompilerParams(vmem_limit_bytes=48 * 2**20),
        name="pack",
        cost_estimate=cost(1),
    )(*sources)


def dot(left, right, left_dim, right_dim, precision=None):
    return lax.dot_general(
        left,
        right,
        (((left_dim,), (right_dim,)), ((), ())),
        precision=precision,
        preferred_element_type=f32,
    )


def shift(cells, axis, up):
    count = lax.axis_size(axis)
    pairs = [(i, i + 1) if up else (i + 1, i) for i in range(count - 1)]
    return lax.ppermute(cells, axis, pairs)


def silu_slope(values):
    sigmoid = jax.nn.sigmoid(values)
    return sigmoid * (1.0 + values * (1.0 - sigmoid))


def gather_cells(padded, row_count, col_count):
    return jnp.concatenate(
        [
            padded[1 + row_off : 1 + row_off + row_count, 1 + col_off : 1 + col_off + col_count]
            for row_off, col_off in OFFSETS
        ],
        axis=-1,
    )


def spread_cells(padded, row_count, col_count, channels):
    summed = jnp.zeros((row_count, col_count, channels), f32)
    for offset_index, (row_off, col_off) in enumerate(OFFSETS):
        summed = summed + padded[
            1 - row_off : 1 - row_off + row_count,
            1 - col_off : 1 - col_off + col_count,
            offset_index * channels : (offset_index + 1) * channels,
        ].astype(f32)
    return summed


def row_items(heights, band_ids, row_count):
    count = heights.shape[0]
    below = jnp.arange(count)[:, None] >= jnp.arange(count)[None, :]
    item_ends = jnp.sum(jnp.where(below, heights[None, :], 0), axis=1)
    row_ids = jnp.arange(row_count, dtype=jnp.int32)
    item_of_row = jnp.sum((item_ends[None, :] <= row_ids[:, None]).astype(jnp.int32), axis=1)
    picked = item_of_row[:, None] == jnp.arange(count, dtype=jnp.int32)[None, :]
    item_top = jnp.sum(jnp.where(picked, (item_ends - heights)[None, :], 0), axis=1)
    row_band = jnp.sum(jnp.where(picked, band_ids[None, :], 0), axis=1)
    band_onehot = (row_band[:, None] == jnp.arange(NBAND, dtype=jnp.int32)[None, :]).astype(f32)
    return (item_of_row, row_ids - item_top, band_onehot)


def tn(left, right):
    return dot(left, right, 0, 0)


def nt(left, right):
    return dot(left, right, 1, 1)


def nn(left, right):
    return dot(left, right, 1, 0)


def masked_scores(key_block, query_block, bias):
    return tn(key_block, query_block) + bias


def block_bias(items_ref, item_query, chunk, key_rows, width):
    rows = []
    for key_row in range(key_rows):
        item = items_ref[chunk * key_rows + key_row]
        rows.append(
            jnp.broadcast_to(jnp.where(item_query == item, 0.0, NEG), (width, item_query.shape[1]))
        )
    return rows[0] if len(rows) == 1 else jnp.concatenate(rows, axis=0)


def lay_out(block, near_ref, *parts):
    @pl.when(block == 0)
    def _():
        at = 0
        for part in parts:
            near_ref[:, at : at + part.shape[1]] = part[...]
            at += part.shape[1]


def attend_kernel(
    heads,
    key_rows,
    key_width,
    items_ref,
    low_ref,
    high_ref,
    item_query_ref,
    query_ref,
    above_ref,
    both_ref,
    below_ref,
    cross_ref,
    caption_key_ref,
    caption_value_ref,
    gate_ref,
    mixed_ref,
    self_ref,
    crossed_ref,
    stats_ref,
    total_ref,
    near_ref,
):
    block = pl.program_id(0)
    head_width = heads * HD
    lay_out(block, near_ref, above_ref, both_ref, below_ref)
    item_query = item_query_ref[0:1, :]
    self_ref[...] = jnp.zeros_like(self_ref)
    total_ref[...] = jnp.zeros_like(total_ref)

    def chunk_step(chunk, carry):
        lanes = pl.ds(pl.multiple_of(chunk * LANES, LANES), LANES)
        bias = block_bias(items_ref, item_query, chunk, key_rows, key_width)
        for head in range(heads):
            part = slice(head * HD, (head + 1) * HD)
            value_part = slice(head_width + head * HD, head_width + (head + 1) * HD)
            scores = masked_scores(near_ref[part, lanes], query_ref[part, :], bias)
            weights = jnp.exp(scores)
            total_ref[head : head + 1, :] += jnp.sum(weights, axis=0, keepdims=True)
            self_ref[part, :] += nn(near_ref[value_part, lanes], weights.astype(bf16))
        return carry

    lax.fori_loop(low_ref[block], high_ref[block], chunk_step, 0)
    stats_ref[...] = jnp.zeros_like(stats_ref)
    for head in range(heads):
        part = slice(head * HD, (head + 1) * HD)
        total = total_ref[head : head + 1, :]
        attended = self_ref[part, :] / total
        self_ref[part, :] = attended
        stats_ref[head : head + 1, :] = jnp.log(total)
        scores = tn(caption_key_ref[part, :], cross_ref[part, :])
        best = jnp.max(scores, axis=0, keepdims=True)
        weights = jnp.exp(scores - best)
        total = jnp.sum(weights, axis=0, keepdims=True)
        crossed = nn(caption_value_ref[part, :], (weights / total).astype(bf16))
        crossed_ref[part, :] = crossed
        stats_ref[heads + head : heads + head + 1, :] = best + jnp.log(total)
        mixed_ref[part, :] = (attended + gate_ref[part, 0:1] * crossed).astype(bf16)


def cross_back_kernel(
    heads,
    cross_ref,
    caption_key_ref,
    caption_value_ref,
    gate_ref,
    grad_ref,
    crossed_ref,
    stats_ref,
    grad_cross_ref,
    grad_key_ref,
    grad_value_ref,
    grad_gate_ref,
):
    @pl.when(pl.program_id(0) == 0)
    def _():
        grad_key_ref[...] = jnp.zeros_like(grad_key_ref)
        grad_value_ref[...] = jnp.zeros_like(grad_value_ref)
        grad_gate_ref[...] = jnp.zeros_like(grad_gate_ref)

    for head in range(heads):
        part = slice(head * HD, (head + 1) * HD)
        gate = gate_ref[part, 0:1]
        grad_wide = grad_ref[part, :].astype(f32)
        grad_crossed = (gate * grad_wide).astype(bf16)
        grad_gate_ref[part, 0:1] += jnp.sum(
            grad_wide * crossed_ref[part, :], axis=1, keepdims=True
        ) * (1.0 - gate * gate)
        scores = tn(caption_key_ref[part, :], cross_ref[part, :])
        weights = jnp.exp(scores - stats_ref[heads + head : heads + head + 1, :])
        grad_weights = tn(caption_value_ref[part, :], grad_crossed)
        delta = jnp.sum(weights * grad_weights, axis=0, keepdims=True)
        grad_scores = (weights * (grad_weights - delta)).astype(bf16)
        grad_cross_ref[part, :] = (
            nn(caption_key_ref[part, :], grad_scores) * (1.0 / math.sqrt(HD))
        ).astype(bf16)
        grad_key_ref[part, :] += nt(cross_ref[part, :], grad_scores)
        grad_value_ref[part, :] += nt(grad_crossed, weights.astype(bf16))


def attend_back_kernel(
    heads,
    key_rows,
    key_width,
    items_ref,
    low_ref,
    high_ref,
    item_query_ref,
    query_ref,
    above_ref,
    both_ref,
    below_ref,
    grad_ref,
    self_ref,
    stats_ref,
    grad_query_ref,
    grad_both_ref,
    delta_ref,
    near_ref,
):
    block = pl.program_id(0)
    head_width = heads * HD
    lay_out(block, near_ref, above_ref, both_ref, below_ref)

    @pl.when(block == 0)
    def _():
        grad_both_ref[...] = jnp.zeros_like(grad_both_ref)

    item_query = item_query_ref[0:1, :]
    grad_query_ref[...] = jnp.zeros_like(grad_query_ref)
    for head in range(heads):
        part = slice(head * HD, (head + 1) * HD)
        delta_ref[head : head + 1, :] = jnp.sum(
            grad_ref[part, :].astype(f32) * self_ref[part, :], axis=0, keepdims=True
        )

    def chunk_step(chunk, carry):
        lanes = pl.ds(pl.multiple_of(chunk * LANES, LANES), LANES)
        bias = block_bias(items_ref, item_query, chunk, key_rows, key_width)
        for head in range(heads):
            part = slice(head * HD, (head + 1) * HD)
            value_part = slice(head_width + head * HD, head_width + (head + 1) * HD)
            key_block = near_ref[part, lanes]
            query_block = query_ref[part, :]
            grad_block = grad_ref[part, :]
            scores = masked_scores(key_block, query_block, bias)
            weights = jnp.exp(scores - stats_ref[head : head + 1, :])
            grad_weights = tn(near_ref[value_part, lanes], grad_block)
            grad_scores = (weights * (grad_weights - delta_ref[head : head + 1, :])).astype(bf16)
            grad_query_ref[part, :] += nn(key_block, grad_scores)
            grad_both_ref[part, lanes] += nt(query_block, grad_scores)
            grad_both_ref[value_part, lanes] += nt(grad_block, weights.astype(bf16))
        return carry

    lax.fori_loop(low_ref[block], high_ref[block], chunk_step, 0)


def turn(values, tables):
    quarter = HD // 4
    first, second, third, fourth = (values[i * quarter : (i + 1) * quarter] for i in range(4))
    cos_rows, sin_rows, cos_cols, sin_cols = (
        tables[i * quarter : (i + 1) * quarter] for i in range(4)
    )
    return jnp.concatenate(
        [
            first * cos_rows - second * sin_rows,
            first * sin_rows + second * cos_rows,
            third * cos_cols - fourth * sin_cols,
            third * sin_cols + fourth * cos_cols,
        ],
        axis=0,
    )


def turn_back(values, tables):
    quarter = HD // 4
    first, second, third, fourth = (values[i * quarter : (i + 1) * quarter] for i in range(4))
    cos_rows, sin_rows, cos_cols, sin_cols = (
        tables[i * quarter : (i + 1) * quarter] for i in range(4)
    )
    return jnp.concatenate(
        [
            first * cos_rows + second * sin_rows,
            second * cos_rows - first * sin_rows,
            third * cos_cols + fourth * sin_cols,
            fourth * cos_cols - third * sin_cols,
        ],
        axis=0,
    )


def mean_inverse(values, axis):
    return lax.rsqrt(jnp.mean(values * values, axis=axis, keepdims=True) + EPS)


def project_kernel(
    heads,
    span,
    near_ref,
    embed_ref,
    vector_ref,
    mod_ref,
    weight_ref,
    table_ref,
    gain_ref,
    embedded_ref,
    normed_ref,
    raw_ref,
    query_ref,
    both_ref,
    cross_ref,
):
    block = pl.program_id(0)
    model = embed_ref.shape[0]
    head_width = heads * HD
    embedded_ref[...] = nt(near_ref[...], embed_ref[...]) + vector_ref[0:1, :]
    for j in range(LANES // span):
        rows = slice(j * span, (j + 1) * span)
        embedded = embedded_ref[rows, :]
        scale = mod_ref[pl.ds(block * (LANES // span) + j, 1), 0:model]
        factor = vector_ref[1:2, :] * (1.0 + scale)
        normed_ref[rows, :] = (embedded * mean_inverse(embedded, -1) * factor).astype(bf16)
    raw = nn(normed_ref[...], weight_ref[...]).astype(bf16).astype(f32).T
    tables = table_ref[...]
    score_scale = 1.0 / math.sqrt(HD)
    raw_ref[...] = raw[0 : 2 * head_width].astype(bf16)
    for head in range(heads):
        part = slice(head * HD, (head + 1) * HD)
        query = raw[part]
        query = turn(query * mean_inverse(query, 0) * gain_ref[part, 0:1], tables)
        query_ref[part, :] = (query.astype(bf16).astype(f32) * score_scale).astype(bf16)
        key = raw[head_width + head * HD : head_width + (head + 1) * HD]
        key = turn(key * mean_inverse(key, 0) * gain_ref[part, 1:2], tables)
        both_ref[part, :] = key.astype(bf16)
    both_ref[head_width:, :] = raw[2 * head_width : 3 * head_width].astype(bf16)
    cross_ref[...] = (raw[3 * head_width :] * score_scale).astype(bf16)


def middle_kernel(
    pieces,
    span,
    own_ref,
    place_ref,
    *refs,
):
    mixed_refs, refs = refs[:pieces], refs[pieces:]
    (
        embedded_ref,
        patch_ref,
        vector_ref,
        mod_ref,
        output_ref,
        gu_ref,
        down_ref,
        unpatch_ref,
        mixed_ref,
        residual_ref,
        inner_ref,
        hidden_ref,
        grad_feed_ref,
        grad_gu_ref,
        part_residual_ref,
        part_branch_ref,
        grad_mixed_ref,
        scale_rows_ref,
        gate_rows_ref,
        gain_ref,
        branch_ref,
        grad_inner_ref,
    ) = refs
    block = pl.program_id(0)
    row_count = LANES // span
    model = embedded_ref.shape[1]
    groups = output_ref.shape[0]
    group = model // groups
    ff_mine = down_ref.shape[0]

    @pl.when(block == 0)
    def _():
        gain_ref[...] = jnp.zeros_like(gain_ref)

    for i, ref in enumerate(mixed_refs):
        size = ref.shape[0]
        mixed_ref[pl.ds(pl.multiple_of(place_ref[i], 32), size), :] = ref[...]
    for g in range(groups):
        branch_ref[:, g * group : (g + 1) * group] = tn(mixed_ref[...], output_ref[g])
    ff_gain = vector_ref[2:3, :]

    def mods(j, which):
        return mod_ref[
            pl.ds(block * row_count + j, 1), which * model : (which + 1) * model
        ]

    for j in range(row_count):
        rows = slice(j * span, (j + 1) * span)
        residual = embedded_ref[rows, :] + jnp.tanh(mods(j, 1)) * branch_ref[rows, :]
        residual_ref[rows, :] = residual
        factor = ff_gain * (1.0 + mods(j, 2))
        inner_ref[rows, :] = (residual * mean_inverse(residual, -1) * factor).astype(bf16)
    inner = inner_ref[...]
    ff_groups = gu_ref.shape[0]
    ff_group = 2 * ff_mine // ff_groups
    half = ff_groups // 2
    grad_inner_ref[...] = nt(patch_ref[...], unpatch_ref[...])
    for j in range(row_count):
        rows = slice(j * span, (j + 1) * span)
        grad_feed_ref[rows, :] = (jnp.tanh(mods(j, 3)) * grad_inner_ref[rows, :]).astype(bf16)
    grad_hidden = nt(grad_feed_ref[...], down_ref[...])
    for g in range(half):
        gate = nn(inner, gu_ref[g])
        upward = nn(inner, gu_ref[half + g])
        sigmoid = jax.nn.sigmoid(gate)
        silu = gate * sigmoid
        cols = slice(g * ff_group, (g + 1) * ff_group)
        hidden_ref[:, cols] = (silu * upward).astype(bf16)
        grad = grad_hidden[:, cols]
        grad_gu_ref[:, cols] = (
            grad * upward * (sigmoid * (1.0 + gate * (1.0 - sigmoid)))
        ).astype(bf16)
        grad_gu_ref[:, ff_mine + g * ff_group : ff_mine + (g + 1) * ff_group] = (
            grad * silu
        ).astype(bf16)
    own_column = lax.broadcasted_iota(jnp.int32, (span, 1), 0)
    mine = (own_column >= own_ref[0]) & (own_column < own_ref[1])
    for j in range(row_count):
        rows = slice(j * span, (j + 1) * span)
        part_residual_ref[rows, :] = jnp.where(mine, grad_inner_ref[rows, :], 0.0)
    total = nt(grad_gu_ref[:, 0:ff_group], gu_ref[0])
    for g in range(1, ff_groups):
        total = total + nt(grad_gu_ref[:, g * ff_group : (g + 1) * ff_group], gu_ref[g])
    grad_inner_ref[...] = total
    for j in range(row_count):
        rows = slice(j * span, (j + 1) * span)
        tanh_one = jnp.tanh(mods(j, 1))
        second_scale = mods(j, 2)
        residual = residual_ref[rows, :]
        inverse = mean_inverse(residual, -1)
        unit = residual * inverse
        grad_inner = grad_inner_ref[rows, :]
        summed = jnp.sum(grad_inner * unit, axis=0, keepdims=True)
        scale_rows_ref[pl.ds(block * row_count + j, 1), :] = summed * ff_gain
        gain_ref[0:1, :] += summed * (1.0 + second_scale)
        grad_unit = grad_inner * (ff_gain * (1.0 + second_scale))
        part = part_residual_ref[rows, :] + inverse * (
            grad_unit - unit * jnp.mean(grad_unit * unit, axis=-1, keepdims=True)
        )
        part_residual_ref[rows, :] = part
        part_branch_ref[rows, :] = (tanh_one * part).astype(bf16)
        gate_rows_ref[pl.ds(block * row_count + j, 1), :] = jnp.sum(
            part * branch_ref[rows, :], axis=0, keepdims=True
        ) * (1.0 - tanh_one * tanh_one)
    total = nt(output_ref[0], part_branch_ref[:, 0:group])
    for g in range(1, groups):
        total = total + nt(output_ref[g], part_branch_ref[:, g * group : (g + 1) * group])
    grad_mixed_ref[...] = total.astype(bf16)


def result_kernel(
    span,
    own_ref,
    hidden_ref,
    residual_ref,
    patch_ref,
    mod_ref,
    down_ref,
    unpatch_ref,
    cells_ref,
    grad_unpatch_ref,
    gate_rows_ref,
    feed_ref,
    grad_ref,
    result_ref,
):
    block = pl.program_id(0)
    row_count = LANES // span
    model = residual_ref.shape[1]

    @pl.when(block == 0)
    def _():
        grad_unpatch_ref[...] = jnp.zeros_like(grad_unpatch_ref)

    feed_ref[...] = nn(hidden_ref[...], down_ref[...])
    grad_ref[...] = nt(patch_ref[...], unpatch_ref[...])
    own_column = lax.broadcasted_iota(jnp.int32, (span, 1), 0)
    mine = (own_column >= own_ref[0]) & (own_column < own_ref[1])
    for j in range(row_count):
        rows = slice(j * span, (j + 1) * span)
        tanh_two = jnp.tanh(mod_ref[pl.ds(block * row_count + j, 1), 3 * model : 4 * model])
        feed = feed_ref[rows, :]
        result_ref[rows, :] = (
            jnp.where(mine, residual_ref[rows, :], 0.0) + tanh_two * feed
        ).astype(bf16)
        gate_rows_ref[pl.ds(block * row_count + j, 1), :] = jnp.sum(
            grad_ref[rows, :] * feed, axis=0, keepdims=True
        ) * (1.0 - tanh_two * tanh_two)
    cells_ref[...] = nn(result_ref[...], unpatch_ref[...])
    grad_unpatch_ref[...] += tn(patch_ref[...], result_ref[...])


def finish_kernel(
    heads,
    span,
    grad_query_ref,
    grad_key_ref,
    grad_value_ref,
    grad_cross_ref,
    raw_ref,
    table_ref,
    gain_ref,
    embedded_ref,
    part_residual_ref,
    near_ref,
    vector_ref,
    mod_ref,
    weight_ref,
    embed_ref,
    grad_raw_ref,
    cells_ref,
    grad_embed_ref,
    scale_rows_ref,
    sums_ref,
    head_sums_ref,
    turned_ref,
    grad_normed_ref,
    part_ref,
):
    block = pl.program_id(0)
    row_count = LANES // span
    model = embedded_ref.shape[1]
    head_width = heads * HD
    score_scale = 1.0 / math.sqrt(HD)

    @pl.when(block == 0)
    def _():
        grad_embed_ref[...] = jnp.zeros_like(grad_embed_ref)
        sums_ref[...] = jnp.zeros_like(sums_ref)
        head_sums_ref[...] = jnp.zeros_like(head_sums_ref)

    tables = table_ref[...]
    for which in range(2):
        for head in range(heads):
            part = slice(head * HD, (head + 1) * HD)
            if which == 0:
                grad = (grad_query_ref[part, :] * score_scale).astype(bf16).astype(f32)
            else:
                grad = grad_key_ref[part, :].astype(bf16).astype(f32)
            at = which * head_width + head * HD
            raw = raw_ref[at : at + HD, :].astype(f32)
            grad = turn_back(grad, tables)
            inverse = mean_inverse(raw, 0)
            unit = raw * inverse
            head_sums_ref[part, which : which + 1] += jnp.sum(grad * unit, axis=1, keepdims=True)
            grad = grad * gain_ref[part, which : which + 1]
            turned_ref[at : at + HD, :] = inverse * (
                grad - unit * jnp.mean(grad * unit, axis=0, keepdims=True)
            )
    turned_ref[2 * head_width : 3 * head_width, :] = grad_value_ref[...].astype(f32)
    turned_ref[3 * head_width :, :] = grad_cross_ref[...].astype(f32)
    grad_raw_ref[...] = turned_ref[...].T.astype(bf16)
    grad_normed_ref[...] = nt(grad_raw_ref[...], weight_ref[...])
    gain = vector_ref[1:2, :]
    for j in range(row_count):
        rows = slice(j * span, (j + 1) * span)
        scale = mod_ref[pl.ds(block * row_count + j, 1), 0:model]
        embedded = embedded_ref[rows, :]
        inverse = mean_inverse(embedded, -1)
        unit = embedded * inverse
        grad_normed = grad_normed_ref[rows, :]
        summed = jnp.sum(grad_normed * unit, axis=0, keepdims=True)
        scale_rows_ref[pl.ds(block * row_count + j, 1), :] = summed * gain
        sums_ref[0:1, :] += summed * (1.0 + scale)
        grad_unit = grad_normed * (gain * (1.0 + scale))
        part = part_residual_ref[rows, :] + inverse * (
            grad_unit - unit * jnp.mean(grad_unit * unit, axis=-1, keepdims=True)
        )
        part = part.astype(bf16)
        part_ref[rows, :] = part
        sums_ref[1:2, :] += jnp.sum(part.astype(f32), axis=0, keepdims=True)
    cells_ref[...] = nn(part_ref[...], embed_ref[...])
    grad_embed_ref[...] += tn(near_ref[...], part_ref[...])


def on_device(
    latents,
    captions,
    item_heights,
    item_bands,
    embedding,
    embed_bias,
    band_table,
    adaptive,
    adaptive_bias,
    attention_gain,
    projection,
    query_gain,
    key_gain,
    cross_query,
    caption_weight,
    cross_gate,
    output_weight,
    feedforward_gain,
    gate_weight,
    up_weight,
    down_weight,
    unpatch_weight,
    cotangent,
):
    rows_n, sub_n, tp_n = (lax.axis_size(a) for a in ALL)
    col_n = sub_n * tp_n
    all_n = rows_n * col_n
    row = lax.axis_index("row")
    sub = lax.axis_index("sub")
    tp = lax.axis_index("tp")
    tile_rows, tile_cols, channels = latents.shape
    grid_rows = tile_rows * rows_n
    grid_cols = tile_cols * col_n
    span = tile_cols * tp_n
    tokens = tile_rows * span
    own = tile_rows * tile_cols
    width = embed_bias.shape[0]
    model = width * col_n
    head_width = model // tp_n
    heads = head_width // HD
    owned = model // all_n
    quarter = width // rows_n
    ff = gate_weight.shape[1]
    ff_part = ff // col_n
    ff_mine = ff // tp_n
    text = captions.shape[0]
    patch = 9 * channels

    index = (row * sub_n + sub) * tp_n + tp
    col = sub * tp_n + tp

    def to_peers(piece):
        spread = jnp.broadcast_to(piece[None], (sub_n,) + piece.shape)
        return spread.reshape((col_n,) + piece.shape[1:])

    def share(pieces):
        whole = row_gather(pieces)
        return whole.transpose(1, 0, 2, 3).reshape(model, pieces.shape[2])

    def my_quarter(weight):
        return lax.dynamic_slice_in_dim(weight, row * quarter, quarter, 0)

    copies = []
    for t in range(tp_n):
        for i in range(3):
            copies.append((0, None, i * model + t * head_width, 2, t, i * head_width, head_width))
        copies.append((1, None, t * head_width, 2, t, 3 * head_width, head_width))
    qkvc_piece = pack(
        copies,
        jax.ShapeDtypeStruct((tp_n, quarter, 4 * head_width), bf16),
        my_quarter(projection),
        my_quarter(cross_query),
    )
    tiles = jnp.concatenate([latents, cotangent], axis=-1).reshape(-1, 128)
    tiles_width = -(-tiles.shape[0] // quarter) * 128
    tiles = jnp.pad(tiles, ((0, quarter * tiles_width // 128 - tiles.shape[0]), (0, 0)))
    tiles = tiles.reshape(tiles_width // 128, quarter, 128).transpose(1, 0, 2)
    tiles = jnp.broadcast_to(tiles.reshape(1, quarter, tiles_width), (tp_n, quarter, tiles_width))
    qkvc_pieces = swap(to_peers(jnp.concatenate([qkvc_piece, tiles], axis=2)), COL)
    weight_qkvc = share(qkvc_pieces[:, :, : 4 * head_width])
    tiles = qkvc_pieces[:, :, 4 * head_width :].reshape(col_n, quarter, tiles_width // 128, 128)
    tiles = tiles.transpose(0, 2, 1, 3).reshape(col_n, -1, 128)
    tiles = tiles[:, : own * 2 * channels // 128].reshape(
        col_n, tile_rows, tile_cols, 2 * channels
    )
    grid = tiles.transpose(1, 0, 2, 3).reshape(tile_rows, grid_cols, 2 * channels)
    grid = jnp.concatenate(
        [
            shift(grid[tile_rows - 1 :], "row", True),
            grid,
            shift(grid[:1], "row", False),
        ],
        axis=0,
    )
    grid = jnp.pad(grid, ((0, 0), (1, 1), (0, 0)))
    bordered = lax.dynamic_slice_in_dim(grid, sub * span, span + 2, 1)
    neighbours = gather_cells(bordered[..., 0:channels], tile_rows, span).reshape(tokens, patch)
    patch_grads = gather_cells(bordered[..., channels : 2 * channels], tile_rows, span)
    patch_grads = patch_grads.reshape(tokens, patch)

    mod_width = adaptive.shape[1] // rows_n
    mod_bias = lax.dynamic_update_slice_in_dim(
        jnp.zeros((adaptive.shape[1],), f32), adaptive_bias.astype(f32), col * adaptive_bias.shape[0], 0
    )
    silu_band = jax.nn.silu(band_table.astype(f32))

    def mod_columns(start, count):
        return (
            jnp.dot(
                silu_band,
                lax.dynamic_slice_in_dim(adaptive, start, count, 1).astype(f32),
                precision=HIGH,
            )
            + lax.dynamic_slice_in_dim(mod_bias, start, count, 0)
        ).astype(bf16)

    columns = jnp.concatenate(
        [
            embedding.T,
            embed_bias[:, None],
            attention_gain[:, None],
            feedforward_gain[:, None],
            band_table.T,
            mod_columns(row * mod_width, mod_width).T.reshape(width, -1),
        ],
        axis=1,
    )
    columns_n = columns.shape[1]
    wide = -(-columns_n // 128) * 128
    columns = jnp.pad(columns, ((0, 0), (0, wide - columns_n)))

    def in_quarters(array):
        parts = array.reshape(-1, quarter, array.shape[1])
        return parts.transpose(1, 0, 2).reshape(quarter, -1)

    def from_quarters(array, columns_each):
        parts = array.reshape(array.shape[:-1] + (-1, columns_each))
        parts = jnp.moveaxis(parts, -2, -3)
        return parts.reshape(parts.shape[:-3] + (-1, columns_each))

    text_part = text // rows_n
    cap_part = jnp.dot(
        lax.dynamic_slice(
            captions,
            (row * text_part, col * caption_weight.shape[0]),
            (text_part, caption_weight.shape[0]),
        ),
        caption_weight,
        preferred_element_type=f32,
    )
    copies = []
    for t in range(tp_n):
        for i in range(2):
            copies.append((0, None, i * model + t * head_width, 1, t, i * head_width, head_width))
    cap_part = pack(
        copies, jax.ShapeDtypeStruct((tp_n, text_part, 2 * head_width), bf16), cap_part
    )
    cap_lanes = 2 * head_width // 128
    cap_part = (
        cap_part.reshape(tp_n, text_part, cap_lanes, 128)
        .transpose(0, 2, 1, 3)
        .reshape(tp_n, -1, quarter, 128)
        .transpose(0, 2, 1, 3)
        .reshape(tp_n, quarter, -1)
    )
    same = jnp.concatenate(
        [in_quarters(columns), in_quarters(mod_columns(0, model).reshape(-1, 256))], axis=1
    )
    same_width = same.shape[1]
    sent = jnp.concatenate(
        [jnp.broadcast_to(same[None], (tp_n,) + same.shape), cap_part], axis=2
    )
    got = swap(to_peers(after(sent, qkvc_pieces)), COL)
    columns = from_quarters(got[:, :, : rows_n * wide], wide).reshape(model, wide)
    embedding_t = columns[:, 0:patch]
    at = patch + 3 + NBAND
    vectors = columns[:, patch:at].T.astype(f32)
    full_band = vectors[3:]
    first_scale = jnp.sum(got[:, :, rows_n * wide : same_width].astype(f32), axis=0)
    first_scale = from_quarters(first_scale, 256).reshape(NBAND, model)
    item_of_row, row_place, band_onehot = row_items(item_heights, item_bands, grid_rows)
    tile_onehot = lax.dynamic_slice_in_dim(band_onehot, row * tile_rows, tile_rows, 0)
    first_mods = jnp.dot(
        tile_onehot, after(first_scale, weight_qkvc, neighbours), precision=HIGH
    )
    mod_part = columns[:, at:columns_n].reshape(col_n, width, -1)
    mod_part = jnp.sum(mod_part.astype(f32), axis=0).reshape(mod_width, NBAND).T
    cap_part = jnp.sum(got[:, :, same_width:].astype(f32), axis=0).astype(bf16)

    output_width = model // rows_n
    output_piece = lax.dynamic_slice_in_dim(output_weight, row * output_width, output_width, 1)
    output_piece = lax.all_gather(output_piece, COL, axis=0, tiled=True)
    full_output = lax.all_gather(output_piece, "row", axis=0)

    shared_mods = NBAND * mod_width // quarter
    shared = row_gather(
        jnp.concatenate([in_quarters(mod_part.reshape(-1, 256).astype(bf16)), cap_part], axis=1)
    )
    caption_heads = (
        from_quarters(shared[:, :, shared_mods:], 128)
        .reshape(rows_n, cap_lanes, text_part, 128)
        .transpose(1, 3, 0, 2)
        .reshape(2 * head_width, text)
    )
    caption_keys = caption_heads[:head_width]
    caption_values = caption_heads[head_width:]

    frequency = THETA ** (-jnp.arange(HD // 4, dtype=f32) / (HD // 4))
    tile_place = lax.dynamic_slice_in_dim(row_place, row * tile_rows, tile_rows, 0)
    row_angles = frequency[:, None] * jnp.repeat(tile_place, span).astype(f32)[None, :]
    col_place = sub * span + jnp.tile(jnp.arange(span), tile_rows)
    col_angles = frequency[:, None] * col_place.astype(f32)[None, :]
    tables = jnp.concatenate(
        [jnp.cos(row_angles), jnp.sin(row_angles), jnp.cos(col_angles), jnp.sin(col_angles)],
        axis=0,
    )
    gate_column = jnp.tanh(_mine(cross_gate, tp, sub_n).astype(f32))[:, None]
    gains = jnp.stack(
        [_mine(query_gain, tp, sub_n).astype(f32), _mine(key_gain, tp, sub_n).astype(f32)], axis=1
    )
    blocks = tokens // LANES

    def by_block(count):
        return pl.BlockSpec((count, LANES), lambda i, *_: (0, i))

    def by_rows(count):
        return pl.BlockSpec((LANES, count), lambda i, *_: (i, 0))

    def whole(*shape):
        return pl.BlockSpec(shape, lambda i, *_: (0,) * len(shape))

    def struct(shape, dtype=f32):
        return jax.ShapeDtypeStruct(shape, dtype)

    vmem = pltpu.CompilerParams(vmem_limit_bytes=56 * 2**20)
    embedded, normed, raw, queries, both, raw_cross = pl.pallas_call(
        functools.partial(project_kernel, heads, span),
        grid=(blocks,),
        in_specs=[
            by_rows(patch),
            whole(model, patch),
            whole(*vectors.shape),
            whole(*first_mods.shape),
            whole(model, 4 * head_width),
            by_block(HD),
            whole(head_width, 2),
        ],
        out_specs=[
            by_rows(model),
            by_rows(model),
            by_block(2 * head_width),
            by_block(head_width),
            by_block(2 * head_width),
            by_block(head_width),
        ],
        out_shape=[
            struct((tokens, model)),
            struct((tokens, model), bf16),
            struct((2 * head_width, tokens), bf16),
            struct((head_width, tokens), bf16),
            struct((2 * head_width, tokens), bf16),
            struct((head_width, tokens), bf16),
        ],
        compiler_params=vmem,
        name="project",
        cost_estimate=cost(10),
    )(neighbours, embedding_t, vectors, first_mods, weight_qkvc, tables, gains)
    modulations = (
        from_quarters(shared[:, :, :shared_mods], 256)
        .reshape(rows_n, NBAND, mod_width)
        .transpose(1, 0, 2)
        .reshape(NBAND, adaptive.shape[1])
        .astype(f32)
    )
    mods = jnp.dot(tile_onehot, modulations, precision=HIGH)

    gu_width = 2 * ff_mine // rows_n
    which_half = rows_n // 2
    gu_source = jnp.where(row < which_half, gate_weight, up_weight)
    gu_piece = lax.dynamic_slice_in_dim(
        gu_source.reshape(width, sub_n, tp_n, which_half, ff_part // which_half),
        lax.rem(row, which_half),
        1,
        3,
    )
    gu_piece = gu_piece.transpose(2, 0, 1, 3, 4).reshape(tp_n, width, gu_width)
    unpatch_piece = jnp.pad(my_quarter(unpatch_weight), ((0, 0), (0, gu_width - patch)))
    gu_piece = jnp.concatenate(
        [gu_piece, jnp.broadcast_to(unpatch_piece[None], (tp_n,) + unpatch_piece.shape)], axis=1
    )
    gu_pieces = swap(to_peers(after(gu_piece, queries)), COL)
    down_mine = down_weight
    if sub_n > 1:
        down_mine = lax.all_gather(down_weight, "sub", axis=0, tiled=True)

    if sub_n > 1:
        both = (
            lax.all_gather(both, "sub", axis=0)
            .reshape(sub_n, 2 * head_width, tile_rows, span)
            .transpose(1, 2, 0, 3)
            .reshape(2 * head_width, tile_rows * grid_cols)
        )
    edge = HALO * grid_cols
    middle_cols = both.shape[1]
    above = shift(both[:, middle_cols - edge :], "row", True)
    below = shift(both[:, :edge], "row", False)

    near_rows = tile_rows + 2 * HALO
    key_rows = max(1, LANES // grid_cols)
    key_width = LANES // key_rows
    block_rows = LANES // span
    items_padded = jnp.concatenate(
        [
            jnp.full((HALO,), -1, jnp.int32),
            item_of_row.astype(jnp.int32),
            jnp.full((HALO,), item_heights.shape[0] + 1, jnp.int32),
        ]
    )
    items_near = lax.dynamic_slice_in_dim(items_padded, row * tile_rows, near_rows, 0)
    item_query = jnp.repeat(items_near[HALO : HALO + tile_rows], span)[None, :]
    chunk_items = jnp.repeat(items_near, grid_cols // (key_width)).reshape(-1, key_rows)
    query_items = items_near[HALO : HALO + tile_rows].reshape(blocks, block_rows)
    before = chunk_items[None, :, -1] < query_items[:, None, 0]
    reached = chunk_items[None, :, 0] <= query_items[:, None, -1]
    low = jnp.sum(before.astype(jnp.int32), axis=1)
    high = jnp.sum(reached.astype(jnp.int32), axis=1)
    chunk_items = chunk_items.reshape(-1)
    near = near_rows * grid_cols

    mixed, self_out, crossed, stats = pl.pallas_call(
        waits_for(functools.partial(attend_kernel, heads, key_rows, key_width), 12, 2),
        grid_spec=pltpu.PrefetchScalarGridSpec(
            num_scalar_prefetch=3,
            grid=(blocks,),
            in_specs=[
                by_block(1),
                by_block(head_width),
                whole(2 * head_width, edge),
                whole(2 * head_width, middle_cols),
                whole(2 * head_width, edge),
                by_block(head_width),
                whole(head_width, text),
                whole(head_width, text),
                whole(head_width, 1),
                ANYWHERE,
                ANYWHERE,
            ],
            out_specs=[by_block(head_width), by_block(head_width), by_block(head_width), by_block(8)],
            scratch_shapes=[
                pltpu.VMEM((8, LANES), f32),
                pltpu.VMEM((2 * head_width, near), bf16),
            ],
        ),
        out_shape=[
            jax.ShapeDtypeStruct((head_width, tokens), bf16),
            jax.ShapeDtypeStruct((head_width, tokens), f32),
            jax.ShapeDtypeStruct((head_width, tokens), f32),
            jax.ShapeDtypeStruct((8, tokens), f32),
        ],
        compiler_params=vmem,
        name="attend",
        cost_estimate=cost(14),
    )(
        chunk_items,
        low,
        high,
        item_query,
        queries,
        above,
        both,
        below,
        raw_cross,
        caption_keys,
        caption_values,
        gate_column,
        mods,
        patch_grads,
    )

    weight_gu = lax.all_gather(after(gu_pieces, mixed, full_output), "row", axis=0)
    full_unpatch = weight_gu[:, :, width:, :patch].transpose(1, 0, 2, 3).reshape(model, patch)
    weight_gu = weight_gu[:, :, :width].reshape(rows_n, model, gu_width)
    pieces, starts = ring_gather(mixed, "tp")
    own_span = jnp.stack([tp * tile_cols, (tp + 1) * tile_cols]).astype(jnp.int32)
    (
        mixed_all,
        residual,
        inner,
        hidden,
        grad_feed,
        grad_gu,
        part_residual,
        part_branch,
        grad_mixed,
        rows_second_scale,
        rows_first_gate,
        grad_ff_gain,
    ) = pl.pallas_call(
        functools.partial(middle_kernel, len(pieces), span),
        grid_spec=pltpu.PrefetchScalarGridSpec(
            num_scalar_prefetch=2,
            grid=(blocks,),
            in_specs=[by_block(piece.shape[0]) for piece in pieces]
            + [
                by_rows(model),
                by_rows(patch),
                whole(*vectors.shape),
                whole(*mods.shape),
                whole(*full_output.shape),
                whole(*weight_gu.shape),
                whole(*down_mine.shape),
                whole(model, patch),
            ],
            out_specs=[
                by_block(model),
                by_rows(model),
                by_rows(model),
                by_rows(ff_mine),
                by_rows(model),
                by_rows(2 * ff_mine),
                by_rows(model),
                by_rows(model),
                by_block(model),
                whole(tile_rows, model),
                whole(tile_rows, model),
                whole(8, model),
            ],
            scratch_shapes=[pltpu.VMEM((LANES, model), f32), pltpu.VMEM((LANES, model), f32)],
        ),
        out_shape=[
            struct((model, tokens), bf16),
            struct((tokens, model)),
            struct((tokens, model), bf16),
            struct((tokens, ff_mine), bf16),
            struct((tokens, model), bf16),
            struct((tokens, 2 * ff_mine), bf16),
            struct((tokens, model)),
            struct((tokens, model), bf16),
            struct((model, tokens), bf16),
            struct((tile_rows, model)),
            struct((tile_rows, model)),
            struct((8, model)),
        ],
        compiler_params=vmem,
        name="middle",
        cost_estimate=cost(35),
    )(
        own_span,
        starts,
        *pieces,
        embedded,
        patch_grads,
        vectors,
        mods,
        full_output,
        weight_gu,
        down_mine,
        full_unpatch,
    )

    def result_part(held):
        return pl.pallas_call(
            waits_for(functools.partial(result_kernel, span), 7, 2),
            grid_spec=pltpu.PrefetchScalarGridSpec(
                num_scalar_prefetch=1,
                grid=(blocks,),
                in_specs=[
                    by_rows(ff_mine),
                    by_rows(model),
                    by_rows(patch),
                    whole(*mods.shape),
                    whole(*down_mine.shape),
                    whole(model, patch),
                    ANYWHERE,
                    ANYWHERE,
                ],
                out_specs=[by_rows(patch), whole(patch, model), whole(tile_rows, model)],
                scratch_shapes=[
                    pltpu.VMEM((LANES, model), f32),
                    pltpu.VMEM((LANES, model), f32),
                    pltpu.VMEM((LANES, model), bf16),
                ],
            ),
            out_shape=[struct((tokens, patch)), struct((patch, model)), struct((tile_rows, model))],
            compiler_params=vmem,
            name="result",
        cost_estimate=cost(9),
        )(own_span, hidden, residual, patch_grads, mods, down_mine, full_unpatch, *held)

    def mixed_block(which):
        return lax.dynamic_slice_in_dim(
            grad_mixed, which * head_width, head_width, 0
        ).astype(f32)

    def gu_part(held):
        return (dot(inner, after(grad_gu, *held), 0, 0).astype(bf16),)

    def output_part(held):
        return (dot(mixed_all, after(part_branch, *held), 1, 0).astype(bf16),)

    grad_mixed, done = ring_scatter(mixed_block, "tp", [gu_part, output_part, result_part])
    grad_mixed = grad_mixed.astype(bf16)
    (grad_gu_part,), (grad_output_part,), (cells, grad_unpatch, rows_second_gate) = done

    def cells_out(*parts):
        around = jnp.concatenate(
            [
                spread_cells(
                    jnp.pad(part.reshape(tile_rows, span, patch), ((2, 2), (2, 2), (0, 0))),
                    tile_rows + 2,
                    span + 2,
                    channels,
                )
                for part in parts
            ],
            axis=-1,
        )
        inside = around[:, 1 : span + 1]
        if sub_n > 1:
            from_left = shift(around[:, span + 1 :].astype(bf16), "sub", True).astype(f32)
            from_right = shift(around[:, :1].astype(bf16), "sub", False).astype(f32)
            inside = (
                inside
                + jnp.pad(from_left, ((0, 0), (0, span - 1), (0, 0)))
                + jnp.pad(from_right, ((0, 0), (span - 1, 0), (0, 0)))
            )
        from_above = shift(inside[tile_rows + 1 :].astype(bf16), "row", True).astype(f32)
        from_below = shift(inside[:1].astype(bf16), "row", False).astype(f32)
        inside = (
            inside[1 : tile_rows + 1]
            + jnp.pad(from_above, ((0, tile_rows - 1), (0, 0), (0, 0)))
            + jnp.pad(from_below, ((tile_rows - 1, 0), (0, 0), (0, 0)))
        )
        inside = (
            inside.astype(bf16)
            .reshape(tile_rows, tp_n, tile_cols, -1)
            .transpose(1, 0, 2, 3)
            .reshape(tp_n, -1, 128)
        )
        rows = -(-inside.shape[1] // owned) * owned
        inside = jnp.pad(inside, ((0, 0), (0, rows - inside.shape[1]), (0, 0)))
        return inside.reshape(tp_n, rows // owned, owned, 128).transpose(0, 2, 1, 3).reshape(
            tp_n, owned, -1
        )

    def cells_in(got):
        inside = jnp.sum(got.astype(f32), axis=0).reshape(owned, -1, 128).transpose(1, 0, 2)
        inside = inside.reshape(-1, 128)[: own * 2 * channels // 128]
        return inside.reshape(tile_rows, tile_cols, 2 * channels).astype(bf16)

    def to_chunks(partial):
        summed = lax.psum_scatter(partial.astype(bf16), "row", scatter_dimension=0, tiled=True)
        if sub_n > 1:
            summed = lax.psum_scatter(summed, "sub", scatter_dimension=0, tiled=True)
        return summed

    def scatter_rows(partial):
        if sub_n > 1:
            return to_chunks(partial)
        return row_scatter(partial).astype(bf16)

    def bands(rows):
        return dot(tile_onehot, rows, 0, 0, HIGH)

    first_cells = cells
    grad_gu_sum = to_chunks(grad_gu_part)
    grad_cross, grad_cap_keys, grad_cap_values, grad_gate_part = pl.pallas_call(
        functools.partial(cross_back_kernel, heads),
        grid=(blocks,),
        in_specs=[
            by_block(head_width),
            whole(head_width, text),
            whole(head_width, text),
            whole(head_width, 1),
            by_block(head_width),
            by_block(head_width),
            by_block(8),
        ],
        out_specs=[
            by_block(head_width),
            whole(head_width, text),
            whole(head_width, text),
            whole(head_width, 128),
        ],
        out_shape=[
            jax.ShapeDtypeStruct((head_width, tokens), bf16),
            jax.ShapeDtypeStruct((head_width, text), f32),
            jax.ShapeDtypeStruct((head_width, text), f32),
            jax.ShapeDtypeStruct((head_width, 128), f32),
        ],
        compiler_params=vmem,
        name="cross_back",
        cost_estimate=cost(7),
    )(raw_cross, caption_keys, caption_values, gate_column, grad_mixed, crossed, stats)

    grad_queries, grad_both = pl.pallas_call(
        functools.partial(attend_back_kernel, heads, key_rows, key_width),
        grid_spec=pltpu.PrefetchScalarGridSpec(
            num_scalar_prefetch=3,
            grid=(blocks,),
            in_specs=[
                by_block(1),
                by_block(head_width),
                whole(2 * head_width, edge),
                whole(2 * head_width, middle_cols),
                whole(2 * head_width, edge),
                by_block(head_width),
                by_block(head_width),
                by_block(8),
            ],
            out_specs=[by_block(head_width), whole(2 * head_width, near)],
            scratch_shapes=[
                pltpu.VMEM((8, LANES), f32),
                pltpu.VMEM((2 * head_width, near), bf16),
            ],
        ),
        out_shape=[
            jax.ShapeDtypeStruct((head_width, tokens), f32),
            jax.ShapeDtypeStruct((2 * head_width, near), f32),
        ],
        compiler_params=vmem,
        name="attend_back",
        cost_estimate=cost(14),
    )(chunk_items, low, high, item_query, queries, above, both, below, grad_mixed, self_out, stats)

    moves = []
    for source in range(all_n):
        source_row, rest = divmod(source, col_n)
        moves.append((source, rest * rows_n + source_row))
    output_sum = to_chunks(grad_output_part)
    got_gu = swap(
        jnp.concatenate(
            [
                after(grad_gu_sum, grad_mixed).reshape(tp_n, owned, -1),
                output_sum.reshape(tp_n, owned, model),
            ],
            axis=2,
        ),
        "tp",
    )
    grad_output = jnp.sum(got_gu[:, :, 2 * ff_mine :].astype(f32), axis=0)
    grad_down_part = dot(hidden, after(grad_feed, grad_queries), 0, 0).astype(bf16)
    grad_down = (
        grad_down_part.reshape(sub_n, rows_n, ff // all_n, model)
        .transpose(1, 0, 2, 3)
        .reshape(-1, model)
    )
    copies = []
    for t in range(tp_n):
        for i in range(2):
            for s in range(sub_n):
                copies.append(
                    (0, t, i * ff_mine + s * ff_part, 1 + i, None, (s * tp_n + t) * ff_part, ff_part)
                )
    grad_gate_weight, grad_up_weight = pack(
        copies, [jax.ShapeDtypeStruct((owned, ff), f32)] * 2, got_gu
    )

    grad_down_sum = to_chunks(grad_down)

    def in_lanes(rows, lanes):
        return rows.reshape(rows.shape[0], -1, lanes).transpose(1, 0, 2).reshape(-1, lanes)

    def from_lanes(rows, count):
        return rows.reshape(-1, count, rows.shape[-1]).transpose(1, 0, 2).reshape(count, -1)

    upper = grad_both[:, :edge].astype(bf16)
    lower = grad_both[:, near - edge :].astype(bf16)
    middle = grad_both[:, edge : near - edge]
    from_above = shift(lower, "row", True).astype(f32)
    from_below = shift(upper, "row", False).astype(f32)
    side = middle.shape[1] - edge
    middle = (
        middle
        + jnp.pad(from_above, ((0, 0), (0, side)))
        + jnp.pad(from_below, ((0, 0), (side, 0)))
    )
    if sub_n > 1:
        middle = (
            middle.astype(bf16)
            .reshape(2 * head_width, tile_rows, sub_n, span)
            .transpose(2, 0, 1, 3)
            .reshape(sub_n, 2 * head_width, tokens)
        )
        middle = jnp.sum(swap(middle, "sub").astype(f32), axis=0)
    grad_keys, grad_values = middle[:head_width], middle[head_width:]

    grad_raw, cells, grad_embedding, rows_first_scale, sums, head_sums = pl.pallas_call(
        functools.partial(finish_kernel, heads, span),
        grid=(blocks,),
        in_specs=[
            by_block(head_width),
            by_block(head_width),
            by_block(head_width),
            by_block(head_width),
            by_block(2 * head_width),
            by_block(HD),
            whole(head_width, 2),
            by_rows(model),
            by_rows(model),
            by_rows(patch),
            whole(*vectors.shape),
            whole(*first_mods.shape),
            whole(model, 4 * head_width),
            whole(model, patch),
        ],
        out_specs=[
            by_rows(4 * head_width),
            by_rows(patch),
            whole(patch, model),
            whole(tile_rows, model),
            whole(8, model),
            whole(head_width, 128),
        ],
        out_shape=[
            struct((tokens, 4 * head_width), bf16),
            struct((tokens, patch)),
            struct((patch, model)),
            struct((tile_rows, model)),
            struct((8, model)),
            struct((head_width, 128)),
        ],
        scratch_shapes=[
            pltpu.VMEM((4 * head_width, LANES), f32),
            pltpu.VMEM((LANES, model), f32),
            pltpu.VMEM((LANES, model), bf16),
        ],
        compiler_params=vmem,
        name="finish",
        cost_estimate=cost(13),
    )(
        grad_queries,
        grad_keys,
        grad_values,
        grad_cross,
        raw,
        tables,
        gains,
        embedded,
        part_residual,
        neighbours,
        vectors,
        first_mods,
        weight_qkvc,
        embedding_t,
    )

    grad_qkvc = dot(normed, grad_raw, 0, 0).astype(bf16)

    def in_lanes(rows, lanes):
        return rows.reshape(rows.shape[0], -1, lanes).transpose(1, 0, 2).reshape(-1, lanes)

    def from_lanes(rows, count):
        return rows.reshape(-1, count, rows.shape[-1]).transpose(1, 0, 2).reshape(count, -1)

    grad_cap = row_scatter(
        after(jnp.concatenate([grad_cap_keys, grad_cap_values], axis=0), grad_qkvc)
    ).astype(bf16)
    if sub_n > 1:
        grad_cap = lax.psum_scatter(grad_cap, "sub", scatter_dimension=0, tiled=True)
    cap_rows = 2 * head_width // (rows_n * sub_n)
    grad_cap = lax.all_gather(grad_cap, ALL, axis=0)
    grad_cap = (
        grad_cap.reshape(rows_n, sub_n, tp_n, cap_rows, text)
        .transpose(2, 0, 1, 3, 4)
        .reshape(tp_n, 2, head_width, text)
        .transpose(1, 0, 2, 3)
        .reshape(2 * model, text)
    )


    def place(vectors):
        return lax.dynamic_update_slice_in_dim(
            jnp.zeros((vectors.shape[0], model), f32), vectors, tp * head_width, 1
        )

    head_vectors = jnp.concatenate(
        [head_sums[:, 0:2], grad_gate_part[:, 0:1], jnp.zeros((head_width, 5), f32)], axis=1
    )
    small = jnp.concatenate(
        [
            grad_embedding,
            grad_unpatch,
            sums,
            grad_ff_gain,
            place(head_vectors.T),
        ],
        axis=0,
    ).astype(bf16)
    small_width = small.shape[0]
    small = small.reshape(small_width, rows_n, model // rows_n).transpose(1, 0, 2)
    small = small.reshape(rows_n * small_width, model // rows_n)
    small, all_mods = row_sums(
        small,
        in_lanes(
            jnp.concatenate(
                [
                    bands(after(rows_first_scale, grad_qkvc, got_gu)),
                    bands(rows_first_gate),
                    bands(rows_second_scale),
                    bands(rows_second_gate),
                ],
                axis=0,
            ),
            model // rows_n,
        ),
    )
    all_mods = spread_all(after(all_mods, grad_down_sum).astype(bf16), COL)
    all_mods = from_lanes(jnp.sum(all_mods.astype(f32), axis=0), 4 * NBAND)
    small = small.astype(bf16).T
    if sub_n > 1:
        small = lax.psum_scatter(small, "sub", scatter_dimension=0, tiled=True)
    small = small.reshape(tp_n, owned, small_width)
    qkvc_width = 4 * head_width
    sent = scatter_rows(grad_qkvc).reshape(tp_n, owned, qkvc_width)
    sent = jnp.concatenate([sent, small, cells_out(first_cells, cells)], axis=2)
    got = swap(after(sent, all_mods), "tp")
    small = jnp.sum(got[:, :, qkvc_width : qkvc_width + small_width].astype(f32), axis=0)
    cells_at = qkvc_width + small_width
    both_cells = cells_in(got[:, :, cells_at:])
    prediction, latent_grad = both_cells[..., :channels], both_cells[..., channels:]
    copies = []
    for t in range(tp_n):
        for i in range(3):
            copies.append((0, t, i * head_width, 1, None, i * model + t * head_width, head_width))
        copies.append((0, t, 3 * head_width, 2, None, t * head_width, head_width))
    grad_projection, grad_cross_query = pack(
        copies,
        [
            jax.ShapeDtypeStruct((owned, 3 * model), f32),
            jax.ShapeDtypeStruct((owned, model), f32),
        ],
        got,
    )
    at = 2 * patch
    grad_embedding = small[:, :patch].T
    grad_unpatch = small[:, patch : 2 * patch]
    vectors = small[:, at:].T

    cap_own = captions.shape[1] // all_n
    own_captions = after(
        lax.dynamic_slice_in_dim(captions, index * cap_own, cap_own, 1), all_mods
    )
    grad_caption = dot(own_captions, grad_cap, 0, 1)

    grad_down = lax.ppermute(grad_down_sum, ALL, moves).astype(f32)
    own_band = lax.dynamic_slice_in_dim(full_band, index * owned, owned, 1)
    own_silu = jax.nn.silu(own_band)
    grad_adaptive = jnp.concatenate(
        [dot(own_silu, all_mods[i * NBAND : (i + 1) * NBAND], 0, 0, HIGH) for i in range(4)], axis=1
    )
    bias_own = 4 * owned
    totals = jnp.sum(all_mods.reshape(4, NBAND, model), axis=1).reshape(-1)
    grad_adaptive_bias = lax.dynamic_slice_in_dim(totals, index * bias_own, bias_own, 0)
    local_rows = my_quarter(adaptive)
    local_band = lax.dynamic_slice_in_dim(band_table, row * quarter, quarter, 1).astype(f32)
    grad_band = sum(
        dot(
            all_mods[i * NBAND : (i + 1) * NBAND],
            local_rows[:, i * model : (i + 1) * model].astype(f32),
            1,
            1,
            HIGH,
        )
        for i in range(4)
    ) * silu_slope(local_band)
    grad_band = lax.ppermute(grad_band, ALL, moves)

    return (
        prediction,
        latent_grad,
        grad_embedding,
        vectors[1],
        grad_band,
        grad_adaptive,
        grad_adaptive_bias,
        vectors[0],
        grad_projection,
        vectors[16],
        vectors[17],
        grad_cross_query,
        grad_caption,
        vectors[18],
        grad_output,
        vectors[8],
        grad_gate_weight,
        grad_up_weight,
        grad_down,
        grad_unpatch,
    )


def _mine(vector, tp, sub_n):
    if sub_n == 1:
        return vector
    size = vector.shape[0] * sub_n
    whole = lax.all_gather(vector, COL, axis=0, tiled=True)
    return lax.dynamic_slice_in_dim(whole, tp * size, size, 0)


def solution(mesh):
    rows_n, col_n = mesh.shape["row"], mesh.shape["col"]

    def run(*args):
        heads = args[5].shape[0] // HD
        tp_n = math.gcd(heads, col_n)
        split = Mesh(mesh.devices.reshape(rows_n, col_n // tp_n, tp_n), ALL)
        in_specs = (
            P("row", COL, None),
            P(),
            P(),
            P(),
            P(None, COL),
            P(COL),
            P(None, COL),
            P(COL, None),
            P(COL),
            P(COL),
            P(COL, None),
            P(COL),
            P(COL),
            P(COL, None),
            P(COL, None),
            P(COL),
            P(COL, None),
            P(COL),
            P(COL, None),
            P(COL, None),
            P(COL, None),
            P(COL, None),
            P("row", COL, None),
        )
        out_specs = (
            P("row", COL, None),
            P("row", COL, None),
            P(None, ALL),
            P(ALL),
            P(None, ALL),
            P(ALL, None),
            P(ALL),
            P(ALL),
            P(ALL, None),
            P(ALL),
            P(ALL),
            P(ALL, None),
            P(ALL, None),
            P(ALL),
            P(ALL, None),
            P(ALL),
            P(ALL, None),
            P(ALL, None),
            P(ALL, None),
            P(ALL, None),
        )
        return jax.shard_map(
            on_device, mesh=split, in_specs=in_specs, out_specs=out_specs, check_vma=False
        )(*args)

    return run
```

```python
import functools
import math

import jax
import jax.numpy as jnp
import numpy as np
from jax import lax
from jax.experimental import pallas as pl
from jax.experimental.pallas import tpu as pltpu
from jax.sharding import Mesh, PartitionSpec as P

HD = 64
NBAND = 8
MOSTH = 8
HALO = 8
LANES = 256

EPS = 1e-06
THETA = 10000.0
NEG = -1e30
HIGH = lax.Precision.HIGHEST
OFFSETS = ((-1, -1), (-1, 0), (-1, 1), (0, -1), (0, 0), (0, 1), (1, -1), (1, 0), (1, 1))
ALL = ("row", "sub", "tp")
COL = ("sub", "tp")
f32 = jnp.float32
bf16 = jnp.bfloat16


def spread_all(value, axes):
    count = lax.axis_size(axes)
    return lax.all_to_all(
        jnp.broadcast_to(value[None], (count,) + value.shape), axes, 0, 0, tiled=True
    )


def swap(value, axes):
    return lax.all_to_all(value, axes, 0, 0, tiled=True)


def nothing(*others):
    return sum(other[(0,) * other.ndim].astype(f32) * 0.0 for other in others)


def after(value, *others):
    return value + nothing(*others).astype(value.dtype)


def waits_for(kernel, at, count):
    def run(*refs):
        return kernel(*refs[:at], *refs[at + count :])

    return run


def cost(microseconds):
    return pl.CostEstimate(
        flops=int(microseconds * 1e9), bytes_accessed=int(microseconds * 3e6), transcendentals=0
    )


ANYWHERE = pl.BlockSpec(memory_space=pl.ANY)


def pairwise(value, flip):
    return lax.ppermute(value, "row", [(i, i ^ flip) for i in range(4)])


def row_gather(value):
    if lax.axis_size("row") != 4:
        return lax.all_gather(value, "row", axis=0)
    row = lax.axis_index("row")
    chip, core = row // 2, row % 2
    other = pairwise(value, 2)
    pair = jnp.stack([jnp.where(chip == 0, value, other), jnp.where(chip == 0, other, value)])
    far = pairwise(pair, 1)
    both = jnp.stack([jnp.where(core == 0, pair, far), jnp.where(core == 0, far, pair)], axis=1)
    return both.reshape((4,) + value.shape)


def row_scatter(value):
    count = lax.axis_size("row")
    if count != 4:
        return lax.psum_scatter(value, "row", scatter_dimension=0, tiled=True)
    row = lax.axis_index("row")
    chip, core = row // 2, row % 2
    parts = value.astype(bf16).reshape((2, 2, value.shape[0] // 4) + value.shape[1:])

    def pick(array, which, axis):
        return lax.dynamic_index_in_dim(array, which, axis, keepdims=False)

    near = pairwise(pick(parts, 1 - core, 1), 1)
    kept = (pick(parts, core, 1).astype(f32) + near.astype(f32)).astype(bf16)
    far = pairwise(pick(kept, 1 - chip, 0), 2)
    return pick(kept, chip, 0).astype(f32) + far.astype(f32)


def ring_of(count):
    return list(range(0, count, 2)) + list(range(count - 1, 0, -2))


def look_up(table, index):
    ids = jnp.arange(len(table))
    return jnp.sum(jnp.where(ids == index, jnp.asarray(table, jnp.int32), 0)).astype(jnp.int32)


def ring_steps(axis):
    count = lax.axis_size(axis)
    ring = ring_of(count)
    place = look_up([ring.index(i) for i in range(count)], lax.axis_index(axis))

    def member(step):
        return look_up(ring, lax.rem(place + (step + count), count))

    def onward(value):
        return lax.ppermute(value, axis, [(ring[i], ring[(i + 1) % count]) for i in range(count)])

    def back(value):
        return lax.ppermute(value, axis, [(ring[(i + 1) % count], ring[i]) for i in range(count)])

    return member, onward, back


def ring_gather(value, axis):
    count = lax.axis_size(axis)
    member, onward, back = ring_steps(axis)
    rows = value.shape[0]
    pieces, starts = [value], [member(0) * rows]
    right = left = value
    for step in range(1, count // 2):
        right, left = onward(right), back(left)
        pieces += [right, left]
        starts += [member(-step) * rows, member(step) * rows]
    half = rows // 2
    far = member(count // 2) * rows
    pieces += [onward(right[:half]), back(left[half:])]
    starts += [far, far + half]
    return pieces, jnp.stack(starts)


def ring_scatter(block, axis, beside):
    count = lax.axis_size(axis)
    member, onward, back = ring_steps(axis)
    beside, done = list(beside), []

    def step_on(right, left):
        held = (right, left)
        right, left = onward(right.astype(bf16)), back(left.astype(bf16))
        if beside:
            done.append(beside.pop(0)(held))
            right, left = after(right.astype(f32), *done[-1]), left.astype(f32)
        return right.astype(f32), left.astype(f32)

    far = block(member(count // 2)).astype(bf16)
    half = far.shape[0] // 2
    far_right, far_left = onward(far[:half]), back(far[half:])
    right = block(member(count // 2 - 1))
    left = block(member(1 - count // 2))
    right = jnp.concatenate([right[:half] + far_right.astype(f32), right[half:]], axis=0)
    left = jnp.concatenate([left[:half], left[half:] + far_left.astype(f32)], axis=0)
    for step in range(count // 2 - 2, 0, -1):
        right, left = step_on(right, left)
        right = right + block(member(step))
        left = left + block(member(-step))
    own = block(member(0))
    right, left = step_on(right, left)
    return right + left + own, done


def pack_kernel(copies, *refs):
    for source, source_lead, source_at, target, target_lead, target_at, size in copies:
        taken = slice(source_at, source_at + size)
        given = slice(target_at, target_at + size)
        value = refs[source][:, taken] if source_lead is None else refs[source][source_lead, :, taken]
        value = value.astype(refs[target].dtype)
        if target_lead is None:
            refs[target][:, given] = value
        else:
            refs[target][target_lead, :, given] = value


def pack(copies, out_shapes, *sources):
    return pl.pallas_call(
        functools.partial(pack_kernel, copies),
        out_shape=out_shapes,
        compiler_params=pltpu.CompilerParams(vmem_limit_bytes=48 * 2**20),
        name="pack",
        cost_estimate=cost(1),
    )(*sources)


def dot(left, right, left_dim, right_dim, precision=None):
    return lax.dot_general(
        left,
        right,
        (((left_dim,), (right_dim,)), ((), ())),
        precision=precision,
        preferred_element_type=f32,
    )


def shift(cells, axis, up):
    count = lax.axis_size(axis)
    pairs = [(i, i + 1) if up else (i + 1, i) for i in range(count - 1)]
    return lax.ppermute(cells, axis, pairs)


def silu_slope(values):
    sigmoid = jax.nn.sigmoid(values)
    return sigmoid * (1.0 + values * (1.0 - sigmoid))


def gather_cells(padded, row_count, col_count):
    return jnp.concatenate(
        [
            padded[1 + row_off : 1 + row_off + row_count, 1 + col_off : 1 + col_off + col_count]
            for row_off, col_off in OFFSETS
        ],
        axis=-1,
    )


def spread_cells(padded, row_count, col_count, channels):
    summed = jnp.zeros((row_count, col_count, channels), f32)
    for offset_index, (row_off, col_off) in enumerate(OFFSETS):
        summed = summed + padded[
            1 - row_off : 1 - row_off + row_count,
            1 - col_off : 1 - col_off + col_count,
            offset_index * channels : (offset_index + 1) * channels,
        ].astype(f32)
    return summed


def row_items(heights, band_ids, row_count):
    count = heights.shape[0]
    below = jnp.arange(count)[:, None] >= jnp.arange(count)[None, :]
    item_ends = jnp.sum(jnp.where(below, heights[None, :], 0), axis=1)
    row_ids = jnp.arange(row_count, dtype=jnp.int32)
    item_of_row = jnp.sum((item_ends[None, :] <= row_ids[:, None]).astype(jnp.int32), axis=1)
    picked = item_of_row[:, None] == jnp.arange(count, dtype=jnp.int32)[None, :]
    item_top = jnp.sum(jnp.where(picked, (item_ends - heights)[None, :], 0), axis=1)
    row_band = jnp.sum(jnp.where(picked, band_ids[None, :], 0), axis=1)
    band_onehot = (row_band[:, None] == jnp.arange(NBAND, dtype=jnp.int32)[None, :]).astype(f32)
    return (item_of_row, row_ids - item_top, band_onehot)


def tn(left, right):
    return dot(left, right, 0, 0)


def nt(left, right):
    return dot(left, right, 1, 1)


def nn(left, right):
    return dot(left, right, 1, 0)


def masked_scores(key_block, query_block, bias):
    return tn(key_block, query_block) + bias


def block_bias(items_ref, item_query, chunk, key_rows, width):
    rows = []
    for key_row in range(key_rows):
        item = items_ref[chunk * key_rows + key_row]
        rows.append(
            jnp.broadcast_to(jnp.where(item_query == item, 0.0, NEG), (width, item_query.shape[1]))
        )
    return rows[0] if len(rows) == 1 else jnp.concatenate(rows, axis=0)


def lay_out(block, near_ref, *parts):
    @pl.when(block == 0)
    def _():
        at = 0
        for part in parts:
            near_ref[:, at : at + part.shape[1]] = part[...]
            at += part.shape[1]


def attend_kernel(
    heads,
    key_rows,
    key_width,
    items_ref,
    low_ref,
    high_ref,
    item_query_ref,
    query_ref,
    above_ref,
    both_ref,
    below_ref,
    cross_ref,
    caption_key_ref,
    caption_value_ref,
    gate_ref,
    mixed_ref,
    self_ref,
    crossed_ref,
    stats_ref,
    total_ref,
    near_ref,
):
    block = pl.program_id(0)
    head_width = heads * HD
    lay_out(block, near_ref, above_ref, both_ref, below_ref)
    item_query = item_query_ref[0:1, :]
    self_ref[...] = jnp.zeros_like(self_ref)
    total_ref[...] = jnp.zeros_like(total_ref)

    def chunk_step(chunk, carry):
        lanes = pl.ds(pl.multiple_of(chunk * LANES, LANES), LANES)
        bias = block_bias(items_ref, item_query, chunk, key_rows, key_width)
        for head in range(heads):
            part = slice(head * HD, (head + 1) * HD)
            value_part = slice(head_width + head * HD, head_width + (head + 1) * HD)
            scores = masked_scores(near_ref[part, lanes], query_ref[part, :], bias)
            weights = jnp.exp(scores)
            total_ref[head : head + 1, :] += jnp.sum(weights, axis=0, keepdims=True)
            self_ref[part, :] += nn(near_ref[value_part, lanes], weights.astype(bf16))
        return carry

    lax.fori_loop(low_ref[block], high_ref[block], chunk_step, 0)
    stats_ref[...] = jnp.zeros_like(stats_ref)
    for head in range(heads):
        part = slice(head * HD, (head + 1) * HD)
        total = total_ref[head : head + 1, :]
        attended = self_ref[part, :] / total
        self_ref[part, :] = attended
        stats_ref[head : head + 1, :] = jnp.log(total)
        scores = tn(caption_key_ref[part, :], cross_ref[part, :])
        best = jnp.max(scores, axis=0, keepdims=True)
        weights = jnp.exp(scores - best)
        total = jnp.sum(weights, axis=0, keepdims=True)
        crossed = nn(caption_value_ref[part, :], (weights / total).astype(bf16))
        crossed_ref[part, :] = crossed
        stats_ref[heads + head : heads + head + 1, :] = best + jnp.log(total)
        mixed_ref[part, :] = (attended + gate_ref[part, 0:1] * crossed).astype(bf16)


def cross_back_kernel(
    heads,
    cross_ref,
    caption_key_ref,
    caption_value_ref,
    gate_ref,
    grad_ref,
    crossed_ref,
    stats_ref,
    grad_cross_ref,
    grad_key_ref,
    grad_value_ref,
    grad_gate_ref,
):
    @pl.when(pl.program_id(0) == 0)
    def _():
        grad_key_ref[...] = jnp.zeros_like(grad_key_ref)
        grad_value_ref[...] = jnp.zeros_like(grad_value_ref)
        grad_gate_ref[...] = jnp.zeros_like(grad_gate_ref)

    for head in range(heads):
        part = slice(head * HD, (head + 1) * HD)
        gate = gate_ref[part, 0:1]
        grad_wide = grad_ref[part, :].astype(f32)
        grad_crossed = (gate * grad_wide).astype(bf16)
        grad_gate_ref[part, 0:1] += jnp.sum(
            grad_wide * crossed_ref[part, :], axis=1, keepdims=True
        ) * (1.0 - gate * gate)
        scores = tn(caption_key_ref[part, :], cross_ref[part, :])
        weights = jnp.exp(scores - stats_ref[heads + head : heads + head + 1, :])
        grad_weights = tn(caption_value_ref[part, :], grad_crossed)
        delta = jnp.sum(weights * grad_weights, axis=0, keepdims=True)
        grad_scores = (weights * (grad_weights - delta)).astype(bf16)
        grad_cross_ref[part, :] = (
            nn(caption_key_ref[part, :], grad_scores) * (1.0 / math.sqrt(HD))
        ).astype(bf16)
        grad_key_ref[part, :] += nt(cross_ref[part, :], grad_scores)
        grad_value_ref[part, :] += nt(grad_crossed, weights.astype(bf16))


def attend_back_kernel(
    heads,
    key_rows,
    key_width,
    items_ref,
    low_ref,
    high_ref,
    item_query_ref,
    query_ref,
    above_ref,
    both_ref,
    below_ref,
    grad_ref,
    self_ref,
    stats_ref,
    grad_query_ref,
    grad_both_ref,
    delta_ref,
    near_ref,
):
    block = pl.program_id(0)
    head_width = heads * HD
    lay_out(block, near_ref, above_ref, both_ref, below_ref)

    @pl.when(block == 0)
    def _():
        grad_both_ref[...] = jnp.zeros_like(grad_both_ref)

    item_query = item_query_ref[0:1, :]
    grad_query_ref[...] = jnp.zeros_like(grad_query_ref)
    for head in range(heads):
        part = slice(head * HD, (head + 1) * HD)
        delta_ref[head : head + 1, :] = jnp.sum(
            grad_ref[part, :].astype(f32) * self_ref[part, :], axis=0, keepdims=True
        )

    def chunk_step(chunk, carry):
        lanes = pl.ds(pl.multiple_of(chunk * LANES, LANES), LANES)
        bias = block_bias(items_ref, item_query, chunk, key_rows, key_width)
        for head in range(heads):
            part = slice(head * HD, (head + 1) * HD)
            value_part = slice(head_width + head * HD, head_width + (head + 1) * HD)
            key_block = near_ref[part, lanes]
            query_block = query_ref[part, :]
            grad_block = grad_ref[part, :]
            scores = masked_scores(key_block, query_block, bias)
            weights = jnp.exp(scores - stats_ref[head : head + 1, :])
            grad_weights = tn(near_ref[value_part, lanes], grad_block)
            grad_scores = (weights * (grad_weights - delta_ref[head : head + 1, :])).astype(bf16)
            grad_query_ref[part, :] += nn(key_block, grad_scores)
            grad_both_ref[part, lanes] += nt(query_block, grad_scores)
            grad_both_ref[value_part, lanes] += nt(grad_block, weights.astype(bf16))
        return carry

    lax.fori_loop(low_ref[block], high_ref[block], chunk_step, 0)


def turn(values, tables):
    quarter = HD // 4
    first, second, third, fourth = (values[i * quarter : (i + 1) * quarter] for i in range(4))
    cos_rows, sin_rows, cos_cols, sin_cols = (
        tables[i * quarter : (i + 1) * quarter] for i in range(4)
    )
    return jnp.concatenate(
        [
            first * cos_rows - second * sin_rows,
            first * sin_rows + second * cos_rows,
            third * cos_cols - fourth * sin_cols,
            third * sin_cols + fourth * cos_cols,
        ],
        axis=0,
    )


def turn_back(values, tables):
    quarter = HD // 4
    first, second, third, fourth = (values[i * quarter : (i + 1) * quarter] for i in range(4))
    cos_rows, sin_rows, cos_cols, sin_cols = (
        tables[i * quarter : (i + 1) * quarter] for i in range(4)
    )
    return jnp.concatenate(
        [
            first * cos_rows + second * sin_rows,
            second * cos_rows - first * sin_rows,
            third * cos_cols + fourth * sin_cols,
            fourth * cos_cols - third * sin_cols,
        ],
        axis=0,
    )


def mean_inverse(values, axis):
    return lax.rsqrt(jnp.mean(values * values, axis=axis, keepdims=True) + EPS)


def project_kernel(
    heads,
    span,
    near_ref,
    embed_ref,
    vector_ref,
    mod_ref,
    weight_ref,
    table_ref,
    gain_ref,
    embedded_ref,
    normed_ref,
    raw_ref,
    query_ref,
    both_ref,
    cross_ref,
):
    block = pl.program_id(0)
    model = embed_ref.shape[0]
    head_width = heads * HD
    embedded_ref[...] = nt(near_ref[...], embed_ref[...]) + vector_ref[0:1, :]
    for j in range(LANES // span):
        rows = slice(j * span, (j + 1) * span)
        embedded = embedded_ref[rows, :]
        scale = mod_ref[pl.ds(block * (LANES // span) + j, 1), 0:model]
        factor = vector_ref[1:2, :] * (1.0 + scale)
        normed_ref[rows, :] = (embedded * mean_inverse(embedded, -1) * factor).astype(bf16)
    raw = nn(normed_ref[...], weight_ref[...]).astype(bf16).astype(f32).T
    tables = table_ref[...]
    score_scale = 1.0 / math.sqrt(HD)
    raw_ref[...] = raw[0 : 2 * head_width].astype(bf16)
    for head in range(heads):
        part = slice(head * HD, (head + 1) * HD)
        query = raw[part]
        query = turn(query * mean_inverse(query, 0) * gain_ref[part, 0:1], tables)
        query_ref[part, :] = (query.astype(bf16).astype(f32) * score_scale).astype(bf16)
        key = raw[head_width + head * HD : head_width + (head + 1) * HD]
        key = turn(key * mean_inverse(key, 0) * gain_ref[part, 1:2], tables)
        both_ref[part, :] = key.astype(bf16)
    both_ref[head_width:, :] = raw[2 * head_width : 3 * head_width].astype(bf16)
    cross_ref[...] = (raw[3 * head_width :] * score_scale).astype(bf16)


def middle_kernel(
    pieces,
    span,
    own_ref,
    place_ref,
    *refs,
):
    mixed_refs, refs = refs[:pieces], refs[pieces:]
    (
        embedded_ref,
        patch_ref,
        vector_ref,
        mod_ref,
        output_ref,
        gu_ref,
        down_ref,
        unpatch_ref,
        mixed_ref,
        residual_ref,
        inner_ref,
        hidden_ref,
        grad_feed_ref,
        grad_gu_ref,
        part_residual_ref,
        part_branch_ref,
        grad_mixed_ref,
        scale_rows_ref,
        gate_rows_ref,
        gain_ref,
        branch_ref,
        grad_inner_ref,
    ) = refs
    block = pl.program_id(0)
    row_count = LANES // span
    model = embedded_ref.shape[1]
    groups = output_ref.shape[0]
    group = model // groups
    ff_mine = down_ref.shape[0]

    @pl.when(block == 0)
    def _():
        gain_ref[...] = jnp.zeros_like(gain_ref)

    for i, ref in enumerate(mixed_refs):
        size = ref.shape[0]
        mixed_ref[pl.ds(pl.multiple_of(place_ref[i], 32), size), :] = ref[...]
    for g in range(groups):
        branch_ref[:, g * group : (g + 1) * group] = tn(mixed_ref[...], output_ref[g])
    ff_gain = vector_ref[2:3, :]

    def mods(j, which):
        return mod_ref[
            pl.ds(block * row_count + j, 1), which * model : (which + 1) * model
        ]

    for j in range(row_count):
        rows = slice(j * span, (j + 1) * span)
        residual = embedded_ref[rows, :] + jnp.tanh(mods(j, 1)) * branch_ref[rows, :]
        residual_ref[rows, :] = residual
        factor = ff_gain * (1.0 + mods(j, 2))
        inner_ref[rows, :] = (residual * mean_inverse(residual, -1) * factor).astype(bf16)
    inner = inner_ref[...]
    ff_groups = gu_ref.shape[0]
    ff_group = 2 * ff_mine // ff_groups
    half = ff_groups // 2
    grad_inner_ref[...] = nt(patch_ref[...], unpatch_ref[...])
    for j in range(row_count):
        rows = slice(j * span, (j + 1) * span)
        grad_feed_ref[rows, :] = (jnp.tanh(mods(j, 3)) * grad_inner_ref[rows, :]).astype(bf16)
    grad_hidden = nt(grad_feed_ref[...], down_ref[...])
    for g in range(half):
        gate = nn(inner, gu_ref[g])
        upward = nn(inner, gu_ref[half + g])
        sigmoid = jax.nn.sigmoid(gate)
        silu = gate * sigmoid
        cols = slice(g * ff_group, (g + 1) * ff_group)
        hidden_ref[:, cols] = (silu * upward).astype(bf16)
        grad = grad_hidden[:, cols]
        grad_gu_ref[:, cols] = (
            grad * upward * (sigmoid * (1.0 + gate * (1.0 - sigmoid)))
        ).astype(bf16)
        grad_gu_ref[:, ff_mine + g * ff_group : ff_mine + (g + 1) * ff_group] = (
            grad * silu
        ).astype(bf16)
    own_column = lax.broadcasted_iota(jnp.int32, (span, 1), 0)
    mine = (own_column >= own_ref[0]) & (own_column < own_ref[1])
    for j in range(row_count):
        rows = slice(j * span, (j + 1) * span)
        part_residual_ref[rows, :] = jnp.where(mine, grad_inner_ref[rows, :], 0.0)
    total = nt(grad_gu_ref[:, 0:ff_group], gu_ref[0])
    for g in range(1, ff_groups):
        total = total + nt(grad_gu_ref[:, g * ff_group : (g + 1) * ff_group], gu_ref[g])
    grad_inner_ref[...] = total
    for j in range(row_count):
        rows = slice(j * span, (j + 1) * span)
        tanh_one = jnp.tanh(mods(j, 1))
        second_scale = mods(j, 2)
        residual = residual_ref[rows, :]
        inverse = mean_inverse(residual, -1)
        unit = residual * inverse
        grad_inner = grad_inner_ref[rows, :]
        summed = jnp.sum(grad_inner * unit, axis=0, keepdims=True)
        scale_rows_ref[pl.ds(block * row_count + j, 1), :] = summed * ff_gain
        gain_ref[0:1, :] += summed * (1.0 + second_scale)
        grad_unit = grad_inner * (ff_gain * (1.0 + second_scale))
        part = part_residual_ref[rows, :] + inverse * (
            grad_unit - unit * jnp.mean(grad_unit * unit, axis=-1, keepdims=True)
        )
        part_residual_ref[rows, :] = part
        part_branch_ref[rows, :] = (tanh_one * part).astype(bf16)
        gate_rows_ref[pl.ds(block * row_count + j, 1), :] = jnp.sum(
            part * branch_ref[rows, :], axis=0, keepdims=True
        ) * (1.0 - tanh_one * tanh_one)
    total = nt(output_ref[0], part_branch_ref[:, 0:group])
    for g in range(1, groups):
        total = total + nt(output_ref[g], part_branch_ref[:, g * group : (g + 1) * group])
    grad_mixed_ref[...] = total.astype(bf16)


def result_kernel(
    span,
    own_ref,
    hidden_ref,
    residual_ref,
    patch_ref,
    mod_ref,
    down_ref,
    unpatch_ref,
    cells_ref,
    grad_unpatch_ref,
    gate_rows_ref,
    feed_ref,
    grad_ref,
    result_ref,
):
    block = pl.program_id(0)
    row_count = LANES // span
    model = residual_ref.shape[1]

    @pl.when(block == 0)
    def _():
        grad_unpatch_ref[...] = jnp.zeros_like(grad_unpatch_ref)

    feed_ref[...] = nn(hidden_ref[...], down_ref[...])
    grad_ref[...] = nt(patch_ref[...], unpatch_ref[...])
    own_column = lax.broadcasted_iota(jnp.int32, (span, 1), 0)
    mine = (own_column >= own_ref[0]) & (own_column < own_ref[1])
    for j in range(row_count):
        rows = slice(j * span, (j + 1) * span)
        tanh_two = jnp.tanh(mod_ref[pl.ds(block * row_count + j, 1), 3 * model : 4 * model])
        feed = feed_ref[rows, :]
        result_ref[rows, :] = (
            jnp.where(mine, residual_ref[rows, :], 0.0) + tanh_two * feed
        ).astype(bf16)
        gate_rows_ref[pl.ds(block * row_count + j, 1), :] = jnp.sum(
            grad_ref[rows, :] * feed, axis=0, keepdims=True
        ) * (1.0 - tanh_two * tanh_two)
    cells_ref[...] = nn(result_ref[...], unpatch_ref[...])
    grad_unpatch_ref[...] += tn(patch_ref[...], result_ref[...])


def finish_kernel(
    heads,
    span,
    grad_query_ref,
    grad_key_ref,
    grad_value_ref,
    grad_cross_ref,
    raw_ref,
    table_ref,
    gain_ref,
    embedded_ref,
    part_residual_ref,
    near_ref,
    vector_ref,
    mod_ref,
    weight_ref,
    embed_ref,
    grad_raw_ref,
    cells_ref,
    grad_embed_ref,
    scale_rows_ref,
    sums_ref,
    head_sums_ref,
    turned_ref,
    grad_normed_ref,
    part_ref,
):
    block = pl.program_id(0)
    row_count = LANES // span
    model = embedded_ref.shape[1]
    head_width = heads * HD
    score_scale = 1.0 / math.sqrt(HD)

    @pl.when(block == 0)
    def _():
        grad_embed_ref[...] = jnp.zeros_like(grad_embed_ref)
        sums_ref[...] = jnp.zeros_like(sums_ref)
        head_sums_ref[...] = jnp.zeros_like(head_sums_ref)

    tables = table_ref[...]
    for which in range(2):
        for head in range(heads):
            part = slice(head * HD, (head + 1) * HD)
            if which == 0:
                grad = (grad_query_ref[part, :] * score_scale).astype(bf16).astype(f32)
            else:
                grad = grad_key_ref[part, :].astype(bf16).astype(f32)
            at = which * head_width + head * HD
            raw = raw_ref[at : at + HD, :].astype(f32)
            grad = turn_back(grad, tables)
            inverse = mean_inverse(raw, 0)
            unit = raw * inverse
            head_sums_ref[part, which : which + 1] += jnp.sum(grad * unit, axis=1, keepdims=True)
            grad = grad * gain_ref[part, which : which + 1]
            turned_ref[at : at + HD, :] = inverse * (
                grad - unit * jnp.mean(grad * unit, axis=0, keepdims=True)
            )
    turned_ref[2 * head_width : 3 * head_width, :] = grad_value_ref[...].astype(f32)
    turned_ref[3 * head_width :, :] = grad_cross_ref[...].astype(f32)
    grad_raw_ref[...] = turned_ref[...].T.astype(bf16)
    grad_normed_ref[...] = nt(grad_raw_ref[...], weight_ref[...])
    gain = vector_ref[1:2, :]
    for j in range(row_count):
        rows = slice(j * span, (j + 1) * span)
        scale = mod_ref[pl.ds(block * row_count + j, 1), 0:model]
        embedded = embedded_ref[rows, :]
        inverse = mean_inverse(embedded, -1)
        unit = embedded * inverse
        grad_normed = grad_normed_ref[rows, :]
        summed = jnp.sum(grad_normed * unit, axis=0, keepdims=True)
        scale_rows_ref[pl.ds(block * row_count + j, 1), :] = summed * gain
        sums_ref[0:1, :] += summed * (1.0 + scale)
        grad_unit = grad_normed * (gain * (1.0 + scale))
        part = part_residual_ref[rows, :] + inverse * (
            grad_unit - unit * jnp.mean(grad_unit * unit, axis=-1, keepdims=True)
        )
        part = part.astype(bf16)
        part_ref[rows, :] = part
        sums_ref[1:2, :] += jnp.sum(part.astype(f32), axis=0, keepdims=True)
    cells_ref[...] = nn(part_ref[...], embed_ref[...])
    grad_embed_ref[...] += tn(near_ref[...], part_ref[...])


def on_device(
    latents,
    captions,
    item_heights,
    item_bands,
    embedding,
    embed_bias,
    band_table,
    adaptive,
    adaptive_bias,
    attention_gain,
    projection,
    query_gain,
    key_gain,
    cross_query,
    caption_weight,
    cross_gate,
    output_weight,
    feedforward_gain,
    gate_weight,
    up_weight,
    down_weight,
    unpatch_weight,
    cotangent,
):
    rows_n, sub_n, tp_n = (lax.axis_size(a) for a in ALL)
    col_n = sub_n * tp_n
    all_n = rows_n * col_n
    row = lax.axis_index("row")
    sub = lax.axis_index("sub")
    tp = lax.axis_index("tp")
    tile_rows, tile_cols, channels = latents.shape
    grid_rows = tile_rows * rows_n
    grid_cols = tile_cols * col_n
    span = tile_cols * tp_n
    tokens = tile_rows * span
    own = tile_rows * tile_cols
    width = embed_bias.shape[0]
    model = width * col_n
    head_width = model // tp_n
    heads = head_width // HD
    owned = model // all_n
    quarter = width // rows_n
    ff = gate_weight.shape[1]
    ff_part = ff // col_n
    ff_mine = ff // tp_n
    text = captions.shape[0]
    patch = 9 * channels

    index = (row * sub_n + sub) * tp_n + tp
    col = sub * tp_n + tp

    def to_peers(piece):
        spread = jnp.broadcast_to(piece[None], (sub_n,) + piece.shape)
        return spread.reshape((col_n,) + piece.shape[1:])

    def share(pieces):
        whole = row_gather(pieces)
        return whole.transpose(1, 0, 2, 3).reshape(model, pieces.shape[2])

    def my_quarter(weight):
        return lax.dynamic_slice_in_dim(weight, row * quarter, quarter, 0)

    copies = []
    for t in range(tp_n):
        for i in range(3):
            copies.append((0, None, i * model + t * head_width, 2, t, i * head_width, head_width))
        copies.append((1, None, t * head_width, 2, t, 3 * head_width, head_width))
    qkvc_piece = pack(
        copies,
        jax.ShapeDtypeStruct((tp_n, quarter, 4 * head_width), bf16),
        my_quarter(projection),
        my_quarter(cross_query),
    )
    tiles = jnp.concatenate([latents, cotangent], axis=-1).reshape(-1, 128)
    tiles_width = -(-tiles.shape[0] // quarter) * 128
    tiles = jnp.pad(tiles, ((0, quarter * tiles_width // 128 - tiles.shape[0]), (0, 0)))
    tiles = tiles.reshape(tiles_width // 128, quarter, 128).transpose(1, 0, 2)
    tiles = jnp.broadcast_to(tiles.reshape(1, quarter, tiles_width), (tp_n, quarter, tiles_width))
    qkvc_pieces = swap(to_peers(jnp.concatenate([qkvc_piece, tiles], axis=2)), COL)
    weight_qkvc = share(qkvc_pieces[:, :, : 4 * head_width])
    tiles = qkvc_pieces[:, :, 4 * head_width :].reshape(col_n, quarter, tiles_width // 128, 128)
    tiles = tiles.transpose(0, 2, 1, 3).reshape(col_n, -1, 128)
    tiles = tiles[:, : own * 2 * channels // 128].reshape(
        col_n, tile_rows, tile_cols, 2 * channels
    )
    grid = tiles.transpose(1, 0, 2, 3).reshape(tile_rows, grid_cols, 2 * channels)
    grid = jnp.concatenate(
        [
            shift(grid[tile_rows - 1 :], "row", True),
            grid,
            shift(grid[:1], "row", False),
        ],
        axis=0,
    )
    grid = jnp.pad(grid, ((0, 0), (1, 1), (0, 0)))
    bordered = lax.dynamic_slice_in_dim(grid, sub * span, span + 2, 1)
    neighbours = gather_cells(bordered[..., 0:channels], tile_rows, span).reshape(tokens, patch)
    patch_grads = gather_cells(bordered[..., channels : 2 * channels], tile_rows, span)
    patch_grads = patch_grads.reshape(tokens, patch)

    mod_width = adaptive.shape[1] // rows_n
    mod_bias = lax.dynamic_update_slice_in_dim(
        jnp.zeros((adaptive.shape[1],), f32), adaptive_bias.astype(f32), col * adaptive_bias.shape[0], 0
    )
    silu_band = jax.nn.silu(band_table.astype(f32))

    def mod_columns(start, count):
        return (
            jnp.dot(
                silu_band,
                lax.dynamic_slice_in_dim(adaptive, start, count, 1).astype(f32),
                precision=HIGH,
            )
            + lax.dynamic_slice_in_dim(mod_bias, start, count, 0)
        ).astype(bf16)

    columns = jnp.concatenate(
        [
            embedding.T,
            embed_bias[:, None],
            attention_gain[:, None],
            feedforward_gain[:, None],
            band_table.T,
            mod_columns(row * mod_width, mod_width).T.reshape(width, -1),
        ],
        axis=1,
    )
    columns_n = columns.shape[1]
    wide = -(-columns_n // 128) * 128
    columns = jnp.pad(columns, ((0, 0), (0, wide - columns_n)))

    def in_quarters(array):
        parts = array.reshape(-1, quarter, array.shape[1])
        return parts.transpose(1, 0, 2).reshape(quarter, -1)

    def from_quarters(array, columns_each):
        parts = array.reshape(array.shape[:-1] + (-1, columns_each))
        parts = jnp.moveaxis(parts, -2, -3)
        return parts.reshape(parts.shape[:-3] + (-1, columns_each))

    text_part = text // rows_n
    cap_part = jnp.dot(
        lax.dynamic_slice(
            captions,
            (row * text_part, col * caption_weight.shape[0]),
            (text_part, caption_weight.shape[0]),
        ),
        caption_weight,
        preferred_element_type=f32,
    )
    copies = []
    for t in range(tp_n):
        for i in range(2):
            copies.append((0, None, i * model + t * head_width, 1, t, i * head_width, head_width))
    cap_part = pack(
        copies, jax.ShapeDtypeStruct((tp_n, text_part, 2 * head_width), bf16), cap_part
    )
    cap_lanes = 2 * head_width // 128
    cap_part = (
        cap_part.reshape(tp_n, text_part, cap_lanes, 128)
        .transpose(0, 2, 1, 3)
        .reshape(tp_n, -1, quarter, 128)
        .transpose(0, 2, 1, 3)
        .reshape(tp_n, quarter, -1)
    )
    same = jnp.concatenate(
        [in_quarters(columns), in_quarters(mod_columns(0, model).reshape(-1, 256))], axis=1
    )
    same_width = same.shape[1]
    sent = jnp.concatenate(
        [jnp.broadcast_to(same[None], (tp_n,) + same.shape), cap_part], axis=2
    )
    got = swap(to_peers(after(sent, qkvc_pieces)), COL)
    columns = from_quarters(got[:, :, : rows_n * wide], wide).reshape(model, wide)
    embedding_t = columns[:, 0:patch]
    at = patch + 3 + NBAND
    vectors = columns[:, patch:at].T.astype(f32)
    full_band = vectors[3:]
    first_scale = jnp.sum(got[:, :, rows_n * wide : same_width].astype(f32), axis=0)
    first_scale = from_quarters(first_scale, 256).reshape(NBAND, model)
    item_of_row, row_place, band_onehot = row_items(item_heights, item_bands, grid_rows)
    tile_onehot = lax.dynamic_slice_in_dim(band_onehot, row * tile_rows, tile_rows, 0)
    first_mods = jnp.dot(
        tile_onehot, after(first_scale, weight_qkvc, neighbours), precision=HIGH
    )
    mod_part = columns[:, at:columns_n].reshape(col_n, width, -1)
    mod_part = jnp.sum(mod_part.astype(f32), axis=0).reshape(mod_width, NBAND).T
    cap_part = jnp.sum(got[:, :, same_width:].astype(f32), axis=0).astype(bf16)

    output_width = model // rows_n
    output_piece = lax.dynamic_slice_in_dim(output_weight, row * output_width, output_width, 1)
    output_piece = lax.all_gather(output_piece, COL, axis=0, tiled=True)
    full_output = lax.all_gather(output_piece, "row", axis=0)

    shared_mods = NBAND * mod_width // quarter
    shared = row_gather(
        jnp.concatenate([in_quarters(mod_part.reshape(-1, 256).astype(bf16)), cap_part], axis=1)
    )
    caption_heads = (
        from_quarters(shared[:, :, shared_mods:], 128)
        .reshape(rows_n, cap_lanes, text_part, 128)
        .transpose(1, 3, 0, 2)
        .reshape(2 * head_width, text)
    )
    caption_keys = caption_heads[:head_width]
    caption_values = caption_heads[head_width:]

    frequency = THETA ** (-jnp.arange(HD // 4, dtype=f32) / (HD // 4))
    tile_place = lax.dynamic_slice_in_dim(row_place, row * tile_rows, tile_rows, 0)
    row_angles = frequency[:, None] * jnp.repeat(tile_place, span).astype(f32)[None, :]
    col_place = sub * span + jnp.tile(jnp.arange(span), tile_rows)
    col_angles = frequency[:, None] * col_place.astype(f32)[None, :]
    tables = jnp.concatenate(
        [jnp.cos(row_angles), jnp.sin(row_angles), jnp.cos(col_angles), jnp.sin(col_angles)],
        axis=0,
    )
    gate_column = jnp.tanh(_mine(cross_gate, tp, sub_n).astype(f32))[:, None]
    gains = jnp.stack(
        [_mine(query_gain, tp, sub_n).astype(f32), _mine(key_gain, tp, sub_n).astype(f32)], axis=1
    )
    blocks = tokens // LANES

    def by_block(count):
        return pl.BlockSpec((count, LANES), lambda i, *_: (0, i))

    def by_rows(count):
        return pl.BlockSpec((LANES, count), lambda i, *_: (i, 0))

    def whole(*shape):
        return pl.BlockSpec(shape, lambda i, *_: (0,) * len(shape))

    def struct(shape, dtype=f32):
        return jax.ShapeDtypeStruct(shape, dtype)

    vmem = pltpu.CompilerParams(vmem_limit_bytes=56 * 2**20)
    embedded, normed, raw, queries, both, raw_cross = pl.pallas_call(
        functools.partial(project_kernel, heads, span),
        grid=(blocks,),
        in_specs=[
            by_rows(patch),
            whole(model, patch),
            whole(*vectors.shape),
            whole(*first_mods.shape),
            whole(model, 4 * head_width),
            by_block(HD),
            whole(head_width, 2),
        ],
        out_specs=[
            by_rows(model),
            by_rows(model),
            by_block(2 * head_width),
            by_block(head_width),
            by_block(2 * head_width),
            by_block(head_width),
        ],
        out_shape=[
            struct((tokens, model)),
            struct((tokens, model), bf16),
            struct((2 * head_width, tokens), bf16),
            struct((head_width, tokens), bf16),
            struct((2 * head_width, tokens), bf16),
            struct((head_width, tokens), bf16),
        ],
        compiler_params=vmem,
        name="project",
        cost_estimate=cost(10),
    )(neighbours, embedding_t, vectors, first_mods, weight_qkvc, tables, gains)
    modulations = (
        from_quarters(shared[:, :, :shared_mods], 256)
        .reshape(rows_n, NBAND, mod_width)
        .transpose(1, 0, 2)
        .reshape(NBAND, adaptive.shape[1])
        .astype(f32)
    )
    mods = jnp.dot(tile_onehot, modulations, precision=HIGH)

    gu_width = 2 * ff_mine // rows_n
    which_half = rows_n // 2
    gu_source = jnp.where(row < which_half, gate_weight, up_weight)
    gu_piece = lax.dynamic_slice_in_dim(
        gu_source.reshape(width, sub_n, tp_n, which_half, ff_part // which_half),
        lax.rem(row, which_half),
        1,
        3,
    )
    gu_piece = gu_piece.transpose(2, 0, 1, 3, 4).reshape(tp_n, width, gu_width)
    unpatch_piece = jnp.pad(my_quarter(unpatch_weight), ((0, 0), (0, gu_width - patch)))
    gu_piece = jnp.concatenate(
        [gu_piece, jnp.broadcast_to(unpatch_piece[None], (tp_n,) + unpatch_piece.shape)], axis=1
    )
    gu_pieces = swap(to_peers(after(gu_piece, queries)), COL)
    down_mine = down_weight
    if sub_n > 1:
        down_mine = lax.all_gather(down_weight, "sub", axis=0, tiled=True)

    if sub_n > 1:
        both = (
            lax.all_gather(both, "sub", axis=0)
            .reshape(sub_n, 2 * head_width, tile_rows, span)
            .transpose(1, 2, 0, 3)
            .reshape(2 * head_width, tile_rows * grid_cols)
        )
    edge = HALO * grid_cols
    middle_cols = both.shape[1]
    above = shift(both[:, middle_cols - edge :], "row", True)
    below = shift(both[:, :edge], "row", False)

    near_rows = tile_rows + 2 * HALO
    key_rows = max(1, LANES // grid_cols)
    key_width = LANES // key_rows
    block_rows = LANES // span
    items_padded = jnp.concatenate(
        [
            jnp.full((HALO,), -1, jnp.int32),
            item_of_row.astype(jnp.int32),
            jnp.full((HALO,), item_heights.shape[0] + 1, jnp.int32),
        ]
    )
    items_near = lax.dynamic_slice_in_dim(items_padded, row * tile_rows, near_rows, 0)
    item_query = jnp.repeat(items_near[HALO : HALO + tile_rows], span)[None, :]
    chunk_items = jnp.repeat(items_near, grid_cols // (key_width)).reshape(-1, key_rows)
    query_items = items_near[HALO : HALO + tile_rows].reshape(blocks, block_rows)
    before = chunk_items[None, :, -1] < query_items[:, None, 0]
    reached = chunk_items[None, :, 0] <= query_items[:, None, -1]
    low = jnp.sum(before.astype(jnp.int32), axis=1)
    high = jnp.sum(reached.astype(jnp.int32), axis=1)
    chunk_items = chunk_items.reshape(-1)
    near = near_rows * grid_cols

    mixed, self_out, crossed, stats = pl.pallas_call(
        waits_for(functools.partial(attend_kernel, heads, key_rows, key_width), 12, 2),
        grid_spec=pltpu.PrefetchScalarGridSpec(
            num_scalar_prefetch=3,
            grid=(blocks,),
            in_specs=[
                by_block(1),
                by_block(head_width),
                whole(2 * head_width, edge),
                whole(2 * head_width, middle_cols),
                whole(2 * head_width, edge),
                by_block(head_width),
                whole(head_width, text),
                whole(head_width, text),
                whole(head_width, 1),
                ANYWHERE,
                ANYWHERE,
            ],
            out_specs=[by_block(head_width), by_block(head_width), by_block(head_width), by_block(8)],
            scratch_shapes=[
                pltpu.VMEM((8, LANES), f32),
                pltpu.VMEM((2 * head_width, near), bf16),
            ],
        ),
        out_shape=[
            jax.ShapeDtypeStruct((head_width, tokens), bf16),
            jax.ShapeDtypeStruct((head_width, tokens), f32),
            jax.ShapeDtypeStruct((head_width, tokens), f32),
            jax.ShapeDtypeStruct((8, tokens), f32),
        ],
        compiler_params=vmem,
        name="attend",
        cost_estimate=cost(14),
    )(
        chunk_items,
        low,
        high,
        item_query,
        queries,
        above,
        both,
        below,
        raw_cross,
        caption_keys,
        caption_values,
        gate_column,
        mods,
        patch_grads,
    )

    weight_gu = lax.all_gather(after(gu_pieces, mixed, full_output), "row", axis=0)
    full_unpatch = weight_gu[:, :, width:, :patch].transpose(1, 0, 2, 3).reshape(model, patch)
    weight_gu = weight_gu[:, :, :width].reshape(rows_n, model, gu_width)
    pieces, starts = ring_gather(mixed, "tp")
    own_span = jnp.stack([tp * tile_cols, (tp + 1) * tile_cols]).astype(jnp.int32)
    (
        mixed_all,
        residual,
        inner,
        hidden,
        grad_feed,
        grad_gu,
        part_residual,
        part_branch,
        grad_mixed,
        rows_second_scale,
        rows_first_gate,
        grad_ff_gain,
    ) = pl.pallas_call(
        functools.partial(middle_kernel, len(pieces), span),
        grid_spec=pltpu.PrefetchScalarGridSpec(
            num_scalar_prefetch=2,
            grid=(blocks,),
            in_specs=[by_block(piece.shape[0]) for piece in pieces]
            + [
                by_rows(model),
                by_rows(patch),
                whole(*vectors.shape),
                whole(*mods.shape),
                whole(*full_output.shape),
                whole(*weight_gu.shape),
                whole(*down_mine.shape),
                whole(model, patch),
            ],
            out_specs=[
                by_block(model),
                by_rows(model),
                by_rows(model),
                by_rows(ff_mine),
                by_rows(model),
                by_rows(2 * ff_mine),
                by_rows(model),
                by_rows(model),
                by_block(model),
                whole(tile_rows, model),
                whole(tile_rows, model),
                whole(8, model),
            ],
            scratch_shapes=[pltpu.VMEM((LANES, model), f32), pltpu.VMEM((LANES, model), f32)],
        ),
        out_shape=[
            struct((model, tokens), bf16),
            struct((tokens, model)),
            struct((tokens, model), bf16),
            struct((tokens, ff_mine), bf16),
            struct((tokens, model), bf16),
            struct((tokens, 2 * ff_mine), bf16),
            struct((tokens, model)),
            struct((tokens, model), bf16),
            struct((model, tokens), bf16),
            struct((tile_rows, model)),
            struct((tile_rows, model)),
            struct((8, model)),
        ],
        compiler_params=vmem,
        name="middle",
        cost_estimate=cost(35),
    )(
        own_span,
        starts,
        *pieces,
        embedded,
        patch_grads,
        vectors,
        mods,
        full_output,
        weight_gu,
        down_mine,
        full_unpatch,
    )

    def result_part(held):
        return pl.pallas_call(
            waits_for(functools.partial(result_kernel, span), 7, 2),
            grid_spec=pltpu.PrefetchScalarGridSpec(
                num_scalar_prefetch=1,
                grid=(blocks,),
                in_specs=[
                    by_rows(ff_mine),
                    by_rows(model),
                    by_rows(patch),
                    whole(*mods.shape),
                    whole(*down_mine.shape),
                    whole(model, patch),
                    ANYWHERE,
                    ANYWHERE,
                ],
                out_specs=[by_rows(patch), whole(patch, model), whole(tile_rows, model)],
                scratch_shapes=[
                    pltpu.VMEM((LANES, model), f32),
                    pltpu.VMEM((LANES, model), f32),
                    pltpu.VMEM((LANES, model), bf16),
                ],
            ),
            out_shape=[struct((tokens, patch)), struct((patch, model)), struct((tile_rows, model))],
            compiler_params=vmem,
            name="result",
        cost_estimate=cost(9),
        )(own_span, hidden, residual, patch_grads, mods, down_mine, full_unpatch, *held)

    def mixed_block(which):
        return lax.dynamic_slice_in_dim(
            grad_mixed, which * head_width, head_width, 0
        ).astype(f32)

    def gu_part(held):
        return (dot(inner, after(grad_gu, *held), 0, 0).astype(bf16),)

    def output_part(held):
        return (dot(mixed_all, after(part_branch, *held), 1, 0).astype(bf16),)

    grad_mixed, done = ring_scatter(mixed_block, "tp", [gu_part, output_part, result_part])
    grad_mixed = grad_mixed.astype(bf16)
    (grad_gu_part,), (grad_output_part,), (cells, grad_unpatch, rows_second_gate) = done

    def cells_out(*parts):
        around = jnp.concatenate(
            [
                spread_cells(
                    jnp.pad(part.reshape(tile_rows, span, patch), ((2, 2), (2, 2), (0, 0))),
                    tile_rows + 2,
                    span + 2,
                    channels,
                )
                for part in parts
            ],
            axis=-1,
        )
        inside = around[:, 1 : span + 1]
        if sub_n > 1:
            from_left = shift(around[:, span + 1 :].astype(bf16), "sub", True).astype(f32)
            from_right = shift(around[:, :1].astype(bf16), "sub", False).astype(f32)
            inside = (
                inside
                + jnp.pad(from_left, ((0, 0), (0, span - 1), (0, 0)))
                + jnp.pad(from_right, ((0, 0), (span - 1, 0), (0, 0)))
            )
        from_above = shift(inside[tile_rows + 1 :].astype(bf16), "row", True).astype(f32)
        from_below = shift(inside[:1].astype(bf16), "row", False).astype(f32)
        inside = (
            inside[1 : tile_rows + 1]
            + jnp.pad(from_above, ((0, tile_rows - 1), (0, 0), (0, 0)))
            + jnp.pad(from_below, ((tile_rows - 1, 0), (0, 0), (0, 0)))
        )
        inside = (
            inside.astype(bf16)
            .reshape(tile_rows, tp_n, tile_cols, -1)
            .transpose(1, 0, 2, 3)
            .reshape(tp_n, -1, 128)
        )
        rows = -(-inside.shape[1] // owned) * owned
        inside = jnp.pad(inside, ((0, 0), (0, rows - inside.shape[1]), (0, 0)))
        return inside.reshape(tp_n, rows // owned, owned, 128).transpose(0, 2, 1, 3).reshape(
            tp_n, owned, -1
        )

    def cells_in(got):
        inside = jnp.sum(got.astype(f32), axis=0).reshape(owned, -1, 128).transpose(1, 0, 2)
        inside = inside.reshape(-1, 128)[: own * 2 * channels // 128]
        return inside.reshape(tile_rows, tile_cols, 2 * channels).astype(bf16)

    def to_chunks(partial):
        summed = lax.psum_scatter(partial.astype(bf16), "row", scatter_dimension=0, tiled=True)
        if sub_n > 1:
            summed = lax.psum_scatter(summed, "sub", scatter_dimension=0, tiled=True)
        return summed

    def scatter_rows(partial):
        if sub_n > 1:
            return to_chunks(partial)
        return row_scatter(partial).astype(bf16)

    def bands(rows):
        return dot(tile_onehot, rows, 0, 0, HIGH)

    first_cells = cells
    grad_gu_sum = to_chunks(grad_gu_part)
    grad_cross, grad_cap_keys, grad_cap_values, grad_gate_part = pl.pallas_call(
        functools.partial(cross_back_kernel, heads),
        grid=(blocks,),
        in_specs=[
            by_block(head_width),
            whole(head_width, text),
            whole(head_width, text),
            whole(head_width, 1),
            by_block(head_width),
            by_block(head_width),
            by_block(8),
        ],
        out_specs=[
            by_block(head_width),
            whole(head_width, text),
            whole(head_width, text),
            whole(head_width, 128),
        ],
        out_shape=[
            jax.ShapeDtypeStruct((head_width, tokens), bf16),
            jax.ShapeDtypeStruct((head_width, text), f32),
            jax.ShapeDtypeStruct((head_width, text), f32),
            jax.ShapeDtypeStruct((head_width, 128), f32),
        ],
        compiler_params=vmem,
        name="cross_back",
        cost_estimate=cost(7),
    )(raw_cross, caption_keys, caption_values, gate_column, grad_mixed, crossed, stats)

    grad_queries, grad_both = pl.pallas_call(
        functools.partial(attend_back_kernel, heads, key_rows, key_width),
        grid_spec=pltpu.PrefetchScalarGridSpec(
            num_scalar_prefetch=3,
            grid=(blocks,),
            in_specs=[
                by_block(1),
                by_block(head_width),
                whole(2 * head_width, edge),
                whole(2 * head_width, middle_cols),
                whole(2 * head_width, edge),
                by_block(head_width),
                by_block(head_width),
                by_block(8),
            ],
            out_specs=[by_block(head_width), whole(2 * head_width, near)],
            scratch_shapes=[
                pltpu.VMEM((8, LANES), f32),
                pltpu.VMEM((2 * head_width, near), bf16),
            ],
        ),
        out_shape=[
            jax.ShapeDtypeStruct((head_width, tokens), f32),
            jax.ShapeDtypeStruct((2 * head_width, near), f32),
        ],
        compiler_params=vmem,
        name="attend_back",
        cost_estimate=cost(14),
    )(chunk_items, low, high, item_query, queries, above, both, below, grad_mixed, self_out, stats)

    moves = []
    for source in range(all_n):
        source_row, rest = divmod(source, col_n)
        moves.append((source, rest * rows_n + source_row))
    output_sum = to_chunks(grad_output_part)
    got_gu = swap(after(grad_gu_sum, grad_mixed).reshape(tp_n, owned, -1), "tp")
    grad_down_part = dot(hidden, after(grad_feed, grad_queries), 0, 0).astype(bf16)
    grad_down = (
        grad_down_part.reshape(sub_n, rows_n, ff // all_n, model)
        .transpose(1, 0, 2, 3)
        .reshape(-1, model)
    )
    copies = []
    for t in range(tp_n):
        for i in range(2):
            for s in range(sub_n):
                copies.append(
                    (0, t, i * ff_mine + s * ff_part, 1 + i, None, (s * tp_n + t) * ff_part, ff_part)
                )
    grad_gate_weight, grad_up_weight = pack(
        copies, [jax.ShapeDtypeStruct((owned, ff), f32)] * 2, got_gu
    )

    grad_down_sum = to_chunks(grad_down)

    upper = grad_both[:, :edge].astype(bf16)
    lower = grad_both[:, near - edge :].astype(bf16)
    middle = grad_both[:, edge : near - edge]
    from_above = shift(lower, "row", True).astype(f32)
    from_below = shift(upper, "row", False).astype(f32)
    side = middle.shape[1] - edge
    middle = (
        middle
        + jnp.pad(from_above, ((0, 0), (0, side)))
        + jnp.pad(from_below, ((0, 0), (side, 0)))
    )
    if sub_n > 1:
        middle = (
            middle.astype(bf16)
            .reshape(2 * head_width, tile_rows, sub_n, span)
            .transpose(2, 0, 1, 3)
            .reshape(sub_n, 2 * head_width, tokens)
        )
        middle = jnp.sum(swap(middle, "sub").astype(f32), axis=0)
    grad_keys, grad_values = middle[:head_width], middle[head_width:]

    grad_raw, cells, grad_embedding, rows_first_scale, sums, head_sums = pl.pallas_call(
        waits_for(functools.partial(finish_kernel, heads, span), 14, 2),
        grid=(blocks,),
        in_specs=[
            by_block(head_width),
            by_block(head_width),
            by_block(head_width),
            by_block(head_width),
            by_block(2 * head_width),
            by_block(HD),
            whole(head_width, 2),
            by_rows(model),
            by_rows(model),
            by_rows(patch),
            whole(*vectors.shape),
            whole(*first_mods.shape),
            whole(model, 4 * head_width),
            whole(model, patch),
            ANYWHERE,
            ANYWHERE,
        ],
        out_specs=[
            by_rows(4 * head_width),
            by_rows(patch),
            whole(patch, model),
            whole(tile_rows, model),
            whole(8, model),
            whole(head_width, 128),
        ],
        out_shape=[
            struct((tokens, 4 * head_width), bf16),
            struct((tokens, patch)),
            struct((patch, model)),
            struct((tile_rows, model)),
            struct((8, model)),
            struct((head_width, 128)),
        ],
        scratch_shapes=[
            pltpu.VMEM((4 * head_width, LANES), f32),
            pltpu.VMEM((LANES, model), f32),
            pltpu.VMEM((LANES, model), bf16),
        ],
        compiler_params=vmem,
        name="finish",
        cost_estimate=cost(13),
    )(
        grad_queries,
        grad_keys,
        grad_values,
        grad_cross,
        raw,
        tables,
        gains,
        embedded,
        part_residual,
        neighbours,
        vectors,
        first_mods,
        weight_qkvc,
        embedding_t,
        output_sum,
        got_gu,
    )

    grad_qkvc = dot(normed, grad_raw, 0, 0).astype(bf16)

    grad_cap = row_scatter(
        after(jnp.concatenate([grad_cap_keys, grad_cap_values], axis=0), grad_raw)
    ).astype(bf16)
    if sub_n > 1:
        grad_cap = lax.psum_scatter(grad_cap, "sub", scatter_dimension=0, tiled=True)
    cap_rows = 2 * head_width // (rows_n * sub_n)


    def place(vectors):
        return lax.dynamic_update_slice_in_dim(
            jnp.zeros((vectors.shape[0], model), f32), vectors, tp * head_width, 1
        )

    head_vectors = jnp.concatenate(
        [head_sums[:, 0:2], grad_gate_part[:, 0:1], jnp.zeros((head_width, 5), f32)], axis=1
    )
    small = jnp.concatenate(
        [
            bands(rows_first_scale),
            bands(rows_first_gate),
            bands(rows_second_scale),
            bands(rows_second_gate),
            grad_embedding,
            grad_unpatch,
            sums,
            grad_ff_gain,
            place(head_vectors.T),
        ],
        axis=0,
    ).astype(bf16)
    small_width = small.shape[0]
    small = small.reshape(small_width, rows_n, model // rows_n).transpose(1, 0, 2)
    small = small.reshape(rows_n * small_width, model // rows_n)
    small = row_scatter(small).astype(bf16)
    mods_rows = 4 * NBAND
    lanes = model // rows_n
    joint = jnp.concatenate(
        [grad_cap, small[:mods_rows].reshape(-1, text)], axis=0
    )
    joint = lax.all_gather(after(joint, grad_down_sum), ALL, axis=0)
    all_mods = joint[:, cap_rows:].astype(f32).reshape(rows_n, col_n, mods_rows, lanes)
    all_mods = jnp.sum(all_mods, axis=1).transpose(1, 0, 2).reshape(mods_rows, model)
    grad_cap = joint[:, :cap_rows]
    small = small[mods_rows:]
    small_width = small_width - mods_rows
    small = small.T
    if sub_n > 1:
        small = lax.psum_scatter(small, "sub", scatter_dimension=0, tiled=True)
    small = small.reshape(tp_n, owned, small_width)
    qkvc_width = 4 * head_width
    sent = scatter_rows(grad_qkvc).reshape(tp_n, owned, qkvc_width)
    sent = jnp.concatenate(
        [sent, output_sum.reshape(tp_n, owned, model), small, cells_out(first_cells, cells)], axis=2
    )
    got = swap(sent, "tp")
    grad_output = jnp.sum(got[:, :, qkvc_width : qkvc_width + model].astype(f32), axis=0)
    small_at = qkvc_width + model
    cells_at = small_at + small_width
    small = jnp.sum(got[:, :, small_at:cells_at].astype(f32), axis=0)
    both_cells = cells_in(got[:, :, cells_at:])
    prediction, latent_grad = both_cells[..., :channels], both_cells[..., channels:]
    copies = []
    for t in range(tp_n):
        for i in range(3):
            copies.append((0, t, i * head_width, 1, None, i * model + t * head_width, head_width))
        copies.append((0, t, 3 * head_width, 2, None, t * head_width, head_width))
    grad_projection, grad_cross_query = pack(
        copies,
        [
            jax.ShapeDtypeStruct((owned, 3 * model), f32),
            jax.ShapeDtypeStruct((owned, model), f32),
        ],
        got,
    )
    at = 2 * patch
    grad_embedding = small[:, :patch].T
    grad_unpatch = small[:, patch : 2 * patch]
    vectors = small[:, at:].T

    grad_cap = (
        grad_cap.reshape(rows_n, sub_n, tp_n, cap_rows, text)
        .transpose(2, 0, 1, 3, 4)
        .reshape(tp_n, 2, head_width, text)
        .transpose(1, 0, 2, 3)
        .reshape(2 * model, text)
    )
    cap_own = captions.shape[1] // all_n
    own_captions = lax.dynamic_slice_in_dim(captions, index * cap_own, cap_own, 1)
    grad_caption = dot(own_captions, grad_cap, 0, 1)

    grad_down = lax.ppermute(grad_down_sum, ALL, moves).astype(f32)
    own_band = lax.dynamic_slice_in_dim(full_band, index * owned, owned, 1)
    own_silu = jax.nn.silu(own_band)
    grad_adaptive = jnp.concatenate(
        [dot(own_silu, all_mods[i * NBAND : (i + 1) * NBAND], 0, 0, HIGH) for i in range(4)], axis=1
    )
    bias_own = 4 * owned
    totals = jnp.sum(all_mods.reshape(4, NBAND, model), axis=1).reshape(-1)
    grad_adaptive_bias = lax.dynamic_slice_in_dim(totals, index * bias_own, bias_own, 0)
    local_rows = my_quarter(adaptive)
    local_band = lax.dynamic_slice_in_dim(band_table, row * quarter, quarter, 1).astype(f32)
    grad_band = sum(
        dot(
            all_mods[i * NBAND : (i + 1) * NBAND],
            local_rows[:, i * model : (i + 1) * model].astype(f32),
            1,
            1,
            HIGH,
        )
        for i in range(4)
    ) * silu_slope(local_band)
    grad_band = lax.ppermute(grad_band, ALL, moves)

    return (
        prediction,
        latent_grad,
        grad_embedding,
        vectors[1],
        grad_band,
        grad_adaptive,
        grad_adaptive_bias,
        vectors[0],
        grad_projection,
        vectors[16],
        vectors[17],
        grad_cross_query,
        grad_caption,
        vectors[18],
        grad_output,
        vectors[8],
        grad_gate_weight,
        grad_up_weight,
        grad_down,
        grad_unpatch,
    )


def _mine(vector, tp, sub_n):
    if sub_n == 1:
        return vector
    size = vector.shape[0] * sub_n
    whole = lax.all_gather(vector, COL, axis=0, tiled=True)
    return lax.dynamic_slice_in_dim(whole, tp * size, size, 0)


def solution(mesh):
    rows_n, col_n = mesh.shape["row"], mesh.shape["col"]

    def run(*args):
        heads = args[5].shape[0] // HD
        tp_n = math.gcd(heads, col_n)
        split = Mesh(mesh.devices.reshape(rows_n, col_n // tp_n, tp_n), ALL)
        in_specs = (
            P("row", COL, None),
            P(),
            P(),
            P(),
            P(None, COL),
            P(COL),
            P(None, COL),
            P(COL, None),
            P(COL),
            P(COL),
            P(COL, None),
            P(COL),
            P(COL),
            P(COL, None),
            P(COL, None),
            P(COL),
            P(COL, None),
            P(COL),
            P(COL, None),
            P(COL, None),
            P(COL, None),
            P(COL, None),
            P("row", COL, None),
        )
        out_specs = (
            P("row", COL, None),
            P("row", COL, None),
            P(None, ALL),
            P(ALL),
            P(None, ALL),
            P(ALL, None),
            P(ALL),
            P(ALL),
            P(ALL, None),
            P(ALL),
            P(ALL),
            P(ALL, None),
            P(ALL, None),
            P(ALL),
            P(ALL, None),
            P(ALL),
            P(ALL, None),
            P(ALL, None),
            P(ALL, None),
            P(ALL, None),
        )
        return jax.shard_map(
            on_device, mesh=split, in_specs=in_specs, out_specs=out_specs, check_vma=False
        )(*args)

    return run
```

```python
import functools
import math

import jax
import jax.numpy as jnp
import numpy as np
from jax import lax
from jax.experimental import pallas as pl
from jax.experimental.pallas import tpu as pltpu
from jax.sharding import Mesh, PartitionSpec as P

HD = 64
NBAND = 8
MOSTH = 8
HALO = 8
LANES = 256

EPS = 1e-06
THETA = 10000.0
NEG = -1e30
HIGH = lax.Precision.HIGHEST
OFFSETS = ((-1, -1), (-1, 0), (-1, 1), (0, -1), (0, 0), (0, 1), (1, -1), (1, 0), (1, 1))
ALL = ("row", "sub", "tp")
COL = ("sub", "tp")
f32 = jnp.float32
bf16 = jnp.bfloat16


def spread_all(value, axes):
    count = lax.axis_size(axes)
    return lax.all_to_all(
        jnp.broadcast_to(value[None], (count,) + value.shape), axes, 0, 0, tiled=True
    )


def swap(value, axes):
    return lax.all_to_all(value, axes, 0, 0, tiled=True)


def nothing(*others):
    return sum(other[(0,) * other.ndim].astype(f32) * 0.0 for other in others)


def after(value, *others):
    return value + nothing(*others).astype(value.dtype)


def waits_for(kernel, at, count):
    def run(*refs):
        return kernel(*refs[:at], *refs[at + count :])

    return run


def cost(microseconds):
    return pl.CostEstimate(
        flops=int(microseconds * 1e9), bytes_accessed=int(microseconds * 3e6), transcendentals=0
    )


ANYWHERE = pl.BlockSpec(memory_space=pl.ANY)


def pairwise(value, flip):
    return lax.ppermute(value, "row", [(i, i ^ flip) for i in range(4)])


def row_gather(value):
    if lax.axis_size("row") != 4:
        return lax.all_gather(value, "row", axis=0)
    row = lax.axis_index("row")
    chip, core = row // 2, row % 2
    other = pairwise(value, 2)
    pair = jnp.stack([jnp.where(chip == 0, value, other), jnp.where(chip == 0, other, value)])
    far = pairwise(pair, 1)
    both = jnp.stack([jnp.where(core == 0, pair, far), jnp.where(core == 0, far, pair)], axis=1)
    return both.reshape((4,) + value.shape)


def row_scatter(value):
    count = lax.axis_size("row")
    if count != 4:
        return lax.psum_scatter(value, "row", scatter_dimension=0, tiled=True)
    row = lax.axis_index("row")
    chip, core = row // 2, row % 2
    parts = value.astype(bf16).reshape((2, 2, value.shape[0] // 4) + value.shape[1:])

    def pick(array, which, axis):
        return lax.dynamic_index_in_dim(array, which, axis, keepdims=False)

    near = pairwise(pick(parts, 1 - core, 1), 1)
    kept = (pick(parts, core, 1).astype(f32) + near.astype(f32)).astype(bf16)
    far = pairwise(pick(kept, 1 - chip, 0), 2)
    return pick(kept, chip, 0).astype(f32) + far.astype(f32)


def ring_of(count):
    return list(range(0, count, 2)) + list(range(count - 1, 0, -2))


def look_up(table, index):
    ids = jnp.arange(len(table))
    return jnp.sum(jnp.where(ids == index, jnp.asarray(table, jnp.int32), 0)).astype(jnp.int32)


def ring_steps(axis):
    count = lax.axis_size(axis)
    ring = ring_of(count)
    place = look_up([ring.index(i) for i in range(count)], lax.axis_index(axis))

    def member(step):
        return look_up(ring, lax.rem(place + (step + count), count))

    def onward(value):
        return lax.ppermute(value, axis, [(ring[i], ring[(i + 1) % count]) for i in range(count)])

    def back(value):
        return lax.ppermute(value, axis, [(ring[(i + 1) % count], ring[i]) for i in range(count)])

    return member, onward, back


def ring_gather(value, axis):
    count = lax.axis_size(axis)
    member, onward, back = ring_steps(axis)
    rows = value.shape[0]
    pieces, starts = [value], [member(0) * rows]
    right = left = value
    for step in range(1, count // 2):
        right, left = onward(right), back(left)
        pieces += [right, left]
        starts += [member(-step) * rows, member(step) * rows]
    half = rows // 2
    far = member(count // 2) * rows
    pieces += [onward(right[:half]), back(left[half:])]
    starts += [far, far + half]
    return pieces, jnp.stack(starts)


def ring_scatter(block, axis, beside):
    count = lax.axis_size(axis)
    member, onward, back = ring_steps(axis)
    beside, done = list(beside), []

    def step_on(right, left):
        held = (right, left)
        right, left = onward(right.astype(bf16)), back(left.astype(bf16))
        if beside:
            done.append(beside.pop(0)(held))
            right, left = after(right.astype(f32), *done[-1]), left.astype(f32)
        return right.astype(f32), left.astype(f32)

    far = block(member(count // 2)).astype(bf16)
    half = far.shape[0] // 2
    far_right, far_left = onward(far[:half]), back(far[half:])
    right = block(member(count // 2 - 1))
    left = block(member(1 - count // 2))
    right = jnp.concatenate([right[:half] + far_right.astype(f32), right[half:]], axis=0)
    left = jnp.concatenate([left[:half], left[half:] + far_left.astype(f32)], axis=0)
    for step in range(count // 2 - 2, 0, -1):
        right, left = step_on(right, left)
        right = right + block(member(step))
        left = left + block(member(-step))
    own = block(member(0))
    right, left = step_on(right, left)
    return right + left + own, done


def pack_kernel(copies, *refs):
    for source, source_lead, source_at, target, target_lead, target_at, size in copies:
        taken = slice(source_at, source_at + size)
        given = slice(target_at, target_at + size)
        value = refs[source][:, taken] if source_lead is None else refs[source][source_lead, :, taken]
        value = value.astype(refs[target].dtype)
        if target_lead is None:
            refs[target][:, given] = value
        else:
            refs[target][target_lead, :, given] = value


def pack(copies, out_shapes, *sources):
    return pl.pallas_call(
        functools.partial(pack_kernel, copies),
        out_shape=out_shapes,
        compiler_params=pltpu.CompilerParams(vmem_limit_bytes=48 * 2**20),
        name="pack",
        cost_estimate=cost(1),
    )(*sources)


def dot(left, right, left_dim, right_dim, precision=None):
    return lax.dot_general(
        left,
        right,
        (((left_dim,), (right_dim,)), ((), ())),
        precision=precision,
        preferred_element_type=f32,
    )


def shift(cells, axis, up):
    count = lax.axis_size(axis)
    pairs = [(i, i + 1) if up else (i + 1, i) for i in range(count - 1)]
    return lax.ppermute(cells, axis, pairs)


def silu_slope(values):
    sigmoid = jax.nn.sigmoid(values)
    return sigmoid * (1.0 + values * (1.0 - sigmoid))


def gather_cells(padded, row_count, col_count):
    return jnp.concatenate(
        [
            padded[1 + row_off : 1 + row_off + row_count, 1 + col_off : 1 + col_off + col_count]
            for row_off, col_off in OFFSETS
        ],
        axis=-1,
    )


def spread_cells(padded, row_count, col_count, channels):
    summed = jnp.zeros((row_count, col_count, channels), f32)
    for offset_index, (row_off, col_off) in enumerate(OFFSETS):
        summed = summed + padded[
            1 - row_off : 1 - row_off + row_count,
            1 - col_off : 1 - col_off + col_count,
            offset_index * channels : (offset_index + 1) * channels,
        ].astype(f32)
    return summed


def row_items(heights, band_ids, row_count):
    count = heights.shape[0]
    below = jnp.arange(count)[:, None] >= jnp.arange(count)[None, :]
    item_ends = jnp.sum(jnp.where(below, heights[None, :], 0), axis=1)
    row_ids = jnp.arange(row_count, dtype=jnp.int32)
    item_of_row = jnp.sum((item_ends[None, :] <= row_ids[:, None]).astype(jnp.int32), axis=1)
    picked = item_of_row[:, None] == jnp.arange(count, dtype=jnp.int32)[None, :]
    item_top = jnp.sum(jnp.where(picked, (item_ends - heights)[None, :], 0), axis=1)
    row_band = jnp.sum(jnp.where(picked, band_ids[None, :], 0), axis=1)
    band_onehot = (row_band[:, None] == jnp.arange(NBAND, dtype=jnp.int32)[None, :]).astype(f32)
    return (item_of_row, row_ids - item_top, band_onehot)


def tn(left, right):
    return dot(left, right, 0, 0)


def nt(left, right):
    return dot(left, right, 1, 1)


def nn(left, right):
    return dot(left, right, 1, 0)


def masked_scores(key_block, query_block, bias):
    return tn(key_block, query_block) + bias


def block_bias(items_ref, item_query, chunk, key_rows, width):
    rows = []
    for key_row in range(key_rows):
        item = items_ref[chunk * key_rows + key_row]
        rows.append(
            jnp.broadcast_to(jnp.where(item_query == item, 0.0, NEG), (width, item_query.shape[1]))
        )
    return rows[0] if len(rows) == 1 else jnp.concatenate(rows, axis=0)


def lay_out(block, near_ref, *parts):
    @pl.when(block == 0)
    def _():
        at = 0
        for part in parts:
            near_ref[:, at : at + part.shape[1]] = part[...]
            at += part.shape[1]


def attend_kernel(
    heads,
    key_rows,
    key_width,
    items_ref,
    low_ref,
    high_ref,
    item_query_ref,
    query_ref,
    above_ref,
    both_ref,
    below_ref,
    cross_ref,
    caption_key_ref,
    caption_value_ref,
    gate_ref,
    mixed_ref,
    self_ref,
    crossed_ref,
    stats_ref,
    total_ref,
    near_ref,
):
    block = pl.program_id(0)
    head_width = heads * HD
    lay_out(block, near_ref, above_ref, both_ref, below_ref)
    item_query = item_query_ref[0:1, :]
    self_ref[...] = jnp.zeros_like(self_ref)
    total_ref[...] = jnp.zeros_like(total_ref)

    def chunk_step(chunk, carry):
        lanes = pl.ds(pl.multiple_of(chunk * LANES, LANES), LANES)
        bias = block_bias(items_ref, item_query, chunk, key_rows, key_width)
        for head in range(heads):
            part = slice(head * HD, (head + 1) * HD)
            value_part = slice(head_width + head * HD, head_width + (head + 1) * HD)
            scores = masked_scores(near_ref[part, lanes], query_ref[part, :], bias)
            weights = jnp.exp(scores)
            total_ref[head : head + 1, :] += jnp.sum(weights, axis=0, keepdims=True)
            self_ref[part, :] += nn(near_ref[value_part, lanes], weights.astype(bf16))
        return carry

    lax.fori_loop(low_ref[block], high_ref[block], chunk_step, 0)
    stats_ref[...] = jnp.zeros_like(stats_ref)
    for head in range(heads):
        part = slice(head * HD, (head + 1) * HD)
        total = total_ref[head : head + 1, :]
        attended = self_ref[part, :] / total
        self_ref[part, :] = attended
        stats_ref[head : head + 1, :] = jnp.log(total)
        scores = tn(caption_key_ref[part, :], cross_ref[part, :])
        best = jnp.max(scores, axis=0, keepdims=True)
        weights = jnp.exp(scores - best)
        total = jnp.sum(weights, axis=0, keepdims=True)
        crossed = nn(caption_value_ref[part, :], (weights / total).astype(bf16))
        crossed_ref[part, :] = crossed
        stats_ref[heads + head : heads + head + 1, :] = best + jnp.log(total)
        mixed_ref[part, :] = (attended + gate_ref[part, 0:1] * crossed).astype(bf16)


def cross_back_kernel(
    heads,
    cross_ref,
    caption_key_ref,
    caption_value_ref,
    gate_ref,
    grad_ref,
    crossed_ref,
    stats_ref,
    grad_cross_ref,
    grad_key_ref,
    grad_value_ref,
    grad_gate_ref,
):
    @pl.when(pl.program_id(0) == 0)
    def _():
        grad_key_ref[...] = jnp.zeros_like(grad_key_ref)
        grad_value_ref[...] = jnp.zeros_like(grad_value_ref)
        grad_gate_ref[...] = jnp.zeros_like(grad_gate_ref)

    for head in range(heads):
        part = slice(head * HD, (head + 1) * HD)
        gate = gate_ref[part, 0:1]
        grad_wide = grad_ref[part, :].astype(f32)
        grad_crossed = (gate * grad_wide).astype(bf16)
        grad_gate_ref[part, 0:1] += jnp.sum(
            grad_wide * crossed_ref[part, :], axis=1, keepdims=True
        ) * (1.0 - gate * gate)
        scores = tn(caption_key_ref[part, :], cross_ref[part, :])
        weights = jnp.exp(scores - stats_ref[heads + head : heads + head + 1, :])
        grad_weights = tn(caption_value_ref[part, :], grad_crossed)
        delta = jnp.sum(weights * grad_weights, axis=0, keepdims=True)
        grad_scores = (weights * (grad_weights - delta)).astype(bf16)
        grad_cross_ref[part, :] = (
            nn(caption_key_ref[part, :], grad_scores) * (1.0 / math.sqrt(HD))
        ).astype(bf16)
        grad_key_ref[part, :] += nt(cross_ref[part, :], grad_scores)
        grad_value_ref[part, :] += nt(grad_crossed, weights.astype(bf16))


def attend_back_kernel(
    heads,
    key_rows,
    key_width,
    items_ref,
    low_ref,
    high_ref,
    item_query_ref,
    query_ref,
    above_ref,
    both_ref,
    below_ref,
    grad_ref,
    self_ref,
    stats_ref,
    grad_query_ref,
    grad_both_ref,
    delta_ref,
    near_ref,
):
    block = pl.program_id(0)
    head_width = heads * HD
    lay_out(block, near_ref, above_ref, both_ref, below_ref)

    @pl.when(block == 0)
    def _():
        grad_both_ref[...] = jnp.zeros_like(grad_both_ref)

    item_query = item_query_ref[0:1, :]
    grad_query_ref[...] = jnp.zeros_like(grad_query_ref)
    for head in range(heads):
        part = slice(head * HD, (head + 1) * HD)
        delta_ref[head : head + 1, :] = jnp.sum(
            grad_ref[part, :].astype(f32) * self_ref[part, :], axis=0, keepdims=True
        )

    def chunk_step(chunk, carry):
        lanes = pl.ds(pl.multiple_of(chunk * LANES, LANES), LANES)
        bias = block_bias(items_ref, item_query, chunk, key_rows, key_width)
        for head in range(heads):
            part = slice(head * HD, (head + 1) * HD)
            value_part = slice(head_width + head * HD, head_width + (head + 1) * HD)
            key_block = near_ref[part, lanes]
            query_block = query_ref[part, :]
            grad_block = grad_ref[part, :]
            scores = masked_scores(key_block, query_block, bias)
            weights = jnp.exp(scores - stats_ref[head : head + 1, :])
            grad_weights = tn(near_ref[value_part, lanes], grad_block)
            grad_scores = (weights * (grad_weights - delta_ref[head : head + 1, :])).astype(bf16)
            grad_query_ref[part, :] += nn(key_block, grad_scores)
            grad_both_ref[part, lanes] += nt(query_block, grad_scores)
            grad_both_ref[value_part, lanes] += nt(grad_block, weights.astype(bf16))
        return carry

    lax.fori_loop(low_ref[block], high_ref[block], chunk_step, 0)


def turn(values, tables):
    quarter = HD // 4
    first, second, third, fourth = (values[i * quarter : (i + 1) * quarter] for i in range(4))
    cos_rows, sin_rows, cos_cols, sin_cols = (
        tables[i * quarter : (i + 1) * quarter] for i in range(4)
    )
    return jnp.concatenate(
        [
            first * cos_rows - second * sin_rows,
            first * sin_rows + second * cos_rows,
            third * cos_cols - fourth * sin_cols,
            third * sin_cols + fourth * cos_cols,
        ],
        axis=0,
    )


def turn_back(values, tables):
    quarter = HD // 4
    first, second, third, fourth = (values[i * quarter : (i + 1) * quarter] for i in range(4))
    cos_rows, sin_rows, cos_cols, sin_cols = (
        tables[i * quarter : (i + 1) * quarter] for i in range(4)
    )
    return jnp.concatenate(
        [
            first * cos_rows + second * sin_rows,
            second * cos_rows - first * sin_rows,
            third * cos_cols + fourth * sin_cols,
            fourth * cos_cols - third * sin_cols,
        ],
        axis=0,
    )


def mean_inverse(values, axis):
    return lax.rsqrt(jnp.mean(values * values, axis=axis, keepdims=True) + EPS)


def project_kernel(
    heads,
    span,
    near_ref,
    embed_ref,
    vector_ref,
    mod_ref,
    weight_ref,
    table_ref,
    gain_ref,
    embedded_ref,
    normed_ref,
    raw_ref,
    query_ref,
    both_ref,
    cross_ref,
):
    block = pl.program_id(0)
    model = embed_ref.shape[0]
    head_width = heads * HD
    embedded_ref[...] = nt(near_ref[...], embed_ref[...]) + vector_ref[0:1, :]
    for j in range(LANES // span):
        rows = slice(j * span, (j + 1) * span)
        embedded = embedded_ref[rows, :]
        scale = mod_ref[pl.ds(block * (LANES // span) + j, 1), 0:model]
        factor = vector_ref[1:2, :] * (1.0 + scale)
        normed_ref[rows, :] = (embedded * mean_inverse(embedded, -1) * factor).astype(bf16)
    raw = nn(normed_ref[...], weight_ref[...]).astype(bf16).astype(f32).T
    tables = table_ref[...]
    score_scale = 1.0 / math.sqrt(HD)
    raw_ref[...] = raw[0 : 2 * head_width].astype(bf16)
    for head in range(heads):
        part = slice(head * HD, (head + 1) * HD)
        query = raw[part]
        query = turn(query * mean_inverse(query, 0) * gain_ref[part, 0:1], tables)
        query_ref[part, :] = (query.astype(bf16).astype(f32) * score_scale).astype(bf16)
        key = raw[head_width + head * HD : head_width + (head + 1) * HD]
        key = turn(key * mean_inverse(key, 0) * gain_ref[part, 1:2], tables)
        both_ref[part, :] = key.astype(bf16)
    both_ref[head_width:, :] = raw[2 * head_width : 3 * head_width].astype(bf16)
    cross_ref[...] = (raw[3 * head_width :] * score_scale).astype(bf16)


def middle_kernel(
    pieces,
    span,
    own_ref,
    place_ref,
    *refs,
):
    mixed_refs, refs = refs[:pieces], refs[pieces:]
    (
        embedded_ref,
        patch_ref,
        vector_ref,
        mod_ref,
        output_ref,
        gu_ref,
        down_ref,
        unpatch_ref,
        mixed_ref,
        residual_ref,
        inner_ref,
        hidden_ref,
        grad_feed_ref,
        grad_gu_ref,
        part_residual_ref,
        part_branch_ref,
        grad_mixed_ref,
        scale_rows_ref,
        gate_rows_ref,
        gain_ref,
        branch_ref,
        grad_inner_ref,
    ) = refs
    block = pl.program_id(0)
    row_count = LANES // span
    model = embedded_ref.shape[1]
    groups = output_ref.shape[0]
    group = model // groups
    ff_mine = down_ref.shape[0]

    @pl.when(block == 0)
    def _():
        gain_ref[...] = jnp.zeros_like(gain_ref)

    for i, ref in enumerate(mixed_refs):
        size = ref.shape[0]
        mixed_ref[pl.ds(pl.multiple_of(place_ref[i], 32), size), :] = ref[...]
    for g in range(groups):
        branch_ref[:, g * group : (g + 1) * group] = tn(mixed_ref[...], output_ref[g])
    ff_gain = vector_ref[2:3, :]

    def mods(j, which):
        return mod_ref[
            pl.ds(block * row_count + j, 1), which * model : (which + 1) * model
        ]

    for j in range(row_count):
        rows = slice(j * span, (j + 1) * span)
        residual = embedded_ref[rows, :] + jnp.tanh(mods(j, 1)) * branch_ref[rows, :]
        residual_ref[rows, :] = residual
        factor = ff_gain * (1.0 + mods(j, 2))
        inner_ref[rows, :] = (residual * mean_inverse(residual, -1) * factor).astype(bf16)
    inner = inner_ref[...]
    ff_groups = gu_ref.shape[0]
    ff_group = 2 * ff_mine // ff_groups
    half = ff_groups // 2
    grad_inner_ref[...] = nt(patch_ref[...], unpatch_ref[...])
    for j in range(row_count):
        rows = slice(j * span, (j + 1) * span)
        grad_feed_ref[rows, :] = (jnp.tanh(mods(j, 3)) * grad_inner_ref[rows, :]).astype(bf16)
    grad_hidden = nt(grad_feed_ref[...], down_ref[...])
    for g in range(half):
        gate = nn(inner, gu_ref[g])
        upward = nn(inner, gu_ref[half + g])
        sigmoid = jax.nn.sigmoid(gate)
        silu = gate * sigmoid
        cols = slice(g * ff_group, (g + 1) * ff_group)
        hidden_ref[:, cols] = (silu * upward).astype(bf16)
        grad = grad_hidden[:, cols]
        grad_gu_ref[:, cols] = (
            grad * upward * (sigmoid * (1.0 + gate * (1.0 - sigmoid)))
        ).astype(bf16)
        grad_gu_ref[:, ff_mine + g * ff_group : ff_mine + (g + 1) * ff_group] = (
            grad * silu
        ).astype(bf16)
    own_column = lax.broadcasted_iota(jnp.int32, (span, 1), 0)
    mine = (own_column >= own_ref[0]) & (own_column < own_ref[1])
    for j in range(row_count):
        rows = slice(j * span, (j + 1) * span)
        part_residual_ref[rows, :] = jnp.where(mine, grad_inner_ref[rows, :], 0.0)
    total = nt(grad_gu_ref[:, 0:ff_group], gu_ref[0])
    for g in range(1, ff_groups):
        total = total + nt(grad_gu_ref[:, g * ff_group : (g + 1) * ff_group], gu_ref[g])
    grad_inner_ref[...] = total
    for j in range(row_count):
        rows = slice(j * span, (j + 1) * span)
        tanh_one = jnp.tanh(mods(j, 1))
        second_scale = mods(j, 2)
        residual = residual_ref[rows, :]
        inverse = mean_inverse(residual, -1)
        unit = residual * inverse
        grad_inner = grad_inner_ref[rows, :]
        summed = jnp.sum(grad_inner * unit, axis=0, keepdims=True)
        scale_rows_ref[pl.ds(block * row_count + j, 1), :] = summed * ff_gain
        gain_ref[0:1, :] += summed * (1.0 + second_scale)
        grad_unit = grad_inner * (ff_gain * (1.0 + second_scale))
        part = part_residual_ref[rows, :] + inverse * (
            grad_unit - unit * jnp.mean(grad_unit * unit, axis=-1, keepdims=True)
        )
        part_residual_ref[rows, :] = part
        part_branch_ref[rows, :] = (tanh_one * part).astype(bf16)
        gate_rows_ref[pl.ds(block * row_count + j, 1), :] = jnp.sum(
            part * branch_ref[rows, :], axis=0, keepdims=True
        ) * (1.0 - tanh_one * tanh_one)
    total = nt(output_ref[0], part_branch_ref[:, 0:group])
    for g in range(1, groups):
        total = total + nt(output_ref[g], part_branch_ref[:, g * group : (g + 1) * group])
    grad_mixed_ref[...] = total.astype(bf16)


def result_kernel(
    span,
    own_ref,
    hidden_ref,
    residual_ref,
    patch_ref,
    mod_ref,
    down_ref,
    unpatch_ref,
    cells_ref,
    grad_unpatch_ref,
    gate_rows_ref,
    feed_ref,
    grad_ref,
    result_ref,
):
    block = pl.program_id(0)
    row_count = LANES // span
    model = residual_ref.shape[1]

    @pl.when(block == 0)
    def _():
        grad_unpatch_ref[...] = jnp.zeros_like(grad_unpatch_ref)

    feed_ref[...] = nn(hidden_ref[...], down_ref[...])
    grad_ref[...] = nt(patch_ref[...], unpatch_ref[...])
    own_column = lax.broadcasted_iota(jnp.int32, (span, 1), 0)
    mine = (own_column >= own_ref[0]) & (own_column < own_ref[1])
    for j in range(row_count):
        rows = slice(j * span, (j + 1) * span)
        tanh_two = jnp.tanh(mod_ref[pl.ds(block * row_count + j, 1), 3 * model : 4 * model])
        feed = feed_ref[rows, :]
        result_ref[rows, :] = (
            jnp.where(mine, residual_ref[rows, :], 0.0) + tanh_two * feed
        ).astype(bf16)
        gate_rows_ref[pl.ds(block * row_count + j, 1), :] = jnp.sum(
            grad_ref[rows, :] * feed, axis=0, keepdims=True
        ) * (1.0 - tanh_two * tanh_two)
    cells_ref[...] = nn(result_ref[...], unpatch_ref[...])
    grad_unpatch_ref[...] += tn(patch_ref[...], result_ref[...])


def finish_kernel(
    heads,
    span,
    grad_query_ref,
    grad_key_ref,
    grad_value_ref,
    grad_cross_ref,
    raw_ref,
    table_ref,
    gain_ref,
    embedded_ref,
    part_residual_ref,
    near_ref,
    vector_ref,
    mod_ref,
    weight_ref,
    embed_ref,
    grad_raw_ref,
    cells_ref,
    grad_embed_ref,
    scale_rows_ref,
    sums_ref,
    head_sums_ref,
    turned_ref,
    grad_normed_ref,
    part_ref,
):
    block = pl.program_id(0)
    row_count = LANES // span
    model = embedded_ref.shape[1]
    head_width = heads * HD
    score_scale = 1.0 / math.sqrt(HD)

    @pl.when(block == 0)
    def _():
        grad_embed_ref[...] = jnp.zeros_like(grad_embed_ref)
        sums_ref[...] = jnp.zeros_like(sums_ref)
        head_sums_ref[...] = jnp.zeros_like(head_sums_ref)

    tables = table_ref[...]
    for which in range(2):
        for head in range(heads):
            part = slice(head * HD, (head + 1) * HD)
            if which == 0:
                grad = (grad_query_ref[part, :] * score_scale).astype(bf16).astype(f32)
            else:
                grad = grad_key_ref[part, :].astype(bf16).astype(f32)
            at = which * head_width + head * HD
            raw = raw_ref[at : at + HD, :].astype(f32)
            grad = turn_back(grad, tables)
            inverse = mean_inverse(raw, 0)
            unit = raw * inverse
            head_sums_ref[part, which : which + 1] += jnp.sum(grad * unit, axis=1, keepdims=True)
            grad = grad * gain_ref[part, which : which + 1]
            turned_ref[at : at + HD, :] = inverse * (
                grad - unit * jnp.mean(grad * unit, axis=0, keepdims=True)
            )
    turned_ref[2 * head_width : 3 * head_width, :] = grad_value_ref[...].astype(f32)
    turned_ref[3 * head_width :, :] = grad_cross_ref[...].astype(f32)
    grad_raw_ref[...] = turned_ref[...].T.astype(bf16)
    grad_normed_ref[...] = nt(grad_raw_ref[...], weight_ref[...])
    gain = vector_ref[1:2, :]
    for j in range(row_count):
        rows = slice(j * span, (j + 1) * span)
        scale = mod_ref[pl.ds(block * row_count + j, 1), 0:model]
        embedded = embedded_ref[rows, :]
        inverse = mean_inverse(embedded, -1)
        unit = embedded * inverse
        grad_normed = grad_normed_ref[rows, :]
        summed = jnp.sum(grad_normed * unit, axis=0, keepdims=True)
        scale_rows_ref[pl.ds(block * row_count + j, 1), :] = summed * gain
        sums_ref[0:1, :] += summed * (1.0 + scale)
        grad_unit = grad_normed * (gain * (1.0 + scale))
        part = part_residual_ref[rows, :] + inverse * (
            grad_unit - unit * jnp.mean(grad_unit * unit, axis=-1, keepdims=True)
        )
        part = part.astype(bf16)
        part_ref[rows, :] = part
        sums_ref[1:2, :] += jnp.sum(part.astype(f32), axis=0, keepdims=True)
    cells_ref[...] = nn(part_ref[...], embed_ref[...])
    grad_embed_ref[...] += tn(near_ref[...], part_ref[...])


def on_device(
    latents,
    captions,
    item_heights,
    item_bands,
    embedding,
    embed_bias,
    band_table,
    adaptive,
    adaptive_bias,
    attention_gain,
    projection,
    query_gain,
    key_gain,
    cross_query,
    caption_weight,
    cross_gate,
    output_weight,
    feedforward_gain,
    gate_weight,
    up_weight,
    down_weight,
    unpatch_weight,
    cotangent,
):
    rows_n, sub_n, tp_n = (lax.axis_size(a) for a in ALL)
    col_n = sub_n * tp_n
    all_n = rows_n * col_n
    row = lax.axis_index("row")
    sub = lax.axis_index("sub")
    tp = lax.axis_index("tp")
    tile_rows, tile_cols, channels = latents.shape
    grid_rows = tile_rows * rows_n
    grid_cols = tile_cols * col_n
    span = tile_cols * tp_n
    tokens = tile_rows * span
    own = tile_rows * tile_cols
    width = embed_bias.shape[0]
    model = width * col_n
    head_width = model // tp_n
    heads = head_width // HD
    owned = model // all_n
    quarter = width // rows_n
    ff = gate_weight.shape[1]
    ff_part = ff // col_n
    ff_mine = ff // tp_n
    text = captions.shape[0]
    patch = 9 * channels

    index = (row * sub_n + sub) * tp_n + tp
    col = sub * tp_n + tp

    def to_peers(piece):
        spread = jnp.broadcast_to(piece[None], (sub_n,) + piece.shape)
        return spread.reshape((col_n,) + piece.shape[1:])

    def share(pieces):
        whole = row_gather(pieces)
        return whole.transpose(1, 0, 2, 3).reshape(model, pieces.shape[2])

    def my_quarter(weight):
        return lax.dynamic_slice_in_dim(weight, row * quarter, quarter, 0)

    copies = []
    for t in range(tp_n):
        for i in range(3):
            copies.append((0, None, i * model + t * head_width, 2, t, i * head_width, head_width))
        copies.append((1, None, t * head_width, 2, t, 3 * head_width, head_width))
    qkvc_piece = pack(
        copies,
        jax.ShapeDtypeStruct((tp_n, quarter, 4 * head_width), bf16),
        my_quarter(projection),
        my_quarter(cross_query),
    )
    tiles = jnp.concatenate([latents, cotangent], axis=-1).reshape(-1, 128)
    tiles_width = -(-tiles.shape[0] // quarter) * 128
    tiles = jnp.pad(tiles, ((0, quarter * tiles_width // 128 - tiles.shape[0]), (0, 0)))
    tiles = tiles.reshape(tiles_width // 128, quarter, 128).transpose(1, 0, 2)
    tiles = jnp.broadcast_to(tiles.reshape(1, quarter, tiles_width), (tp_n, quarter, tiles_width))
    qkvc_pieces = swap(to_peers(jnp.concatenate([qkvc_piece, tiles], axis=2)), COL)
    weight_qkvc = share(qkvc_pieces[:, :, : 4 * head_width])
    tiles = qkvc_pieces[:, :, 4 * head_width :].reshape(col_n, quarter, tiles_width // 128, 128)
    tiles = tiles.transpose(0, 2, 1, 3).reshape(col_n, -1, 128)
    tiles = tiles[:, : own * 2 * channels // 128].reshape(
        col_n, tile_rows, tile_cols, 2 * channels
    )
    grid = tiles.transpose(1, 0, 2, 3).reshape(tile_rows, grid_cols, 2 * channels)
    grid = jnp.concatenate(
        [
            shift(grid[tile_rows - 1 :], "row", True),
            grid,
            shift(grid[:1], "row", False),
        ],
        axis=0,
    )
    grid = jnp.pad(grid, ((0, 0), (1, 1), (0, 0)))
    bordered = lax.dynamic_slice_in_dim(grid, sub * span, span + 2, 1)
    neighbours = gather_cells(bordered[..., 0:channels], tile_rows, span).reshape(tokens, patch)
    patch_grads = gather_cells(bordered[..., channels : 2 * channels], tile_rows, span)
    patch_grads = patch_grads.reshape(tokens, patch)

    mod_width = adaptive.shape[1] // rows_n
    mod_bias = lax.dynamic_update_slice_in_dim(
        jnp.zeros((adaptive.shape[1],), f32), adaptive_bias.astype(f32), col * adaptive_bias.shape[0], 0
    )
    silu_band = jax.nn.silu(band_table.astype(f32))

    def mod_columns(start, count):
        return (
            jnp.dot(
                silu_band,
                lax.dynamic_slice_in_dim(adaptive, start, count, 1).astype(f32),
                precision=HIGH,
            )
            + lax.dynamic_slice_in_dim(mod_bias, start, count, 0)
        ).astype(bf16)

    columns = jnp.concatenate(
        [
            embedding.T,
            embed_bias[:, None],
            attention_gain[:, None],
            feedforward_gain[:, None],
            band_table.T,
            mod_columns(row * mod_width, mod_width).T.reshape(width, -1),
        ],
        axis=1,
    )
    columns_n = columns.shape[1]
    wide = -(-columns_n // 128) * 128
    columns = jnp.pad(columns, ((0, 0), (0, wide - columns_n)))

    def in_quarters(array):
        parts = array.reshape(-1, quarter, array.shape[1])
        return parts.transpose(1, 0, 2).reshape(quarter, -1)

    def from_quarters(array, columns_each):
        parts = array.reshape(array.shape[:-1] + (-1, columns_each))
        parts = jnp.moveaxis(parts, -2, -3)
        return parts.reshape(parts.shape[:-3] + (-1, columns_each))

    text_part = text // rows_n
    cap_part = jnp.dot(
        lax.dynamic_slice(
            captions,
            (row * text_part, col * caption_weight.shape[0]),
            (text_part, caption_weight.shape[0]),
        ),
        caption_weight,
        preferred_element_type=f32,
    )
    copies = []
    for t in range(tp_n):
        for i in range(2):
            copies.append((0, None, i * model + t * head_width, 1, t, i * head_width, head_width))
    cap_part = pack(
        copies, jax.ShapeDtypeStruct((tp_n, text_part, 2 * head_width), bf16), cap_part
    )
    cap_lanes = 2 * head_width // 128
    cap_part = (
        cap_part.reshape(tp_n, text_part, cap_lanes, 128)
        .transpose(0, 2, 1, 3)
        .reshape(tp_n, -1, quarter, 128)
        .transpose(0, 2, 1, 3)
        .reshape(tp_n, quarter, -1)
    )
    same = jnp.concatenate(
        [in_quarters(columns), in_quarters(mod_columns(0, model).reshape(-1, 256))], axis=1
    )
    same_width = same.shape[1]
    sent = jnp.concatenate(
        [jnp.broadcast_to(same[None], (tp_n,) + same.shape), cap_part], axis=2
    )
    got = swap(to_peers(after(sent, qkvc_pieces)), COL)
    columns = from_quarters(got[:, :, : rows_n * wide], wide).reshape(model, wide)
    embedding_t = columns[:, 0:patch]
    at = patch + 3 + NBAND
    vectors = columns[:, patch:at].T.astype(f32)
    full_band = vectors[3:]
    first_scale = jnp.sum(got[:, :, rows_n * wide : same_width].astype(f32), axis=0)
    first_scale = from_quarters(first_scale, 256).reshape(NBAND, model)
    item_of_row, row_place, band_onehot = row_items(item_heights, item_bands, grid_rows)
    tile_onehot = lax.dynamic_slice_in_dim(band_onehot, row * tile_rows, tile_rows, 0)
    first_mods = jnp.dot(
        tile_onehot, after(first_scale, weight_qkvc, neighbours), precision=HIGH
    )
    mod_part = columns[:, at:columns_n].reshape(col_n, width, -1)
    mod_part = jnp.sum(mod_part.astype(f32), axis=0).reshape(mod_width, NBAND).T
    cap_part = jnp.sum(got[:, :, same_width:].astype(f32), axis=0).astype(bf16)

    output_width = model // rows_n
    output_piece = lax.dynamic_slice_in_dim(output_weight, row * output_width, output_width, 1)
    output_piece = lax.all_gather(output_piece, COL, axis=0, tiled=True)
    full_output = lax.all_gather(output_piece, "row", axis=0)

    shared_mods = NBAND * mod_width // quarter
    shared = row_gather(
        jnp.concatenate([in_quarters(mod_part.reshape(-1, 256).astype(bf16)), cap_part], axis=1)
    )
    caption_heads = (
        from_quarters(shared[:, :, shared_mods:], 128)
        .reshape(rows_n, cap_lanes, text_part, 128)
        .transpose(1, 3, 0, 2)
        .reshape(2 * head_width, text)
    )
    caption_keys = caption_heads[:head_width]
    caption_values = caption_heads[head_width:]

    frequency = THETA ** (-jnp.arange(HD // 4, dtype=f32) / (HD // 4))
    tile_place = lax.dynamic_slice_in_dim(row_place, row * tile_rows, tile_rows, 0)
    row_angles = frequency[:, None] * jnp.repeat(tile_place, span).astype(f32)[None, :]
    col_place = sub * span + jnp.tile(jnp.arange(span), tile_rows)
    col_angles = frequency[:, None] * col_place.astype(f32)[None, :]
    tables = jnp.concatenate(
        [jnp.cos(row_angles), jnp.sin(row_angles), jnp.cos(col_angles), jnp.sin(col_angles)],
        axis=0,
    )
    gate_column = jnp.tanh(_mine(cross_gate, tp, sub_n).astype(f32))[:, None]
    gains = jnp.stack(
        [_mine(query_gain, tp, sub_n).astype(f32), _mine(key_gain, tp, sub_n).astype(f32)], axis=1
    )
    blocks = tokens // LANES

    def by_block(count):
        return pl.BlockSpec((count, LANES), lambda i, *_: (0, i))

    def by_rows(count):
        return pl.BlockSpec((LANES, count), lambda i, *_: (i, 0))

    def whole(*shape):
        return pl.BlockSpec(shape, lambda i, *_: (0,) * len(shape))

    def struct(shape, dtype=f32):
        return jax.ShapeDtypeStruct(shape, dtype)

    vmem = pltpu.CompilerParams(vmem_limit_bytes=56 * 2**20)
    embedded, normed, raw, queries, both, raw_cross = pl.pallas_call(
        functools.partial(project_kernel, heads, span),
        grid=(blocks,),
        in_specs=[
            by_rows(patch),
            whole(model, patch),
            whole(*vectors.shape),
            whole(*first_mods.shape),
            whole(model, 4 * head_width),
            by_block(HD),
            whole(head_width, 2),
        ],
        out_specs=[
            by_rows(model),
            by_rows(model),
            by_block(2 * head_width),
            by_block(head_width),
            by_block(2 * head_width),
            by_block(head_width),
        ],
        out_shape=[
            struct((tokens, model)),
            struct((tokens, model), bf16),
            struct((2 * head_width, tokens), bf16),
            struct((head_width, tokens), bf16),
            struct((2 * head_width, tokens), bf16),
            struct((head_width, tokens), bf16),
        ],
        compiler_params=vmem,
        name="project",
        cost_estimate=cost(10),
    )(neighbours, embedding_t, vectors, first_mods, weight_qkvc, tables, gains)
    modulations = (
        from_quarters(shared[:, :, :shared_mods], 256)
        .reshape(rows_n, NBAND, mod_width)
        .transpose(1, 0, 2)
        .reshape(NBAND, adaptive.shape[1])
        .astype(f32)
    )
    mods = jnp.dot(tile_onehot, modulations, precision=HIGH)

    gu_width = 2 * ff_mine // rows_n
    which_half = rows_n // 2
    gu_source = jnp.where(row < which_half, gate_weight, up_weight)
    gu_piece = lax.dynamic_slice_in_dim(
        gu_source.reshape(width, sub_n, tp_n, which_half, ff_part // which_half),
        lax.rem(row, which_half),
        1,
        3,
    )
    gu_piece = gu_piece.transpose(2, 0, 1, 3, 4).reshape(tp_n, width, gu_width)
    unpatch_piece = jnp.pad(my_quarter(unpatch_weight), ((0, 0), (0, gu_width - patch)))
    gu_piece = jnp.concatenate(
        [gu_piece, jnp.broadcast_to(unpatch_piece[None], (tp_n,) + unpatch_piece.shape)], axis=1
    )
    gu_pieces = swap(to_peers(after(gu_piece, queries)), COL)
    down_mine = down_weight
    if sub_n > 1:
        down_mine = lax.all_gather(down_weight, "sub", axis=0, tiled=True)

    if sub_n > 1:
        both = (
            lax.all_gather(both, "sub", axis=0)
            .reshape(sub_n, 2 * head_width, tile_rows, span)
            .transpose(1, 2, 0, 3)
            .reshape(2 * head_width, tile_rows * grid_cols)
        )
    edge = HALO * grid_cols
    middle_cols = both.shape[1]
    above = shift(both[:, middle_cols - edge :], "row", True)
    below = shift(both[:, :edge], "row", False)

    near_rows = tile_rows + 2 * HALO
    key_rows = max(1, LANES // grid_cols)
    key_width = LANES // key_rows
    block_rows = LANES // span
    items_padded = jnp.concatenate(
        [
            jnp.full((HALO,), -1, jnp.int32),
            item_of_row.astype(jnp.int32),
            jnp.full((HALO,), item_heights.shape[0] + 1, jnp.int32),
        ]
    )
    items_near = lax.dynamic_slice_in_dim(items_padded, row * tile_rows, near_rows, 0)
    item_query = jnp.repeat(items_near[HALO : HALO + tile_rows], span)[None, :]
    chunk_items = jnp.repeat(items_near, grid_cols // (key_width)).reshape(-1, key_rows)
    query_items = items_near[HALO : HALO + tile_rows].reshape(blocks, block_rows)
    before = chunk_items[None, :, -1] < query_items[:, None, 0]
    reached = chunk_items[None, :, 0] <= query_items[:, None, -1]
    low = jnp.sum(before.astype(jnp.int32), axis=1)
    high = jnp.sum(reached.astype(jnp.int32), axis=1)
    chunk_items = chunk_items.reshape(-1)
    near = near_rows * grid_cols

    mixed, self_out, crossed, stats = pl.pallas_call(
        waits_for(functools.partial(attend_kernel, heads, key_rows, key_width), 12, 2),
        grid_spec=pltpu.PrefetchScalarGridSpec(
            num_scalar_prefetch=3,
            grid=(blocks,),
            in_specs=[
                by_block(1),
                by_block(head_width),
                whole(2 * head_width, edge),
                whole(2 * head_width, middle_cols),
                whole(2 * head_width, edge),
                by_block(head_width),
                whole(head_width, text),
                whole(head_width, text),
                whole(head_width, 1),
                ANYWHERE,
                ANYWHERE,
            ],
            out_specs=[by_block(head_width), by_block(head_width), by_block(head_width), by_block(8)],
            scratch_shapes=[
                pltpu.VMEM((8, LANES), f32),
                pltpu.VMEM((2 * head_width, near), bf16),
            ],
        ),
        out_shape=[
            jax.ShapeDtypeStruct((head_width, tokens), bf16),
            jax.ShapeDtypeStruct((head_width, tokens), f32),
            jax.ShapeDtypeStruct((head_width, tokens), f32),
            jax.ShapeDtypeStruct((8, tokens), f32),
        ],
        compiler_params=vmem,
        name="attend",
        cost_estimate=cost(14),
    )(
        chunk_items,
        low,
        high,
        item_query,
        queries,
        above,
        both,
        below,
        raw_cross,
        caption_keys,
        caption_values,
        gate_column,
        mods,
        patch_grads,
    )

    weight_gu = lax.all_gather(after(gu_pieces, mixed, full_output), "row", axis=0)
    full_unpatch = weight_gu[:, :, width:, :patch].transpose(1, 0, 2, 3).reshape(model, patch)
    weight_gu = weight_gu[:, :, :width].reshape(rows_n, model, gu_width)
    pieces, starts = ring_gather(mixed, "tp")
    own_span = jnp.stack([tp * tile_cols, (tp + 1) * tile_cols]).astype(jnp.int32)
    (
        mixed_all,
        residual,
        inner,
        hidden,
        grad_feed,
        grad_gu,
        part_residual,
        part_branch,
        grad_mixed,
        rows_second_scale,
        rows_first_gate,
        grad_ff_gain,
    ) = pl.pallas_call(
        functools.partial(middle_kernel, len(pieces), span),
        grid_spec=pltpu.PrefetchScalarGridSpec(
            num_scalar_prefetch=2,
            grid=(blocks,),
            in_specs=[by_block(piece.shape[0]) for piece in pieces]
            + [
                by_rows(model),
                by_rows(patch),
                whole(*vectors.shape),
                whole(*mods.shape),
                whole(*full_output.shape),
                whole(*weight_gu.shape),
                whole(*down_mine.shape),
                whole(model, patch),
            ],
            out_specs=[
                by_block(model),
                by_rows(model),
                by_rows(model),
                by_rows(ff_mine),
                by_rows(model),
                by_rows(2 * ff_mine),
                by_rows(model),
                by_rows(model),
                by_block(model),
                whole(tile_rows, model),
                whole(tile_rows, model),
                whole(8, model),
            ],
            scratch_shapes=[pltpu.VMEM((LANES, model), f32), pltpu.VMEM((LANES, model), f32)],
        ),
        out_shape=[
            struct((model, tokens), bf16),
            struct((tokens, model)),
            struct((tokens, model), bf16),
            struct((tokens, ff_mine), bf16),
            struct((tokens, model), bf16),
            struct((tokens, 2 * ff_mine), bf16),
            struct((tokens, model)),
            struct((tokens, model), bf16),
            struct((model, tokens), bf16),
            struct((tile_rows, model)),
            struct((tile_rows, model)),
            struct((8, model)),
        ],
        compiler_params=vmem,
        name="middle",
        cost_estimate=cost(35),
    )(
        own_span,
        starts,
        *pieces,
        embedded,
        patch_grads,
        vectors,
        mods,
        full_output,
        weight_gu,
        down_mine,
        full_unpatch,
    )

    def result_part(held):
        return pl.pallas_call(
            waits_for(functools.partial(result_kernel, span), 7, 2),
            grid_spec=pltpu.PrefetchScalarGridSpec(
                num_scalar_prefetch=1,
                grid=(blocks,),
                in_specs=[
                    by_rows(ff_mine),
                    by_rows(model),
                    by_rows(patch),
                    whole(*mods.shape),
                    whole(*down_mine.shape),
                    whole(model, patch),
                    ANYWHERE,
                    ANYWHERE,
                ],
                out_specs=[by_rows(patch), whole(patch, model), whole(tile_rows, model)],
                scratch_shapes=[
                    pltpu.VMEM((LANES, model), f32),
                    pltpu.VMEM((LANES, model), f32),
                    pltpu.VMEM((LANES, model), bf16),
                ],
            ),
            out_shape=[struct((tokens, patch)), struct((patch, model)), struct((tile_rows, model))],
            compiler_params=vmem,
            name="result",
        cost_estimate=cost(9),
        )(own_span, hidden, residual, patch_grads, mods, down_mine, full_unpatch, *held)

    def mixed_block(which):
        return lax.dynamic_slice_in_dim(
            grad_mixed, which * head_width, head_width, 0
        ).astype(f32)

    def gu_part(held):
        return (dot(inner, after(grad_gu, *held), 0, 0).astype(bf16),)

    def output_part(held):
        return (dot(mixed_all, after(part_branch, *held), 1, 0).astype(bf16),)

    grad_mixed, done = ring_scatter(mixed_block, "tp", [gu_part, output_part, result_part])
    grad_mixed = grad_mixed.astype(bf16)
    (grad_gu_part,), (grad_output_part,), (cells, grad_unpatch, rows_second_gate) = done

    def cells_out(*parts):
        around = jnp.concatenate(
            [
                spread_cells(
                    jnp.pad(part.reshape(tile_rows, span, patch), ((2, 2), (2, 2), (0, 0))),
                    tile_rows + 2,
                    span + 2,
                    channels,
                )
                for part in parts
            ],
            axis=-1,
        )
        inside = around[:, 1 : span + 1]
        if sub_n > 1:
            from_left = shift(around[:, span + 1 :].astype(bf16), "sub", True).astype(f32)
            from_right = shift(around[:, :1].astype(bf16), "sub", False).astype(f32)
            inside = (
                inside
                + jnp.pad(from_left, ((0, 0), (0, span - 1), (0, 0)))
                + jnp.pad(from_right, ((0, 0), (span - 1, 0), (0, 0)))
            )
        from_above = shift(inside[tile_rows + 1 :].astype(bf16), "row", True).astype(f32)
        from_below = shift(inside[:1].astype(bf16), "row", False).astype(f32)
        inside = (
            inside[1 : tile_rows + 1]
            + jnp.pad(from_above, ((0, tile_rows - 1), (0, 0), (0, 0)))
            + jnp.pad(from_below, ((tile_rows - 1, 0), (0, 0), (0, 0)))
        )
        inside = (
            inside.astype(bf16)
            .reshape(tile_rows, tp_n, tile_cols, -1)
            .transpose(1, 0, 2, 3)
            .reshape(tp_n, -1, 128)
        )
        rows = -(-inside.shape[1] // owned) * owned
        inside = jnp.pad(inside, ((0, 0), (0, rows - inside.shape[1]), (0, 0)))
        return inside.reshape(tp_n, rows // owned, owned, 128).transpose(0, 2, 1, 3).reshape(
            tp_n, owned, -1
        )

    def cells_in(got):
        inside = jnp.sum(got.astype(f32), axis=0).reshape(owned, -1, 128).transpose(1, 0, 2)
        inside = inside.reshape(-1, 128)[: own * 2 * channels // 128]
        return inside.reshape(tile_rows, tile_cols, 2 * channels).astype(bf16)

    def to_chunks(partial):
        summed = lax.psum_scatter(partial.astype(bf16), "row", scatter_dimension=0, tiled=True)
        if sub_n > 1:
            summed = lax.psum_scatter(summed, "sub", scatter_dimension=0, tiled=True)
        return summed

    def scatter_rows(partial):
        if sub_n > 1:
            return to_chunks(partial)
        return row_scatter(partial).astype(bf16)

    def bands(rows):
        return dot(tile_onehot, rows, 0, 0, HIGH)

    first_cells = cells
    grad_gu_sum = to_chunks(grad_gu_part)
    grad_cross, grad_cap_keys, grad_cap_values, grad_gate_part = pl.pallas_call(
        functools.partial(cross_back_kernel, heads),
        grid=(blocks,),
        in_specs=[
            by_block(head_width),
            whole(head_width, text),
            whole(head_width, text),
            whole(head_width, 1),
            by_block(head_width),
            by_block(head_width),
            by_block(8),
        ],
        out_specs=[
            by_block(head_width),
            whole(head_width, text),
            whole(head_width, text),
            whole(head_width, 128),
        ],
        out_shape=[
            jax.ShapeDtypeStruct((head_width, tokens), bf16),
            jax.ShapeDtypeStruct((head_width, text), f32),
            jax.ShapeDtypeStruct((head_width, text), f32),
            jax.ShapeDtypeStruct((head_width, 128), f32),
        ],
        compiler_params=vmem,
        name="cross_back",
        cost_estimate=cost(7),
    )(raw_cross, caption_keys, caption_values, gate_column, grad_mixed, crossed, stats)

    grad_queries, grad_both = pl.pallas_call(
        functools.partial(attend_back_kernel, heads, key_rows, key_width),
        grid_spec=pltpu.PrefetchScalarGridSpec(
            num_scalar_prefetch=3,
            grid=(blocks,),
            in_specs=[
                by_block(1),
                by_block(head_width),
                whole(2 * head_width, edge),
                whole(2 * head_width, middle_cols),
                whole(2 * head_width, edge),
                by_block(head_width),
                by_block(head_width),
                by_block(8),
            ],
            out_specs=[by_block(head_width), whole(2 * head_width, near)],
            scratch_shapes=[
                pltpu.VMEM((8, LANES), f32),
                pltpu.VMEM((2 * head_width, near), bf16),
            ],
        ),
        out_shape=[
            jax.ShapeDtypeStruct((head_width, tokens), f32),
            jax.ShapeDtypeStruct((2 * head_width, near), f32),
        ],
        compiler_params=vmem,
        name="attend_back",
        cost_estimate=cost(14),
    )(chunk_items, low, high, item_query, queries, above, both, below, grad_mixed, self_out, stats)

    moves = []
    for source in range(all_n):
        source_row, rest = divmod(source, col_n)
        moves.append((source, rest * rows_n + source_row))
    output_sum = to_chunks(grad_output_part)
    got_gu = swap(after(grad_gu_sum, grad_mixed).reshape(tp_n, owned, -1), "tp")
    grad_down_part = dot(hidden, after(grad_feed, grad_queries), 0, 0).astype(bf16)
    grad_down = (
        grad_down_part.reshape(sub_n, rows_n, ff // all_n, model)
        .transpose(1, 0, 2, 3)
        .reshape(-1, model)
    )
    copies = []
    for t in range(tp_n):
        for i in range(2):
            for s in range(sub_n):
                copies.append(
                    (0, t, i * ff_mine + s * ff_part, 1 + i, None, (s * tp_n + t) * ff_part, ff_part)
                )
    grad_gate_weight, grad_up_weight = pack(
        copies, [jax.ShapeDtypeStruct((owned, ff), f32)] * 2, got_gu
    )

    grad_down_sum = to_chunks(grad_down)

    upper = grad_both[:, :edge].astype(bf16)
    lower = grad_both[:, near - edge :].astype(bf16)
    middle = grad_both[:, edge : near - edge]
    from_above = shift(lower, "row", True).astype(f32)
    from_below = shift(upper, "row", False).astype(f32)
    side = middle.shape[1] - edge
    middle = (
        middle
        + jnp.pad(from_above, ((0, 0), (0, side)))
        + jnp.pad(from_below, ((0, 0), (side, 0)))
    )
    if sub_n > 1:
        middle = (
            middle.astype(bf16)
            .reshape(2 * head_width, tile_rows, sub_n, span)
            .transpose(2, 0, 1, 3)
            .reshape(sub_n, 2 * head_width, tokens)
        )
        middle = jnp.sum(swap(middle, "sub").astype(f32), axis=0)
    grad_keys, grad_values = middle[:head_width], middle[head_width:]

    grad_raw, cells, grad_embedding, rows_first_scale, sums, head_sums = pl.pallas_call(
        waits_for(functools.partial(finish_kernel, heads, span), 14, 1),
        grid=(blocks,),
        in_specs=[
            by_block(head_width),
            by_block(head_width),
            by_block(head_width),
            by_block(head_width),
            by_block(2 * head_width),
            by_block(HD),
            whole(head_width, 2),
            by_rows(model),
            by_rows(model),
            by_rows(patch),
            whole(*vectors.shape),
            whole(*first_mods.shape),
            whole(model, 4 * head_width),
            whole(model, patch),
            ANYWHERE,
        ],
        out_specs=[
            by_rows(4 * head_width),
            by_rows(patch),
            whole(patch, model),
            whole(tile_rows, model),
            whole(8, model),
            whole(head_width, 128),
        ],
        out_shape=[
            struct((tokens, 4 * head_width), bf16),
            struct((tokens, patch)),
            struct((patch, model)),
            struct((tile_rows, model)),
            struct((8, model)),
            struct((head_width, 128)),
        ],
        scratch_shapes=[
            pltpu.VMEM((4 * head_width, LANES), f32),
            pltpu.VMEM((LANES, model), f32),
            pltpu.VMEM((LANES, model), bf16),
        ],
        compiler_params=vmem,
        name="finish",
        cost_estimate=cost(13),
    )(
        grad_queries,
        grad_keys,
        grad_values,
        grad_cross,
        raw,
        tables,
        gains,
        embedded,
        part_residual,
        neighbours,
        vectors,
        first_mods,
        weight_qkvc,
        embedding_t,
        output_sum,
    )

    grad_qkvc = dot(normed, after(grad_raw, got_gu), 0, 0).astype(bf16)

    grad_cap = row_scatter(
        after(jnp.concatenate([grad_cap_keys, grad_cap_values], axis=0), grad_raw)
    ).astype(bf16)
    if sub_n > 1:
        grad_cap = lax.psum_scatter(grad_cap, "sub", scatter_dimension=0, tiled=True)
    cap_rows = 2 * head_width // (rows_n * sub_n)


    def place(vectors):
        return lax.dynamic_update_slice_in_dim(
            jnp.zeros((vectors.shape[0], model), f32), vectors, tp * head_width, 1
        )

    head_vectors = jnp.concatenate(
        [head_sums[:, 0:2], grad_gate_part[:, 0:1], jnp.zeros((head_width, 5), f32)], axis=1
    )
    small = jnp.concatenate(
        [
            bands(rows_first_scale),
            bands(rows_first_gate),
            bands(rows_second_scale),
            bands(rows_second_gate),
            grad_embedding,
            grad_unpatch,
            sums,
            grad_ff_gain,
            place(head_vectors.T),
        ],
        axis=0,
    ).astype(bf16)
    small_width = small.shape[0]
    small = small.reshape(small_width, rows_n, model // rows_n).transpose(1, 0, 2)
    small = small.reshape(rows_n * small_width, model // rows_n)
    small = row_scatter(small).astype(bf16)
    mods_rows = 4 * NBAND
    lanes = model // rows_n
    joint = jnp.concatenate(
        [grad_cap, small[:mods_rows].reshape(-1, text)], axis=0
    )
    joint = lax.all_gather(after(joint, grad_down_sum), ALL, axis=0)
    all_mods = joint[:, cap_rows:].astype(f32).reshape(rows_n, col_n, mods_rows, lanes)
    all_mods = jnp.sum(all_mods, axis=1).transpose(1, 0, 2).reshape(mods_rows, model)
    grad_cap = joint[:, :cap_rows]
    small = small[mods_rows:]
    small_width = small_width - mods_rows
    small = small.T
    if sub_n > 1:
        small = lax.psum_scatter(small, "sub", scatter_dimension=0, tiled=True)
    small = small.reshape(tp_n, owned, small_width)
    qkvc_width = 4 * head_width
    sent = scatter_rows(grad_qkvc).reshape(tp_n, owned, qkvc_width)
    sent = jnp.concatenate(
        [sent, output_sum.reshape(tp_n, owned, model), small, cells_out(first_cells, cells)], axis=2
    )
    got = swap(sent, "tp")
    grad_output = jnp.sum(got[:, :, qkvc_width : qkvc_width + model].astype(f32), axis=0)
    small_at = qkvc_width + model
    cells_at = small_at + small_width
    small = jnp.sum(got[:, :, small_at:cells_at].astype(f32), axis=0)
    both_cells = cells_in(got[:, :, cells_at:])
    prediction, latent_grad = both_cells[..., :channels], both_cells[..., channels:]
    copies = []
    for t in range(tp_n):
        for i in range(3):
            copies.append((0, t, i * head_width, 1, None, i * model + t * head_width, head_width))
        copies.append((0, t, 3 * head_width, 2, None, t * head_width, head_width))
    grad_projection, grad_cross_query = pack(
        copies,
        [
            jax.ShapeDtypeStruct((owned, 3 * model), f32),
            jax.ShapeDtypeStruct((owned, model), f32),
        ],
        got,
    )
    at = 2 * patch
    grad_embedding = small[:, :patch].T
    grad_unpatch = small[:, patch : 2 * patch]
    vectors = small[:, at:].T

    grad_cap = (
        grad_cap.reshape(rows_n, sub_n, tp_n, cap_rows, text)
        .transpose(2, 0, 1, 3, 4)
        .reshape(tp_n, 2, head_width, text)
        .transpose(1, 0, 2, 3)
        .reshape(2 * model, text)
    )
    cap_own = captions.shape[1] // all_n
    own_captions = lax.dynamic_slice_in_dim(captions, index * cap_own, cap_own, 1)
    grad_caption = dot(own_captions, grad_cap, 0, 1)

    grad_down = lax.ppermute(grad_down_sum, ALL, moves).astype(f32)
    own_band = lax.dynamic_slice_in_dim(full_band, index * owned, owned, 1)
    own_silu = jax.nn.silu(own_band)
    grad_adaptive = jnp.concatenate(
        [dot(own_silu, all_mods[i * NBAND : (i + 1) * NBAND], 0, 0, HIGH) for i in range(4)], axis=1
    )
    bias_own = 4 * owned
    totals = jnp.sum(all_mods.reshape(4, NBAND, model), axis=1).reshape(-1)
    grad_adaptive_bias = lax.dynamic_slice_in_dim(totals, index * bias_own, bias_own, 0)
    local_rows = my_quarter(adaptive)
    local_band = lax.dynamic_slice_in_dim(band_table, row * quarter, quarter, 1).astype(f32)
    grad_band = sum(
        dot(
            all_mods[i * NBAND : (i + 1) * NBAND],
            local_rows[:, i * model : (i + 1) * model].astype(f32),
            1,
            1,
            HIGH,
        )
        for i in range(4)
    ) * silu_slope(local_band)
    grad_band = lax.ppermute(grad_band, ALL, moves)

    return (
        prediction,
        latent_grad,
        grad_embedding,
        vectors[1],
        grad_band,
        grad_adaptive,
        grad_adaptive_bias,
        vectors[0],
        grad_projection,
        vectors[16],
        vectors[17],
        grad_cross_query,
        grad_caption,
        vectors[18],
        grad_output,
        vectors[8],
        grad_gate_weight,
        grad_up_weight,
        grad_down,
        grad_unpatch,
    )


def _mine(vector, tp, sub_n):
    if sub_n == 1:
        return vector
    size = vector.shape[0] * sub_n
    whole = lax.all_gather(vector, COL, axis=0, tiled=True)
    return lax.dynamic_slice_in_dim(whole, tp * size, size, 0)


def solution(mesh):
    rows_n, col_n = mesh.shape["row"], mesh.shape["col"]

    def run(*args):
        heads = args[5].shape[0] // HD
        tp_n = math.gcd(heads, col_n)
        split = Mesh(mesh.devices.reshape(rows_n, col_n // tp_n, tp_n), ALL)
        in_specs = (
            P("row", COL, None),
            P(),
            P(),
            P(),
            P(None, COL),
            P(COL),
            P(None, COL),
            P(COL, None),
            P(COL),
            P(COL),
            P(COL, None),
            P(COL),
            P(COL),
            P(COL, None),
            P(COL, None),
            P(COL),
            P(COL, None),
            P(COL),
            P(COL, None),
            P(COL, None),
            P(COL, None),
            P(COL, None),
            P("row", COL, None),
        )
        out_specs = (
            P("row", COL, None),
            P("row", COL, None),
            P(None, ALL),
            P(ALL),
            P(None, ALL),
            P(ALL, None),
            P(ALL),
            P(ALL),
            P(ALL, None),
            P(ALL),
            P(ALL),
            P(ALL, None),
            P(ALL, None),
            P(ALL),
            P(ALL, None),
            P(ALL),
            P(ALL, None),
            P(ALL, None),
            P(ALL, None),
            P(ALL, None),
        )
        return jax.shard_map(
            on_device, mesh=split, in_specs=in_specs, out_specs=out_specs, check_vma=False
        )(*args)

    return run
```
